256 devices in a mesh: section: 8 (over x, core), dp: 32 (over y, z).
Axes of the slice: x: 4, y: 4, z: 8, core: 2. Of those that a mesh axis runs over, the one named last changes fastest.
Arguments:
- stack_input: bfloat16 [4096, 12288], P('dp'), may hold values from -6 to 6
- out_cotangent: bfloat16 [4096, 12288], P('dp'), may hold values from -6 to 6
- norm_gain: float32 [8, 12288], P('section'), may hold values from 0.5 to 1.5
- master_in: float32 [8, 12288, 128], P('section', 'dp'), may hold values from -0.0546875 to 0.0546875
- master_out: float32 [8, 128, 12288], P('section', None, 'dp'), may hold values from -0.5 to 0.5
- first_in: float32 [8, 12288, 128], P('section', 'dp'), may hold values from -3 to 3
- first_out: float32 [8, 128, 12288], P('section', None, 'dp'), may hold values from -0.1 to 0.1
- second_in: float32 [8, 12288, 128], P('section', 'dp'), may hold values from 0.02 to 0.5
- second_out: float32 [8, 128, 12288], P('section', None, 'dp'), may hold values from 0.02 to 0.5
Outputs:
- section_outputs: bfloat16 [8, 4096, 12288], P('section', 'dp')
- new_master_in: float32 [8, 12288, 128], P('section', 'dp')
- new_master_out: float32 [8, 128, 12288], P('section', None, 'dp')
- new_first_in: float32 [8, 12288, 128], P('section', 'dp')
- new_first_out: float32 [8, 128, 12288], P('section', None, 'dp')
- new_second_in: float32 [8, 12288, 128], P('section', 'dp')
- new_second_out: float32 [8, 128, 12288], P('section', None, 'dp')
The draws below stay inside these ranges and needn't reach their ends.
All inputs are finite; a program needn't handle non-finite values.
Results may differ from the reference program's by a relative error of at most 0.018.
Values may be sent and summed in bfloat16 or wider, within the bound.
No kernel may reach another device: no remote copies, remote signals or barrier semaphores. Data moves between devices by JAX's collectives and lax.ppermute only.
A program may use at most 128 MiB of HBM per device.

```python
import math
import jax
import jax.numpy as jnp
from jax import lax

D = 12288
R = 128
STEP = 10
TOKENS = 4096
N_SECTION = 8


def block_levels(key, dims, pieces, smallest, top_value):
    def one(axis_at, shards_of):
        steps = jax.random.uniform(jax.random.fold_in(jax.random.fold_in(key, 6), axis_at), (shards_of,), jnp.float32, smallest / len(pieces), top_value / len(pieces))
        return jnp.repeat(jnp.exp(steps), dims[axis_at] // shards_of).reshape((-1,) + (1,) * (len(dims) - axis_at - 1))

    level = one(*pieces[0])
    for cut in pieces[1:]:
        level = level * one(*cut)
    return level


def noise(rng, shape, deviation, most, pieces=(), kind=jnp.bfloat16):
    entries = deviation * jax.random.normal(rng, shape, jnp.float32)
    if pieces:
        entries = entries * block_levels(rng, shape, pieces, -0.22, 0.18)
    return jnp.clip(entries, -most, most).astype(kind)


def setup_inputs(seed: int = 0) -> dict:
    keys = jax.random.split(jax.random.key(seed), 10)
    return {
        "stack_input": noise(keys[0], (TOKENS, D), 1.0, 6.0, ((0, 32),)),
        "out_cotangent": noise(keys[1], (TOKENS, D), 1.0, 6.0, ((0, 32),)),
        "norm_gain": jnp.clip(1.0 + 0.1 * jax.random.normal(keys[2], (N_SECTION, D), jnp.float32), 0.5, 1.5),
        "master_in": noise(keys[3], (N_SECTION, D, R), D ** -0.5, 0.0546875, ((0, 8), (1, 32)), jnp.float32),
        "master_out": noise(keys[4], (N_SECTION, R, D), R ** -0.5, 0.5, ((0, 8), (2, 32)), jnp.float32),
        "first_in": noise(keys[5], (N_SECTION, D, R), 0.5, 3.0, ((0, 8), (1, 32)), jnp.float32),
        "first_out": noise(keys[6], (N_SECTION, R, D), 0.02, 0.1, ((0, 8), (2, 32)), jnp.float32),
        "second_in": jnp.clip(jnp.exp(math.log(0.5) - 3.218876 * jax.random.uniform(keys[7], (N_SECTION, D, R), jnp.float32) ** block_levels(keys[7], (N_SECTION, D, R), ((0, 8), (1, 32)), -0.2, 0.2)), 0.02, 0.5),
        "second_out": jnp.clip(jnp.exp(math.log(0.5) - 3.218876 * jax.random.uniform(keys[8], (N_SECTION, R, D), jnp.float32) ** block_levels(keys[8], (N_SECTION, R, D), ((0, 8), (2, 32)), -0.2, 0.2)), 0.02, 0.5),
    }


norm_eps = 1e-05
gelu_coef = 0.7978845608028654
beta_one = 0.9
beta_two = 0.95
adam_eps = 1e-08
learn_rate = 0.05
decay_rate = 0.1
clip_rms = 0.5

def gelu_pair(hidden_pre):
    inner_arg = gelu_coef * (hidden_pre + 0.044715 * hidden_pre * hidden_pre * hidden_pre)
    tangent = jnp.tanh(inner_arg)
    gelu_value = 0.5 * hidden_pre * (1.0 + tangent)
    gelu_slope = 0.5 * (1.0 + tangent) + 0.5 * hidden_pre * (1.0 - tangent * tangent) * gelu_coef * (1.0 + 3.0 * 0.044715 * hidden_pre * hidden_pre)
    return (gelu_value, gelu_slope)

def contract_rows(left_arr, right_arr):
    return lax.dot_general(left_arr, right_arr, (((0,), (0,)), ((), ())), preferred_element_type=jnp.float32)

def contract_last(left_arr, right_arr):
    return lax.dot_general(left_arr, right_arr, (((1,), (1,)), ((), ())), preferred_element_type=jnp.float32)

def norm_parts(inputs, gain_row):
    wide_input = inputs.astype(jnp.float32)
    inv_rms = lax.rsqrt(lax.optimization_barrier(jnp.mean(wide_input * wide_input, axis=-1, keepdims=True)) + norm_eps)
    normed = (wide_input * inv_rms * gain_row).astype(jnp.bfloat16)
    return (wide_input, inv_rms, normed)

def layer_forward(inputs, gain_row, weight_in, weight_out):
    wide_input, inv_rms, normed = norm_parts(inputs, gain_row)
    hidden_pre = jnp.dot(normed, weight_in, preferred_element_type=jnp.float32)
    gelu_value, gelu_slope = gelu_pair(hidden_pre)
    act_low = gelu_value.astype(jnp.bfloat16)
    result = (wide_input + jnp.dot(act_low, weight_out, preferred_element_type=jnp.float32)).astype(jnp.bfloat16)
    return (result, hidden_pre)

def layer_backward(inputs, gain_row, weight_in, weight_out, hidden_pre, incoming):
    wide_input, inv_rms, normed = norm_parts(inputs, gain_row)
    gelu_value, gelu_slope = gelu_pair(hidden_pre)
    act_low = gelu_value.astype(jnp.bfloat16)
    d_act = contract_last(incoming, weight_out)
    d_pre = (d_act * gelu_slope).astype(jnp.bfloat16)
    scaled = contract_last(d_pre, weight_in) * gain_row
    d_inputs = incoming.astype(jnp.float32) + inv_rms * scaled - wide_input * inv_rms ** 3 * lax.optimization_barrier(jnp.mean(wide_input * scaled, axis=-1, keepdims=True))
    return (d_inputs.astype(jnp.bfloat16), d_pre, act_low, normed)

def adam_update(master, first, second, grad):
    first_new = beta_one * first + (1.0 - beta_one) * grad
    second_new = beta_two * second + (1.0 - beta_two) * grad * grad
    first_hat = first_new / (1.0 - beta_one ** STEP)
    second_hat = second_new / (1.0 - beta_two ** STEP)
    master_new = master - learn_rate * (first_hat / (jnp.sqrt(second_hat) + adam_eps) + decay_rate * master)
    return (master_new, first_new, second_new)

def reference(stack_input, out_cotangent, norm_gain, master_in, master_out, first_in, first_out, second_in, second_out):
    work_in = master_in.astype(jnp.bfloat16)
    work_out = master_out.astype(jnp.bfloat16)
    kept_inputs = []
    kept_pre = []
    outputs_list = []
    current = stack_input
    for section_num in range(N_SECTION):
        kept_inputs.append(current)
        current, hidden_pre = layer_forward(current, norm_gain[section_num], work_in[section_num], work_out[section_num])
        kept_pre.append(hidden_pre)
        outputs_list.append(current)
    incoming = out_cotangent
    grads_in = [None] * N_SECTION
    grads_out = [None] * N_SECTION
    for section_num in reversed(range(N_SECTION)):
        d_inputs, d_pre, act_low, normed = layer_backward(kept_inputs[section_num], norm_gain[section_num], work_in[section_num], work_out[section_num], kept_pre[section_num], incoming)
        grads_in[section_num] = contract_rows(normed, d_pre)
        grads_out[section_num] = contract_rows(act_low, incoming)
        incoming = d_inputs
    grad_in = jnp.stack(grads_in)
    grad_out = jnp.stack(grads_out)
    total_sq = jnp.sum(grad_in * grad_in) + jnp.sum(grad_out * grad_out)
    norm_limit = clip_rms * math.sqrt(2.0 * D * R * N_SECTION)
    clip_factor = norm_limit / jnp.maximum(jnp.sqrt(total_sq), norm_limit)
    new_in, new_first_in, new_second_in = adam_update(master_in, first_in, second_in, clip_factor * grad_in)
    new_out, new_first_out, new_second_out = adam_update(master_out, first_out, second_out, clip_factor * grad_out)
    return (jnp.stack(outputs_list), new_in, new_out, new_first_in, new_first_out, new_second_in, new_second_out)
```

```python
import functools
import math

import jax
import jax.numpy as jnp
from jax import lax
from jax.experimental import pallas as pl
from jax.experimental.pallas import tpu as pltpu
from jax.sharding import Mesh, PartitionSpec as P

STEP = 10

norm_eps = 1e-05
gelu_coef = 0.7978845608028654
beta_one = 0.9
beta_two = 0.95
adam_eps = 1e-08
learn_rate = 0.05
decay_rate = 0.1
clip_rms = 0.5

LOW = jnp.bfloat16
WIDE = jnp.float32
PLANE = ("s", "y")
VMEM_BYTES = 48 * 1024 * 1024


def dot_nn(left, right):
    return lax.dot_general(left, right, (((1,), (0,)), ((), ())), preferred_element_type=WIDE)


def dot_nt(left, right):
    return lax.dot_general(left, right, (((1,), (1,)), ((), ())), preferred_element_type=WIDE)


def dot_tn(left, right):
    return lax.dot_general(left, right, (((0,), (0,)), ((), ())), preferred_element_type=WIDE)


def gelu_pair(hidden_pre):
    inner_arg = gelu_coef * (hidden_pre + 0.044715 * hidden_pre * hidden_pre * hidden_pre)
    tangent = jnp.tanh(inner_arg)
    gelu_value = 0.5 * hidden_pre * (1.0 + tangent)
    gelu_slope = 0.5 * (1.0 + tangent) + 0.5 * hidden_pre * (
        1.0 - tangent * tangent
    ) * gelu_coef * (1.0 + 3.0 * 0.044715 * hidden_pre * hidden_pre)
    return (gelu_value, gelu_slope)


def adam_update(master, first, second, grad):
    first_new = beta_one * first + (1.0 - beta_one) * grad
    second_new = beta_two * second + (1.0 - beta_two) * grad * grad
    first_hat = first_new / (1.0 - beta_one**STEP)
    second_hat = second_new / (1.0 - beta_two**STEP)
    master_new = master - learn_rate * (
        first_hat / (jnp.sqrt(second_hat) + adam_eps) + decay_rate * master
    )
    return (master_new, first_new, second_new)


def local_call(kernel, out_shape, operands, scratch=(), flops=0):
    specs = jax.tree.map(lambda _: pl.BlockSpec(memory_space=pltpu.VMEM), out_shape)
    moved = sum(a.size * a.dtype.itemsize for a in operands)
    moved += sum(a.size * a.dtype.itemsize for a in jax.tree.leaves(out_shape))
    return pl.pallas_call(
        kernel,
        out_shape=out_shape,
        in_specs=[pl.BlockSpec(memory_space=pltpu.VMEM)] * len(operands),
        out_specs=specs,
        scratch_shapes=list(scratch),
        compiler_params=pltpu.CompilerParams(vmem_limit_bytes=VMEM_BYTES),
        cost_estimate=pl.CostEstimate(flops=flops, bytes_accessed=moved, transcendentals=0),
    )(*operands)


def project_kernel(rank, rows_ref, weight_ref, out_ref):
    groups, both_rows, _ = rows_ref.shape
    layers = weight_ref.shape[0]
    half = both_rows // 2
    planes = out_ref.shape[0]
    piece = half // planes
    for group in range(groups):
        inputs = rows_ref[group, :half, :]
        cots = rows_ref[group, half:, :]
        for layer in range(layers):
            weight = weight_ref[layer]
            first = dot_nn(inputs, weight).astype(LOW)
            second = dot_nn(cots, weight[:, rank:]).astype(LOW)
            for plane in range(planes):
                sel = slice(plane * piece, (plane + 1) * piece)
                base = layer * 3 * rank
                out_ref[plane, group, :, base : base + 2 * rank] = first[sel]
                out_ref[plane, group, :, base + 2 * rank : base + 3 * rank] = second[sel]


def recursion_kernel(layers, rank, width, parts_ref, square_ref, cross_ref, out_ref, sums_ref):
    sources = parts_ref.shape[0]
    sums_ref[...] = parts_ref[0].astype(WIDE)

    def add_source(source, _):
        sums_ref[...] += parts_ref[source].astype(WIDE)
        return 0

    lax.fori_loop(1, sources, add_source, 0)
    rank3 = 3 * rank
    down = [sums_ref[:, k * rank3 : k * rank3 + rank] for k in range(layers)]
    up = [sums_ref[:, k * rank3 + rank : k * rank3 + 2 * rank] for k in range(layers)]
    back = [sums_ref[:, k * rank3 + 2 * rank : (k + 1) * rank3] for k in range(layers)]
    square = square_ref[:, 0:1]

    acts, pres, invs = [], [], []
    for s in range(layers):
        inv = lax.rsqrt(jnp.maximum(square, 0.0) / width + norm_eps)
        pre = inv * down[s]
        act, _ = gelu_pair(pre)
        act = act.astype(LOW)
        acts.append(act)
        pres.append(pre)
        invs.append(inv)
        out_ref[:, s * rank : (s + 1) * rank] = act
        low = s * rank
        forward = dot_nn(act, cross_ref[low : low + rank, low:])
        before = up[s]
        up[s] = before + forward[:, :rank]
        square = square + jnp.sum(act.astype(WIDE) * (before + up[s]), axis=-1, keepdims=True)
        if s + 1 < layers:
            mirrored = dot_nt(act, cross_ref[low + rank :, low : low + rank])
            for k in range(s + 1, layers):
                at = (k - s) * rank
                down[k] = down[k] + forward[:, at : at + rank]
                up[k] = up[k] + mirrored[:, at - rank : at]

    trailing = jnp.zeros_like(square)
    lane = lax.broadcasted_iota(jnp.int32, (square.shape[0], rank), 1)
    tail = jnp.zeros((square.shape[0], rank), WIDE)
    for s in reversed(range(layers)):
        _, slope = gelu_pair(pres[s])
        d_pre = (back[s] - trailing * up[s]) * slope
        coef = invs[s] * invs[s] * (1.0 / width) * jnp.sum(d_pre * pres[s], axis=-1, keepdims=True)
        moved = (invs[s] * d_pre).astype(LOW)
        out_ref[:, (layers + s) * rank : (layers + s + 1) * rank] = moved
        coef_high = coef.astype(LOW).astype(WIDE)
        tail = tail + jnp.where(lane == s, coef_high, 0.0)
        tail = tail + jnp.where(lane == s + layers, coef - coef_high, 0.0)
        if s > 0:
            low = s * rank
            gain_term = dot_nt(moved, cross_ref[:low, low : low + rank])
            scaled_act = (trailing * acts[s].astype(WIDE)).astype(LOW)
            norm_term = dot_nn(scaled_act, cross_ref[low : low + rank, :low])
            for k in range(s):
                sel = slice(k * rank, (k + 1) * rank)
                back[k] = back[k] + gain_term[:, sel] - norm_term[:, sel]
        trailing = trailing + coef
    out_ref[:, 2 * layers * rank :] = tail.astype(LOW)


def expand_kernel(
    layers, rank, rows_ref, weight_ref, coded_ref, out_ref, grad_ref, wide_ref, act_ref, moved_ref, coef_ref
):
    groups, both_rows, features = rows_ref.shape
    half = both_rows // 2
    planes = coded_ref.shape[0]
    piece = coded_ref.shape[2]
    span = layers * rank
    for group in range(groups):
        base = group * half
        wide_ref[base : base + half, :] = rows_ref[group, :half, :].astype(WIDE)
        for plane in range(planes):
            at = base + plane * piece
            act_ref[at : at + piece, :] = coded_ref[plane, group, :, :span]
            moved_ref[at : at + piece, :] = coded_ref[plane, group, :, span : 2 * span]
            coef_ref[at : at + piece, :] = coded_ref[plane, group, :, 2 * span :].astype(WIDE)

    for layer in range(layers):
        up_weight = weight_ref[layer, :, rank:]
        act = act_ref[:, layer * rank : (layer + 1) * rank]
        total = wide_ref[...] + dot_nt(act, up_weight)
        wide_ref[...] = total
        lowered = total.astype(LOW)
        for group in range(groups):
            out_ref[layer, group] = lowered[group * half : (group + 1) * half]

    for group in range(groups):
        base = group * half
        wide_ref[base : base + half, :] = rows_ref[group, half:, :].astype(WIDE)
    for layer in reversed(range(layers)):
        delta = wide_ref[...].astype(LOW)
        act = act_ref[:, layer * rank : (layer + 1) * rank]
        moved = moved_ref[:, layer * rank : (layer + 1) * rank]
        if layer > 0:
            current = out_ref[layer - 1].reshape(groups * half, features)
        else:
            current = rows_ref[:, :half, :].reshape(groups * half, features)
        grad_ref[layer, :, features:] = dot_tn(act, delta).astype(LOW)
        grad_ref[layer, :, :features] = dot_tn(moved, current).astype(LOW)
        if layer > 0:
            coef = coef_ref[:, layer : layer + 1] + coef_ref[:, layers + layer : layers + layer + 1]
            wide_ref[...] += dot_nt(moved, weight_ref[layer, :, :rank]) - coef * current.astype(WIDE)


def shards(
    stack_input,
    out_cotangent,
    norm_gain,
    master_in,
    master_out,
    first_in,
    first_out,
    second_in,
    second_out,
):
    layers, count_y, count_z = (lax.axis_size(a) for a in ("s", "y", "z"))
    pos_s, pos_y, pos_z = (lax.axis_index(a) for a in ("s", "y", "z"))
    sources = layers * count_y
    tok_rows, model_width = stack_input.shape
    features, rank = master_in.shape[1:]
    piece = tok_rows // layers
    swap = [(a * count_z + b, b * count_z + a) for a in range(layers) for b in range(count_z)]

    gain_own = lax.dynamic_slice_in_dim(norm_gain[0], (pos_y * count_z + pos_z) * features, features, 0)
    work_in = master_in[0].astype(LOW).astype(WIDE)
    gained_in = (work_in * gain_own[:, None]).astype(LOW)
    turned_out = master_out[0].astype(LOW).T
    packed = jnp.concatenate([gained_in, turned_out], axis=1)
    swapped = lax.ppermute(packed, ("s", "z"), swap)
    gain_swapped = lax.ppermute(gain_own, ("s", "z"), swap)
    weights = lax.all_gather(swapped, "z", axis=0)

    def blocks_of(rows):
        return jnp.stack(
            [
                lax.dynamic_slice_in_dim(rows, (g * count_z + pos_s) * features, features, 1)
                for g in range(count_y)
            ]
        )

    rows = jnp.concatenate([blocks_of(stack_input), blocks_of(out_cotangent)], axis=1)
    rows = lax.all_to_all(rows, "y", 0, 0, tiled=True)
    own_rows = lax.dynamic_slice_in_dim(stack_input, pos_s * piece, piece, 0).astype(WIDE)
    square = jnp.sum(own_rows * own_rows, axis=-1, keepdims=True)
    square = jnp.broadcast_to(square, (piece, 128))

    cross = lax.dot_general(
        swapped[:, rank:], weights, (((0,), (1,)), ((), ())), preferred_element_type=WIDE
    )
    later = (jnp.arange(layers) > pos_z)[None, :, None]
    cross = jnp.where(later, cross[..., :rank], cross[..., rank:]).astype(LOW)
    cut_r, cut_c = rank // layers, layers * rank // count_y
    cross = cross.reshape(layers, cut_r, count_y, cut_c).transpose(0, 2, 1, 3)
    cross = cross.reshape(sources, cut_r, cut_c)
    cross = lax.all_to_all(cross, PLANE, 0, 0, tiled=True)
    cross = jnp.sum(cross.astype(WIDE), axis=0, keepdims=True).astype(LOW)
    cross = jnp.broadcast_to(cross, (sources, cut_r, cut_c))
    cross = lax.all_to_all(cross, PLANE, 0, 0, tiled=True)
    cross = cross.reshape(layers, count_y, cut_r, cut_c).transpose(0, 2, 1, 3)
    cross = cross.reshape(rank, layers * rank)
    cross, rows, weights = lax.optimization_barrier((cross, rows, weights))
    cross = lax.all_gather(cross, "z", axis=0, tiled=True)

    parts = local_call(
        functools.partial(project_kernel, rank),
        jax.ShapeDtypeStruct((layers, count_y, piece, layers * 3 * rank), LOW),
        (rows, weights),
        flops=2 * rows.shape[0] * tok_rows * features * layers * rank * 3,
    )
    parts = parts.reshape(sources, piece, layers * 3 * rank)
    parts = lax.all_to_all(parts, PLANE, 0, 0, tiled=True)
    coded_width = 2 * layers * rank + rank
    coded = local_call(
        functools.partial(recursion_kernel, layers, rank, float(model_width)),
        jax.ShapeDtypeStruct((piece, coded_width), LOW),
        (parts, square, cross),
        scratch=[pltpu.VMEM((piece, layers * 3 * rank), WIDE)],
    )
    coded = jnp.broadcast_to(coded[None], (sources, piece, coded_width))
    coded = lax.all_to_all(coded, PLANE, 0, 0, tiled=True)
    coded = coded.reshape(layers, count_y, piece, coded_width)

    group_tokens = count_y * tok_rows
    outputs, grads = local_call(
        functools.partial(expand_kernel, layers, rank),
        (
            jax.ShapeDtypeStruct((layers, count_y, tok_rows, features), LOW),
            jax.ShapeDtypeStruct((layers, rank, 2 * features), LOW),
        ),
        (rows, weights, coded),
        scratch=[
            pltpu.VMEM((group_tokens, features), WIDE),
            pltpu.VMEM((group_tokens, layers * rank), LOW),
            pltpu.VMEM((group_tokens, layers * rank), LOW),
            pltpu.VMEM((group_tokens, rank), WIDE),
        ],
        flops=8 * group_tokens * features * layers * rank,
    )
    grads = lax.psum_scatter(grads, "z", scatter_dimension=0, tiled=True)[0]
    outputs = outputs.reshape(sources, tok_rows, features)
    outputs = lax.all_to_all(outputs, PLANE, 0, 0, tiled=True)
    outputs = outputs.reshape(layers, count_y, tok_rows, features).transpose(2, 1, 0, 3)
    section_rows = outputs.reshape(1, tok_rows, model_width)

    wide_grads = grads.astype(WIDE)
    swapped_in = wide_grads[:, :features] * gain_swapped[None, :]
    swapped_out = wide_grads[:, features:]
    local_sq = jnp.sum(swapped_in * swapped_in) + jnp.sum(swapped_out * swapped_out)
    everyone = ("s", "y", "z")
    total = jnp.broadcast_to(local_sq, (sources * count_z, 1, 128))
    total_sq = jnp.sum(lax.all_to_all(total, everyone, 0, 0, tiled=True)[:, 0, 0])
    norm_limit = clip_rms * math.sqrt(2.0 * model_width * rank * layers)
    clip_factor = norm_limit / jnp.maximum(jnp.sqrt(total_sq), norm_limit)

    own_grads = lax.ppermute(grads, ("s", "z"), swap).astype(WIDE)
    shard_in = (own_grads[:, :features] * gain_own[None, :]).T
    shard_out = own_grads[:, features:]
    new_in, new_first_in, new_second_in = adam_update(
        master_in[0], first_in[0], second_in[0], clip_factor * shard_in
    )
    new_out, new_first_out, new_second_out = adam_update(
        master_out[0], first_out[0], second_out[0], clip_factor * shard_out
    )
    return (
        section_rows,
        new_in[None],
        new_out[None],
        new_first_in[None],
        new_first_out[None],
        new_second_in[None],
        new_second_out[None],
    )


def solution(mesh):
    layers, groups = mesh.shape["section"], mesh.shape["dp"]
    fine = Mesh(mesh.devices.reshape(layers, groups // layers, layers), ("s", "y", "z"))
    split = ("y", "z")
    by_rows = P("s", split, None)
    by_cols = P("s", None, split)
    in_specs = (
        P(split, None),
        P(split, None),
        P("s", None),
        by_rows,
        by_cols,
        by_rows,
        by_cols,
        by_rows,
        by_cols,
    )
    out_specs = (by_rows, by_rows, by_cols, by_rows, by_cols, by_rows, by_cols)
    return jax.shard_map(shards, mesh=fine, in_specs=in_specs, out_specs=out_specs, check_vma=False)
```

```python
import functools
import math

import jax
import jax.numpy as jnp
from jax import lax
from jax.experimental import pallas as pl
from jax.experimental.pallas import tpu as pltpu
from jax.sharding import Mesh, PartitionSpec as P

STEP = 10

norm_eps = 1e-05
gelu_coef = 0.7978845608028654
beta_one = 0.9
beta_two = 0.95
adam_eps = 1e-08
learn_rate = 0.05
decay_rate = 0.1
clip_rms = 0.5

LOW = jnp.bfloat16
WIDE = jnp.float32
SECTION = ("x", "c")
PLANE = ("x", "c", "y")
EVERYONE = ("x", "c", "y", "z")
SHIFTS = (0, 1, -1, 2)
VMEM_BYTES = 48 * 1024 * 1024


def dot_nn(left, right):
    return lax.dot_general(left, right, (((1,), (0,)), ((), ())), preferred_element_type=WIDE)


def dot_nt(left, right):
    return lax.dot_general(left, right, (((1,), (1,)), ((), ())), preferred_element_type=WIDE)


def dot_tn(left, right):
    return lax.dot_general(left, right, (((0,), (0,)), ((), ())), preferred_element_type=WIDE)


def gelu_pair(hidden_pre):
    inner_arg = gelu_coef * (hidden_pre + 0.044715 * hidden_pre * hidden_pre * hidden_pre)
    tangent = jnp.tanh(inner_arg)
    gelu_value = 0.5 * hidden_pre * (1.0 + tangent)
    gelu_slope = 0.5 * (1.0 + tangent) + 0.5 * hidden_pre * (
        1.0 - tangent * tangent
    ) * gelu_coef * (1.0 + 3.0 * 0.044715 * hidden_pre * hidden_pre)
    return (gelu_value, gelu_slope)


def adam_update(master, first, second, grad):
    first_new = beta_one * first + (1.0 - beta_one) * grad
    second_new = beta_two * second + (1.0 - beta_two) * grad * grad
    first_hat = first_new / (1.0 - beta_one**STEP)
    second_hat = second_new / (1.0 - beta_two**STEP)
    master_new = master - learn_rate * (
        first_hat / (jnp.sqrt(second_hat) + adam_eps) + decay_rate * master
    )
    return (master_new, first_new, second_new)


def local_call(kernel, out_shape, operands, scalars=None, scratch=(), flops=0):
    specs = jax.tree.map(lambda _: pl.BlockSpec(memory_space=pltpu.VMEM), out_shape)
    moved = sum(a.size * a.dtype.itemsize for a in operands)
    moved += sum(a.size * a.dtype.itemsize for a in jax.tree.leaves(out_shape))
    in_specs = [pl.BlockSpec(memory_space=pltpu.VMEM)] * len(operands)
    if scalars is not None:
        operands = (scalars,) + tuple(operands)
        in_specs = [pl.BlockSpec(memory_space=pltpu.SMEM)] + in_specs
    return pl.pallas_call(
        kernel,
        out_shape=out_shape,
        in_specs=in_specs,
        out_specs=specs,
        scratch_shapes=list(scratch),
        compiler_params=pltpu.CompilerParams(vmem_limit_bytes=VMEM_BYTES),
        cost_estimate=pl.CostEstimate(flops=flops, bytes_accessed=moved, transcendentals=0),
    )(*operands)


def shifted(block, axis, distance):
    size = lax.axis_size(axis)
    return lax.ppermute(block, axis, [(i, (i + distance) % size) for i in range(size)])


def gather_line(block, axis):
    return jnp.stack([block] + [shifted(block, axis, d) for d in SHIFTS[1:]])


def pack_kernel(gain_ref, in_ref, out_ref, pack_ref):
    features, rank = in_ref.shape[1:]
    gain = jnp.broadcast_to(gain_ref[...], (rank, features)).T
    work_in = in_ref[0].astype(LOW).astype(WIDE)
    pack_ref[:, :rank] = (work_in * gain).astype(LOW)
    pack_ref[:, rank:] = out_ref[0].T.astype(LOW)


def project_kernel(rank, place_ref, rows_ref, weight_ref, keep_ref, send_ref):
    groups, both_rows, _ = rows_ref.shape
    layers = weight_ref.shape[0]
    half = both_rows // 2
    columns = keep_ref.shape[0]
    piece = half // (2 * columns)
    core, section = place_ref[0], place_ref[1]
    for layer in range(layers):
        weight = weight_ref[lax.rem(section + layer, layers)]
        base = layer * 3 * rank
        for group in range(groups):
            first = dot_nn(rows_ref[group, :half, :], weight).astype(LOW)
            second = dot_nn(rows_ref[group, half:, :], weight[:, rank:]).astype(LOW)
            for column in range(columns):
                low = 2 * column * piece
                even, odd = slice(low, low + piece), slice(low + piece, low + 2 * piece)
                for value, at, width in ((first, base, 2 * rank), (second, base + 2 * rank, rank)):
                    lanes = slice(at, at + width)
                    keep_ref[column, group, :, lanes] = jnp.where(core == 0, value[even], value[odd])
                    send_ref[column, group, :, lanes] = jnp.where(core == 0, value[odd], value[even])


def recursion_kernel(
    layers, rank, width, place_ref, parts_ref, square_ref, near_ref, far_ref, out_ref, sums_ref, cross_ref
):
    core, column = place_ref[0], place_ref[2]
    count = len(SHIFTS)
    for slot, distance in enumerate(SHIFTS):
        owner = lax.rem(column - distance + count, count)
        for piece_ref, from_core in ((near_ref, core), (far_ref, 1 - core)):
            start = pl.multiple_of((2 * owner + from_core) * rank, rank)
            cross_ref[pl.ds(start, rank), :] = piece_ref[slot]

    total = parts_ref[0].astype(WIDE)
    for source in range(1, parts_ref.shape[0]):
        total = total + parts_ref[source].astype(WIDE)
    sums_ref[...] = total
    rank3 = 3 * rank
    down = [sums_ref[:, k * rank3 : k * rank3 + rank] for k in range(layers)]
    up = [sums_ref[:, k * rank3 + rank : k * rank3 + 2 * rank] for k in range(layers)]
    back = [sums_ref[:, k * rank3 + 2 * rank : (k + 1) * rank3] for k in range(layers)]
    square = square_ref[:, 0:1]

    acts, pres, invs = [], [], []
    for s in range(layers):
        inv = lax.rsqrt(jnp.maximum(square, 0.0) / width + norm_eps)
        pre = inv * down[s]
        act, _ = gelu_pair(pre)
        act = act.astype(LOW)
        acts.append(act)
        pres.append(pre)
        invs.append(inv)
        out_ref[:, s * rank : (s + 1) * rank] = act
        low = s * rank
        forward = dot_nn(act, cross_ref[low : low + rank, low:])
        before = up[s]
        up[s] = before + forward[:, :rank]
        square = square + jnp.sum(act.astype(WIDE) * (before + up[s]), axis=-1, keepdims=True)
        if s + 1 < layers:
            mirrored = dot_nt(act, cross_ref[low + rank :, low : low + rank])
            for k in range(s + 1, layers):
                at = (k - s) * rank
                down[k] = down[k] + forward[:, at : at + rank]
                up[k] = up[k] + mirrored[:, at - rank : at]

    trailing = jnp.zeros_like(square)
    lane = lax.broadcasted_iota(jnp.int32, (square.shape[0], rank), 1)
    tail = jnp.zeros((square.shape[0], rank), WIDE)
    for s in reversed(range(layers)):
        _, slope = gelu_pair(pres[s])
        d_pre = (back[s] - trailing * up[s]) * slope
        coef = invs[s] * invs[s] * (1.0 / width) * jnp.sum(d_pre * pres[s], axis=-1, keepdims=True)
        moved = (invs[s] * d_pre).astype(LOW)
        out_ref[:, (layers + s) * rank : (layers + s + 1) * rank] = moved
        coef_high = coef.astype(LOW).astype(WIDE)
        tail = tail + jnp.where(lane == s, coef_high, 0.0)
        tail = tail + jnp.where(lane == s + layers, coef - coef_high, 0.0)
        if s > 0:
            low = s * rank
            gain_term = dot_nt(moved, cross_ref[:low, low : low + rank])
            scaled_act = (trailing * acts[s].astype(WIDE)).astype(LOW)
            norm_term = dot_nn(scaled_act, cross_ref[low : low + rank, :low])
            for k in range(s):
                sel = slice(k * rank, (k + 1) * rank)
                back[k] = back[k] + gain_term[:, sel] - norm_term[:, sel]
        trailing = trailing + coef
    out_ref[:, 2 * layers * rank :] = tail.astype(LOW)


def expand_kernel(
    layers,
    rank,
    place_ref,
    rows_ref,
    weight_ref,
    near_ref,
    far_ref,
    out_ref,
    grad_ref,
    wide_ref,
    act_ref,
    moved_ref,
    coef_ref,
):
    groups, both_rows, features = rows_ref.shape
    half = both_rows // 2
    piece = near_ref.shape[2]
    span = layers * rank
    core, section, column, line = (place_ref[i] for i in range(4))
    count = len(SHIFTS)
    for group in range(groups):
        base = group * half
        wide_ref[base : base + half, :] = rows_ref[group, :half, :].astype(WIDE)
    for slot_y, step_y in enumerate(SHIFTS):
        group = lax.rem(line - step_y + count, count)
        for slot_x, step_x in enumerate(SHIFTS):
            owner = lax.rem(column - step_x + count, count)
            for coded_ref, from_core in ((near_ref, core), (far_ref, 1 - core)):
                at = pl.multiple_of(group * half + (2 * owner + from_core) * piece, piece)
                dest = pl.ds(at, piece)
                act_ref[dest, :] = coded_ref[slot_y, slot_x, :, :span]
                moved_ref[dest, :] = coded_ref[slot_y, slot_x, :, span : 2 * span]
                coef_ref[dest, :] = coded_ref[slot_y, slot_x, :, 2 * span :].astype(WIDE)

    for layer in range(layers):
        up_weight = weight_ref[lax.rem(section + layer, layers), :, rank:]
        act = act_ref[:, layer * rank : (layer + 1) * rank]
        total = wide_ref[...] + dot_nt(act, up_weight)
        wide_ref[...] = total
        lowered = total.astype(LOW)
        for group in range(groups):
            out_ref[layer, group] = lowered[group * half : (group + 1) * half]

    for group in range(groups):
        base = group * half
        wide_ref[base : base + half, :] = rows_ref[group, half:, :].astype(WIDE)
    for layer in reversed(range(layers)):
        slot = lax.rem(section + layer, layers)
        delta = wide_ref[...].astype(LOW)
        act = act_ref[:, layer * rank : (layer + 1) * rank]
        moved = moved_ref[:, layer * rank : (layer + 1) * rank]
        if layer > 0:
            current = out_ref[layer - 1].reshape(groups * half, features)
        else:
            current = rows_ref[:, :half, :].reshape(groups * half, features)
        grad_ref[slot, :, features:] = dot_tn(act, delta).astype(LOW)
        grad_ref[slot, :, :features] = dot_tn(moved, current).astype(LOW)
        if layer > 0:
            coef = coef_ref[:, layer : layer + 1] + coef_ref[:, layers + layer : layers + layer + 1]
            wide_ref[...] += dot_nt(moved, weight_ref[slot, :, :rank]) - coef * current.astype(WIDE)


def square_kernel(gain_ref, grad_ref, out_ref):
    features = gain_ref.shape[1]
    grad_in = grad_ref[:, :features].astype(WIDE) * gain_ref[...]
    grad_out = grad_ref[:, features:].astype(WIDE)
    total = jnp.sum(grad_in * grad_in) + jnp.sum(grad_out * grad_out)
    out_ref[...] = jnp.full(out_ref.shape, total, WIDE)


def order_kernel(block_ref, out_ref):
    layers, features = block_ref.shape[0], block_ref.shape[3]
    for layer in range(layers):
        out_ref[:, layer * features : (layer + 1) * features] = block_ref[layer, 0]


def update_kernel(limit, sums_ref, gain_ref, grad_ref, *refs):
    features = gain_ref.shape[1]
    sources = refs[:6]
    results = refs[6:]
    total = jnp.sum(sums_ref[...], axis=0, keepdims=True)
    clip = limit / jnp.maximum(jnp.sqrt(total), limit)
    grad_in = (grad_ref[:, :features].astype(WIDE) * gain_ref[...]).T * clip
    updated = adam_update(sources[0][0], sources[1][0], sources[2][0], grad_in)
    for ref, value in zip(results[:3], updated):
        ref[0] = value
    grad_out = grad_ref[:, features:].astype(WIDE) * clip[:, 0:1]
    updated = adam_update(sources[3][0], sources[4][0], sources[5][0], grad_out)
    for ref, value in zip(results[3:], updated):
        ref[0] = value


def shards(
    stack_input,
    out_cotangent,
    norm_gain,
    master_in,
    master_out,
    first_in,
    first_out,
    second_in,
    second_out,
):
    count_x, count_c, count_y, count_z = (lax.axis_size(a) for a in EVERYONE)
    pos_x, pos_c, pos_y, pos_z = (lax.axis_index(a) for a in EVERYONE)
    layers = count_x * count_c
    pos_s = pos_x * count_c + pos_c
    place = jnp.stack([pos_c, pos_s, pos_x, pos_y]).astype(jnp.int32)
    sources = layers * count_y
    tok_rows, model_width = stack_input.shape
    features, rank = master_in.shape[1:]
    piece = tok_rows // layers
    swap_core = [(0, 1), (1, 0)]
    route = [(a * count_z + b, b * count_z + (a + b) % count_z) for a in range(layers) for b in range(count_z)]
    back_route = [(j, i) for i, j in route]
    across = SECTION + ("z",)

    gain_own = lax.dynamic_slice_in_dim(norm_gain, (pos_y * count_z + pos_z) * features, features, 1)
    packed = local_call(
        pack_kernel, jax.ShapeDtypeStruct((features, 2 * rank), LOW), (gain_own, master_in, master_out)
    )
    swapped = lax.ppermute(packed, across, route)
    gain_swapped = lax.ppermute(gain_own, across, route)
    weights = lax.all_gather(swapped, "z", axis=0)

    def blocks_of(rows):
        return jnp.stack(
            [
                lax.dynamic_slice_in_dim(rows, (g * count_z + pos_s) * features, features, 1)
                for g in range(count_y)
            ]
        )

    rows = jnp.concatenate([blocks_of(stack_input), blocks_of(out_cotangent)], axis=1)
    rows = lax.all_to_all(rows, "y", 0, 0, tiled=True)
    own_rows = lax.dynamic_slice_in_dim(stack_input, pos_s * piece, piece, 0).astype(WIDE)
    square = jnp.sum(own_rows * own_rows, axis=-1, keepdims=True)
    square = jnp.broadcast_to(square, (piece, 128))

    lined = gather_line(packed, "x")
    lined = jnp.stack([lined, lax.ppermute(lined, "c", swap_core)])
    cross = lax.dot_general(
        packed[:, rank:], lined, (((0,), (2,)), ((), ())), preferred_element_type=WIDE
    )
    cross = cross.transpose(1, 2, 0, 3)
    ordered = []
    for layer in range(layers):
        owner, from_core = divmod(layer, count_c)
        away = lax.rem(pos_x - owner + count_x, count_x)
        slot = jnp.where(away == count_x - 1, 2, jnp.where(away == 2, 3, away))
        block = lax.dynamic_slice(
            cross, (lax.rem(pos_c + from_core, 2), slot, 0, 0), (1, 1, rank, 2 * rank)
        )[0, 0]
        ordered.append(jnp.where(layer > pos_s, block[:, :rank], block[:, rank:]).astype(LOW))
    cut_r, cut_c = rank // count_z, layers * rank // count_y
    cross = jnp.stack(ordered, axis=1).reshape(count_z, cut_r, count_y, cut_c)
    cross = cross.transpose(2, 0, 1, 3).reshape(count_y * count_z, cut_r, cut_c)
    cross = lax.all_to_all(cross, ("y", "z"), 0, 0, tiled=True)
    cross = jnp.sum(cross.astype(WIDE), axis=0, keepdims=True).astype(LOW)
    cross = jnp.broadcast_to(cross, (count_y * count_z, cut_r, cut_c))
    cross = lax.all_to_all(cross, ("y", "z"), 0, 0, tiled=True)
    cross = cross.reshape(count_y, count_z, cut_r, cut_c).transpose(1, 2, 0, 3)
    cross = cross.reshape(rank, layers * rank)
    cross_near = gather_line(cross, "x")
    cross_far = lax.ppermute(cross_near, "c", swap_core)

    part_shape = jax.ShapeDtypeStruct((count_x, count_y, piece, layers * 3 * rank), LOW)
    keep, send = local_call(
        functools.partial(project_kernel, rank),
        (part_shape, part_shape),
        (rows, weights),
        scalars=place,
        flops=2 * rows.shape[0] * tok_rows * features * layers * rank * 3,
    )
    came = lax.ppermute(send, "c", swap_core)
    parts = (keep.astype(WIDE) + came.astype(WIDE)).astype(LOW)
    parts = parts.reshape(count_x * count_y, piece, layers * 3 * rank)
    parts = lax.all_to_all(parts, ("x", "y"), 0, 0, tiled=True)
    coded_width = 2 * layers * rank + rank
    coded = local_call(
        functools.partial(recursion_kernel, layers, rank, float(model_width)),
        jax.ShapeDtypeStruct((piece, coded_width), LOW),
        (parts, square, cross_near, cross_far),
        scalars=place,
        scratch=[
            pltpu.VMEM((piece, layers * 3 * rank), WIDE),
            pltpu.VMEM((layers * rank, layers * rank), LOW),
        ],
    )
    coded_near = gather_line(gather_line(coded, "x"), "y")
    coded_far = lax.ppermute(coded_near, "c", swap_core)

    group_tokens = count_y * tok_rows
    outputs, grads = local_call(
        functools.partial(expand_kernel, layers, rank),
        (
            jax.ShapeDtypeStruct((layers, count_y, tok_rows, features), LOW),
            jax.ShapeDtypeStruct((layers, rank, 2 * features), LOW),
        ),
        (rows, weights, coded_near, coded_far),
        scalars=place,
        scratch=[
            pltpu.VMEM((group_tokens, features), WIDE),
            pltpu.VMEM((group_tokens, layers * rank), LOW),
            pltpu.VMEM((group_tokens, layers * rank), LOW),
            pltpu.VMEM((group_tokens, rank), WIDE),
        ],
        flops=8 * group_tokens * features * layers * rank,
    )
    grads = lax.psum_scatter(grads, "z", scatter_dimension=0, tiled=True)[0]
    outputs = outputs.reshape(sources, tok_rows, features)
    outputs = lax.all_to_all(outputs, PLANE, 0, 0, tiled=True)
    outputs = outputs.reshape(layers, count_y, tok_rows, features)
    section_rows = pl.pallas_call(
        order_kernel,
        grid=(count_y,),
        out_shape=jax.ShapeDtypeStruct((tok_rows, model_width), LOW),
        in_specs=[pl.BlockSpec((layers, 1, tok_rows, features), lambda i: (0, i, 0, 0))],
        out_specs=pl.BlockSpec((tok_rows, layers * features), lambda i: (0, i)),
        compiler_params=pltpu.CompilerParams(vmem_limit_bytes=VMEM_BYTES),
    )(outputs)

    own_grads = lax.ppermute(grads, across, back_route)
    squares = local_call(
        square_kernel, jax.ShapeDtypeStruct((sources * count_z, 128), WIDE), (gain_swapped, grads)
    )
    squares = lax.all_to_all(squares, EVERYONE, 0, 0, tiled=True)
    norm_limit = clip_rms * math.sqrt(2.0 * model_width * rank * layers)
    shape_in = jax.ShapeDtypeStruct(master_in.shape, WIDE)
    shape_out = jax.ShapeDtypeStruct(master_out.shape, WIDE)
    updated = local_call(
        functools.partial(update_kernel, norm_limit),
        (shape_in,) * 3 + (shape_out,) * 3,
        (squares, gain_own, own_grads, master_in, first_in, second_in, master_out, first_out, second_out),
    )
    new_in, new_first_in, new_second_in, new_out, new_first_out, new_second_out = updated
    return (
        section_rows[None],
        new_in,
        new_out,
        new_first_in,
        new_first_out,
        new_second_in,
        new_second_out,
    )


def solution(mesh):
    layers, groups = mesh.shape["section"], mesh.shape["dp"]
    sizes = (layers // 2, 2, groups // layers, layers)
    fine = Mesh(mesh.devices.reshape(sizes), EVERYONE)
    split = ("y", "z")
    by_rows = P(SECTION, split, None)
    by_cols = P(SECTION, None, split)
    in_specs = (
        P(split, None),
        P(split, None),
        P(SECTION, None),
        by_rows,
        by_cols,
        by_rows,
        by_cols,
        by_rows,
        by_cols,
    )
    out_specs = (by_rows, by_rows, by_cols, by_rows, by_cols, by_rows, by_cols)
    return jax.shard_map(shards, mesh=fine, in_specs=in_specs, out_specs=out_specs, check_vma=False)
```

```python
import functools
import math

import jax
import jax.numpy as jnp
from jax import lax
from jax.experimental import pallas as pl
from jax.experimental.pallas import tpu as pltpu
from jax.sharding import Mesh, PartitionSpec as P

STEP = 10

norm_eps = 1e-05
gelu_coef = 0.7978845608028654
beta_one = 0.9
beta_two = 0.95
adam_eps = 1e-08
learn_rate = 0.05
decay_rate = 0.1
clip_rms = 0.5

LOW = jnp.bfloat16
WIDE = jnp.float32
SECTION = ("x", "c")
PLANE = ("x", "c", "y")
EVERYONE = ("x", "c", "y", "z")
SHIFTS = (0, 1, -1, 2)
TURNS = (0, 4, 3, 7, 2, 6, 1, 5)
VMEM_BYTES = 48 * 1024 * 1024


def dot_nn(left, right):
    return lax.dot_general(left, right, (((1,), (0,)), ((), ())), preferred_element_type=WIDE)


def dot_nt(left, right):
    return lax.dot_general(left, right, (((1,), (1,)), ((), ())), preferred_element_type=WIDE)


def dot_tn(left, right):
    return lax.dot_general(left, right, (((0,), (0,)), ((), ())), preferred_element_type=WIDE)


def gelu_pair(hidden_pre):
    inner_arg = gelu_coef * (hidden_pre + 0.044715 * hidden_pre * hidden_pre * hidden_pre)
    tangent = jnp.tanh(inner_arg)
    gelu_value = 0.5 * hidden_pre * (1.0 + tangent)
    gelu_slope = 0.5 * (1.0 + tangent) + 0.5 * hidden_pre * (
        1.0 - tangent * tangent
    ) * gelu_coef * (1.0 + 3.0 * 0.044715 * hidden_pre * hidden_pre)
    return (gelu_value, gelu_slope)


def adam_update(master, first, second, grad):
    first_new = beta_one * first + (1.0 - beta_one) * grad
    second_new = beta_two * second + (1.0 - beta_two) * grad * grad
    first_hat = first_new / (1.0 - beta_one**STEP)
    second_hat = second_new / (1.0 - beta_two**STEP)
    master_new = master - learn_rate * (
        first_hat / (jnp.sqrt(second_hat) + adam_eps) + decay_rate * master
    )
    return (master_new, first_new, second_new)


def local_call(kernel, out_shape, operands, scalars=None, scratch=(), flops=0):
    specs = jax.tree.map(lambda _: pl.BlockSpec(memory_space=pltpu.VMEM), out_shape)
    moved = sum(a.size * a.dtype.itemsize for a in operands)
    moved += sum(a.size * a.dtype.itemsize for a in jax.tree.leaves(out_shape))
    in_specs = [pl.BlockSpec(memory_space=pltpu.VMEM)] * len(operands)
    if scalars is not None:
        operands = (scalars,) + tuple(operands)
        in_specs = [pl.BlockSpec(memory_space=pltpu.SMEM)] + in_specs
    return pl.pallas_call(
        kernel,
        out_shape=out_shape,
        in_specs=in_specs,
        out_specs=specs,
        scratch_shapes=list(scratch),
        compiler_params=pltpu.CompilerParams(vmem_limit_bytes=VMEM_BYTES),
        cost_estimate=pl.CostEstimate(flops=flops, bytes_accessed=moved, transcendentals=0),
    )(*operands)


def shifted(block, axis, distance):
    size = lax.axis_size(axis)
    return lax.ppermute(block, axis, [(i, (i + distance) % size) for i in range(size)])


def gather_line(block, axis):
    return jnp.stack([block] + [shifted(block, axis, d) for d in SHIFTS[1:]])


def pack_kernel(gain_ref, in_ref, out_ref, pack_ref):
    features, rank = in_ref.shape[1:]
    gain = jnp.broadcast_to(gain_ref[...], (rank, features)).T
    work_in = in_ref[0].astype(LOW).astype(WIDE)
    pack_ref[:, :rank] = (work_in * gain).astype(LOW)
    pack_ref[:, rank:] = out_ref[0].T.astype(LOW)


def project_kernel(rank, place_ref, rows_ref, weight_ref, keep_ref, send_ref):
    groups, both_rows, _ = rows_ref.shape
    layers = weight_ref.shape[0]
    half = both_rows // 2
    columns = keep_ref.shape[0]
    piece = half // (2 * columns)
    core, section = place_ref[0], place_ref[1]
    for layer in range(layers):
        weight = weight_ref[lax.rem(section + TURNS[layer], layers)]
        base = layer * 3 * rank
        for group in range(groups):
            first = dot_nn(rows_ref[group, :half, :], weight).astype(LOW)
            second = dot_nn(rows_ref[group, half:, :], weight[:, rank:]).astype(LOW)
            for column in range(columns):
                low = 2 * column * piece
                even, odd = slice(low, low + piece), slice(low + piece, low + 2 * piece)
                for value, at, width in ((first, base, 2 * rank), (second, base + 2 * rank, rank)):
                    lanes = slice(at, at + width)
                    keep_ref[column, group, :, lanes] = jnp.where(core == 0, value[even], value[odd])
                    send_ref[column, group, :, lanes] = jnp.where(core == 0, value[odd], value[even])


def recursion_kernel(
    layers, rank, width, place_ref, parts_ref, square_ref, near_ref, far_ref, out_ref, sums_ref, cross_ref
):
    core, column = place_ref[0], place_ref[2]
    count = len(SHIFTS)
    for slot, distance in enumerate(SHIFTS):
        owner = lax.rem(column - distance + count, count)
        for piece_ref, from_core in ((near_ref, core), (far_ref, 1 - core)):
            start = pl.multiple_of((2 * owner + from_core) * rank, rank)
            cross_ref[pl.ds(start, rank), :] = piece_ref[slot]

    total = parts_ref[0].astype(WIDE)
    for source in range(1, parts_ref.shape[0]):
        total = total + parts_ref[source].astype(WIDE)
    sums_ref[...] = total
    rank3 = 3 * rank
    down = [sums_ref[:, k * rank3 : k * rank3 + rank] for k in range(layers)]
    up = [sums_ref[:, k * rank3 + rank : k * rank3 + 2 * rank] for k in range(layers)]
    back = [sums_ref[:, k * rank3 + 2 * rank : (k + 1) * rank3] for k in range(layers)]
    square = square_ref[:, 0:1]

    acts, pres, invs = [], [], []
    for s in range(layers):
        inv = lax.rsqrt(jnp.maximum(square, 0.0) / width + norm_eps)
        pre = inv * down[s]
        act, _ = gelu_pair(pre)
        act = act.astype(LOW)
        acts.append(act)
        pres.append(pre)
        invs.append(inv)
        out_ref[:, s * rank : (s + 1) * rank] = act
        low = s * rank
        forward = dot_nn(act, cross_ref[low : low + rank, low:])
        before = up[s]
        up[s] = before + forward[:, :rank]
        square = square + jnp.sum(act.astype(WIDE) * (before + up[s]), axis=-1, keepdims=True)
        if s + 1 < layers:
            mirrored = dot_nt(act, cross_ref[low + rank :, low : low + rank])
            for k in range(s + 1, layers):
                at = (k - s) * rank
                down[k] = down[k] + forward[:, at : at + rank]
                up[k] = up[k] + mirrored[:, at - rank : at]

    trailing = jnp.zeros_like(square)
    lane = lax.broadcasted_iota(jnp.int32, (square.shape[0], rank), 1)
    tail = jnp.zeros((square.shape[0], rank), WIDE)
    for s in reversed(range(layers)):
        _, slope = gelu_pair(pres[s])
        d_pre = (back[s] - trailing * up[s]) * slope
        coef = invs[s] * invs[s] * (1.0 / width) * jnp.sum(d_pre * pres[s], axis=-1, keepdims=True)
        moved = (invs[s] * d_pre).astype(LOW)
        out_ref[:, (layers + s) * rank : (layers + s + 1) * rank] = moved
        coef_high = coef.astype(LOW).astype(WIDE)
        tail = tail + jnp.where(lane == s, coef_high, 0.0)
        tail = tail + jnp.where(lane == s + layers, coef - coef_high, 0.0)
        if s > 0:
            low = s * rank
            gain_term = dot_nt(moved, cross_ref[:low, low : low + rank])
            scaled_act = (trailing * acts[s].astype(WIDE)).astype(LOW)
            norm_term = dot_nn(scaled_act, cross_ref[low : low + rank, :low])
            for k in range(s):
                sel = slice(k * rank, (k + 1) * rank)
                back[k] = back[k] + gain_term[:, sel] - norm_term[:, sel]
        trailing = trailing + coef
    out_ref[:, 2 * layers * rank :] = tail.astype(LOW)


def expand_kernel(
    layers,
    rank,
    place_ref,
    rows_ref,
    weight_ref,
    near_ref,
    far_ref,
    out_ref,
    grad_ref,
    wide_ref,
    act_ref,
    moved_ref,
    coef_ref,
):
    groups, both_rows, features = rows_ref.shape
    half = both_rows // 2
    piece = near_ref.shape[2]
    span = layers * rank
    core, section, column, line = (place_ref[i] for i in range(4))
    count = len(SHIFTS)
    for group in range(groups):
        base = group * half
        wide_ref[base : base + half, :] = rows_ref[group, :half, :].astype(WIDE)
    for slot_y, step_y in enumerate(SHIFTS):
        group = lax.rem(line - step_y + count, count)
        for slot_x, step_x in enumerate(SHIFTS):
            owner = lax.rem(column - step_x + count, count)
            for coded_ref, from_core in ((near_ref, core), (far_ref, 1 - core)):
                at = pl.multiple_of(group * half + (2 * owner + from_core) * piece, piece)
                dest = pl.ds(at, piece)
                act_ref[dest, :] = coded_ref[slot_y, slot_x, :, :span]
                moved_ref[dest, :] = coded_ref[slot_y, slot_x, :, span : 2 * span]
                coef_ref[dest, :] = coded_ref[slot_y, slot_x, :, 2 * span :].astype(WIDE)

    for layer in range(layers):
        up_weight = weight_ref[lax.rem(section + TURNS[layer], layers), :, rank:]
        act = act_ref[:, layer * rank : (layer + 1) * rank]
        total = wide_ref[...] + dot_nt(act, up_weight)
        wide_ref[...] = total
        lowered = total.astype(LOW)
        for group in range(groups):
            out_ref[layer, group] = lowered[group * half : (group + 1) * half]

    for group in range(groups):
        base = group * half
        wide_ref[base : base + half, :] = rows_ref[group, half:, :].astype(WIDE)
    for layer in reversed(range(layers)):
        slot = lax.rem(section + TURNS[layer], layers)
        delta = wide_ref[...].astype(LOW)
        act = act_ref[:, layer * rank : (layer + 1) * rank]
        moved = moved_ref[:, layer * rank : (layer + 1) * rank]
        if layer > 0:
            current = out_ref[layer - 1].reshape(groups * half, features)
        else:
            current = rows_ref[:, :half, :].reshape(groups * half, features)
        grad_ref[slot, :, features:] = dot_tn(act, delta).astype(LOW)
        grad_ref[slot, :, :features] = dot_tn(moved, current).astype(LOW)
        if layer > 0:
            coef = coef_ref[:, layer : layer + 1] + coef_ref[:, layers + layer : layers + layer + 1]
            wide_ref[...] += dot_nt(moved, weight_ref[slot, :, :rank]) - coef * current.astype(WIDE)


def square_kernel(gain_ref, grad_ref, out_ref):
    features = gain_ref.shape[1]
    grad_in = grad_ref[:, :features].astype(WIDE) * gain_ref[...]
    grad_out = grad_ref[:, features:].astype(WIDE)
    total = jnp.sum(grad_in * grad_in) + jnp.sum(grad_out * grad_out)
    out_ref[...] = jnp.full(out_ref.shape, total, WIDE)


def order_kernel(block_ref, out_ref):
    layers, features = block_ref.shape[0], block_ref.shape[3]
    for layer in range(layers):
        out_ref[:, layer * features : (layer + 1) * features] = block_ref[layer, 0]


def update_kernel(limit, sums_ref, gain_ref, grad_ref, *refs):
    features = gain_ref.shape[1]
    sources = refs[:6]
    results = refs[6:]
    total = jnp.sum(sums_ref[...], axis=0, keepdims=True)
    clip = limit / jnp.maximum(jnp.sqrt(total), limit)
    grad_in = (grad_ref[:, :features].astype(WIDE) * gain_ref[...]).T * clip
    updated = adam_update(sources[0][0], sources[1][0], sources[2][0], grad_in)
    for ref, value in zip(results[:3], updated):
        ref[0] = value
    grad_out = grad_ref[:, features:].astype(WIDE) * clip[:, 0:1]
    updated = adam_update(sources[3][0], sources[4][0], sources[5][0], grad_out)
    for ref, value in zip(results[3:], updated):
        ref[0] = value


def shards(
    stack_input,
    out_cotangent,
    norm_gain,
    master_in,
    master_out,
    first_in,
    first_out,
    second_in,
    second_out,
):
    count_x, count_c, count_y, count_z = (lax.axis_size(a) for a in EVERYONE)
    pos_x, pos_c, pos_y, pos_z = (lax.axis_index(a) for a in EVERYONE)
    layers = count_x * count_c
    pos_s = pos_x * count_c + pos_c
    place = jnp.stack([pos_c, pos_s, pos_x, pos_y]).astype(jnp.int32)
    sources = layers * count_y
    tok_rows, model_width = stack_input.shape
    features, rank = master_in.shape[1:]
    piece = tok_rows // layers
    swap_core = [(0, 1), (1, 0)]
    route = [
        (a * count_z + b, b * count_z + (b + TURNS[a]) % count_z)
        for a in range(layers)
        for b in range(count_z)
    ]
    back_route = [(j, i) for i, j in route]
    across = SECTION + ("z",)

    gain_own = lax.dynamic_slice_in_dim(norm_gain, (pos_y * count_z + pos_z) * features, features, 1)
    packed = local_call(
        pack_kernel, jax.ShapeDtypeStruct((features, 2 * rank), LOW), (gain_own, master_in, master_out)
    )
    swapped = lax.ppermute(packed, across, route)
    lined = lax.all_gather(packed, SECTION, axis=0)
    swapped, lined = lax.optimization_barrier((swapped, lined))
    weights = lax.all_gather(swapped, "z", axis=0)

    def blocks_of(rows):
        return jnp.stack(
            [
                lax.dynamic_slice_in_dim(rows, (g * count_z + pos_s) * features, features, 1)
                for g in range(count_y)
            ]
        )

    rows = jnp.concatenate([blocks_of(stack_input), blocks_of(out_cotangent)], axis=1)
    rows = lax.all_to_all(rows, "y", 0, 0, tiled=True)
    own_rows = lax.dynamic_slice_in_dim(stack_input, pos_s * piece, piece, 0).astype(WIDE)
    square = jnp.sum(own_rows * own_rows, axis=-1, keepdims=True)
    square = jnp.broadcast_to(square, (piece, 128))

    cross = lax.dot_general(
        packed[:, rank:], lined, (((0,), (1,)), ((), ())), preferred_element_type=WIDE
    )
    later = (jnp.arange(layers) > pos_s)[None, :, None]
    cross = jnp.where(later, cross[..., :rank], cross[..., rank:]).astype(LOW)
    cut_r, cut_c = rank // count_z, layers * rank // count_y
    cross = cross.reshape(count_z, cut_r, count_y, cut_c)
    cross = cross.transpose(2, 0, 1, 3).reshape(count_y * count_z, cut_r, cut_c)
    cross, rows = lax.optimization_barrier((cross, rows))
    cross = lax.all_to_all(cross, ("y", "z"), 0, 0, tiled=True)
    cross = jnp.sum(cross.astype(WIDE), axis=0, keepdims=True).astype(LOW)
    cross = jnp.broadcast_to(cross, (count_y * count_z, cut_r, cut_c))
    cross = lax.all_to_all(cross, ("y", "z"), 0, 0, tiled=True)
    cross = cross.reshape(count_y, count_z, cut_r, cut_c).transpose(1, 2, 0, 3)
    cross = cross.reshape(rank, layers * rank)
    cross, rows = lax.optimization_barrier((cross, rows))
    cross_near = gather_line(cross, "x")
    cross_far = lax.ppermute(cross_near, "c", swap_core)

    part_shape = jax.ShapeDtypeStruct((count_x, count_y, piece, layers * 3 * rank), LOW)
    keep, send = local_call(
        functools.partial(project_kernel, rank),
        (part_shape, part_shape),
        (rows, weights),
        scalars=place,
        flops=2 * rows.shape[0] * tok_rows * features * layers * rank * 3,
    )
    came = lax.ppermute(send, "c", swap_core)
    parts = (keep.astype(WIDE) + came.astype(WIDE)).astype(LOW)
    parts = parts.reshape(count_x * count_y, piece, layers * 3 * rank)
    parts = lax.all_to_all(parts, ("x", "y"), 0, 0, tiled=True)
    coded_width = 2 * layers * rank + rank
    coded = local_call(
        functools.partial(recursion_kernel, layers, rank, float(model_width)),
        jax.ShapeDtypeStruct((piece, coded_width), LOW),
        (parts, square, cross_near, cross_far),
        scalars=place,
        scratch=[
            pltpu.VMEM((piece, layers * 3 * rank), WIDE),
            pltpu.VMEM((layers * rank, layers * rank), LOW),
        ],
    )
    coded_near = gather_line(gather_line(coded, "x"), "y")
    coded_far = lax.ppermute(coded_near, "c", swap_core)

    group_tokens = count_y * tok_rows
    outputs, grads = local_call(
        functools.partial(expand_kernel, layers, rank),
        (
            jax.ShapeDtypeStruct((layers, count_y, tok_rows, features), LOW),
            jax.ShapeDtypeStruct((layers, rank, 2 * features), LOW),
        ),
        (rows, weights, coded_near, coded_far),
        scalars=place,
        scratch=[
            pltpu.VMEM((group_tokens, features), WIDE),
            pltpu.VMEM((group_tokens, layers * rank), LOW),
            pltpu.VMEM((group_tokens, layers * rank), LOW),
            pltpu.VMEM((group_tokens, rank), WIDE),
        ],
        flops=8 * group_tokens * features * layers * rank,
    )
    grads = lax.psum_scatter(grads, "z", scatter_dimension=0, tiled=True)[0]
    outputs = outputs.reshape(sources, tok_rows, features)
    outputs = lax.all_to_all(outputs, PLANE, 0, 0, tiled=True)
    outputs = outputs.reshape(layers, count_y, tok_rows, features)
    section_rows = pl.pallas_call(
        order_kernel,
        grid=(count_y,),
        out_shape=jax.ShapeDtypeStruct((tok_rows, model_width), LOW),
        in_specs=[pl.BlockSpec((layers, 1, tok_rows, features), lambda i: (0, i, 0, 0))],
        out_specs=pl.BlockSpec((tok_rows, layers * features), lambda i: (0, i)),
        compiler_params=pltpu.CompilerParams(vmem_limit_bytes=VMEM_BYTES),
    )(outputs)

    own_grads = lax.ppermute(grads, across, back_route)
    squares = local_call(
        square_kernel, jax.ShapeDtypeStruct((sources * count_z, 128), WIDE), (gain_own, own_grads)
    )
    squares = lax.all_to_all(squares, EVERYONE, 0, 0, tiled=True)
    norm_limit = clip_rms * math.sqrt(2.0 * model_width * rank * layers)
    shape_in = jax.ShapeDtypeStruct(master_in.shape, WIDE)
    shape_out = jax.ShapeDtypeStruct(master_out.shape, WIDE)
    updated = local_call(
        functools.partial(update_kernel, norm_limit),
        (shape_in,) * 3 + (shape_out,) * 3,
        (squares, gain_own, own_grads, master_in, first_in, second_in, master_out, first_out, second_out),
    )
    new_in, new_first_in, new_second_in, new_out, new_first_out, new_second_out = updated
    return (
        section_rows[None],
        new_in,
        new_out,
        new_first_in,
        new_first_out,
        new_second_in,
        new_second_out,
    )


def solution(mesh):
    layers, groups = mesh.shape["section"], mesh.shape["dp"]
    sizes = (layers // 2, 2, groups // layers, layers)
    fine = Mesh(mesh.devices.reshape(sizes), EVERYONE)
    split = ("y", "z")
    by_rows = P(SECTION, split, None)
    by_cols = P(SECTION, None, split)
    in_specs = (
        P(split, None),
        P(split, None),
        P(SECTION, None),
        by_rows,
        by_cols,
        by_rows,
        by_cols,
        by_rows,
        by_cols,
    )
    out_specs = (by_rows, by_rows, by_cols, by_rows, by_cols, by_rows, by_cols)
    return jax.shard_map(shards, mesh=fine, in_specs=in_specs, out_specs=out_specs, check_vma=False)
```

```python
import functools
import math

import jax
import jax.numpy as jnp
from jax import lax
from jax.experimental import pallas as pl
from jax.experimental.pallas import tpu as pltpu
from jax.sharding import Mesh, PartitionSpec as P

STEP = 10

norm_eps = 1e-05
gelu_coef = 0.7978845608028654
beta_one = 0.9
beta_two = 0.95
adam_eps = 1e-08
learn_rate = 0.05
decay_rate = 0.1
clip_rms = 0.5

LOW = jnp.bfloat16
WIDE = jnp.float32
SECTION = ("x", "c")
PLANE = ("x", "c", "y")
EVERYONE = ("x", "c", "y", "z")
SHIFTS = (0, 1, -1, 2)
TURNS = (0, 4, 3, 7, 2, 6, 1, 5)
VMEM_BYTES = 48 * 1024 * 1024


def dot_nn(left, right):
    return lax.dot_general(left, right, (((1,), (0,)), ((), ())), preferred_element_type=WIDE)


def dot_nt(left, right):
    return lax.dot_general(left, right, (((1,), (1,)), ((), ())), preferred_element_type=WIDE)


def dot_tn(left, right):
    return lax.dot_general(left, right, (((0,), (0,)), ((), ())), preferred_element_type=WIDE)


def gelu_pair(hidden_pre):
    inner_arg = gelu_coef * (hidden_pre + 0.044715 * hidden_pre * hidden_pre * hidden_pre)
    tangent = jnp.tanh(inner_arg)
    gelu_value = 0.5 * hidden_pre * (1.0 + tangent)
    gelu_slope = 0.5 * (1.0 + tangent) + 0.5 * hidden_pre * (
        1.0 - tangent * tangent
    ) * gelu_coef * (1.0 + 3.0 * 0.044715 * hidden_pre * hidden_pre)
    return (gelu_value, gelu_slope)


def adam_update(master, first, second, grad):
    first_new = beta_one * first + (1.0 - beta_one) * grad
    second_new = beta_two * second + (1.0 - beta_two) * grad * grad
    first_hat = first_new / (1.0 - beta_one**STEP)
    second_hat = second_new / (1.0 - beta_two**STEP)
    master_new = master - learn_rate * (
        first_hat / (jnp.sqrt(second_hat) + adam_eps) + decay_rate * master
    )
    return (master_new, first_new, second_new)


def local_call(kernel, out_shape, operands, scalars=None, scratch=(), flops=0):
    specs = jax.tree.map(lambda _: pl.BlockSpec(memory_space=pltpu.VMEM), out_shape)
    moved = sum(a.size * a.dtype.itemsize for a in operands)
    moved += sum(a.size * a.dtype.itemsize for a in jax.tree.leaves(out_shape))
    in_specs = [pl.BlockSpec(memory_space=pltpu.VMEM)] * len(operands)
    if scalars is not None:
        operands = (scalars,) + tuple(operands)
        in_specs = [pl.BlockSpec(memory_space=pltpu.SMEM)] + in_specs
    return pl.pallas_call(
        kernel,
        out_shape=out_shape,
        in_specs=in_specs,
        out_specs=specs,
        scratch_shapes=list(scratch),
        compiler_params=pltpu.CompilerParams(vmem_limit_bytes=VMEM_BYTES),
        cost_estimate=pl.CostEstimate(flops=flops, bytes_accessed=moved, transcendentals=0),
    )(*operands)


def shifted(block, axis, distance):
    size = lax.axis_size(axis)
    return lax.ppermute(block, axis, [(i, (i + distance) % size) for i in range(size)])


def gather_line(block, axis):
    return jnp.stack([block] + [shifted(block, axis, d) for d in SHIFTS[1:]])


def pack_kernel(gain_ref, in_ref, out_ref, pack_ref):
    features, rank = in_ref.shape[1:]
    gain = jnp.broadcast_to(gain_ref[...], (rank, features)).T
    work_in = in_ref[0].astype(LOW).astype(WIDE)
    pack_ref[:, :rank] = (work_in * gain).astype(LOW)
    pack_ref[:, rank:] = out_ref[0].T.astype(LOW)


def cross_kernel(rank, place_ref, own_ref, near_ref, far_ref, out_ref):
    core, section, column = place_ref[0], place_ref[1], place_ref[2]
    count = len(SHIFTS)
    cut = out_ref.shape[1]
    cuts = rank // cut
    own = own_ref[:, rank:].T
    for slot, step in enumerate(SHIFTS):
        owner = lax.rem(column - step + count, count)
        blocks = []
        for line_ref, from_core in ((near_ref, core), (far_ref, 1 - core)):
            both = dot_nn(own, line_ref[slot])
            later = 2 * owner + from_core > section
            blocks.append(jnp.where(later, both[:, :rank], both[:, rank:]).astype(LOW))
        even = jnp.where(core == 0, blocks[0], blocks[1])
        odd = jnp.where(core == 0, blocks[1], blocks[0])
        for k in range(cuts):
            sel = slice(k * cut, (k + 1) * cut)
            out_ref[owner * cuts + k, :, :rank] = even[sel]
            out_ref[owner * cuts + k, :, rank:] = odd[sel]


def project_kernel(rank, place_ref, rows_ref, weight_ref, keep_ref, send_ref):
    groups, both_rows, _ = rows_ref.shape
    layers = weight_ref.shape[0]
    half = both_rows // 2
    columns = keep_ref.shape[0]
    piece = half // (2 * columns)
    core, section = place_ref[0], place_ref[1]
    for layer in range(layers):
        weight = weight_ref[lax.rem(section + TURNS[layer], layers)]
        base = layer * 3 * rank
        for group in range(groups):
            first = dot_nn(rows_ref[group, :half, :], weight).astype(LOW)
            second = dot_nn(rows_ref[group, half:, :], weight[:, rank:]).astype(LOW)
            for column in range(columns):
                low = 2 * column * piece
                even, odd = slice(low, low + piece), slice(low + piece, low + 2 * piece)
                for value, at, width in ((first, base, 2 * rank), (second, base + 2 * rank, rank)):
                    lanes = slice(at, at + width)
                    keep_ref[column, group, :, lanes] = jnp.where(core == 0, value[even], value[odd])
                    send_ref[column, group, :, lanes] = jnp.where(core == 0, value[odd], value[even])


def recursion_kernel(
    layers, rank, width, place_ref, parts_ref, square_ref, near_ref, far_ref, act_ref, moved_ref, sums_ref, cross_ref
):
    core, column = place_ref[0], place_ref[2]
    count = len(SHIFTS)
    pieces, cut = near_ref.shape[1:3]
    cuts = rank // cut
    for slot, distance in enumerate(SHIFTS):
        owner = lax.rem(column - distance + count, count)
        for piece_ref, from_core in ((near_ref, core), (far_ref, 1 - core)):
            start = (2 * owner + from_core) * rank
            for k in range(pieces):
                at = pl.multiple_of(start + (k % cuts) * cut, cut)
                low = (k // cuts) * 2 * rank
                cross_ref[pl.ds(at, cut), low : low + 2 * rank] = piece_ref[slot, k]

    total = parts_ref[0].astype(WIDE)
    for source in range(1, parts_ref.shape[0]):
        total = total + parts_ref[source].astype(WIDE)
    sums_ref[...] = total
    rank3 = 3 * rank
    down = [sums_ref[:, k * rank3 : k * rank3 + rank] for k in range(layers)]
    up = [sums_ref[:, k * rank3 + rank : k * rank3 + 2 * rank] for k in range(layers)]
    back = [sums_ref[:, k * rank3 + 2 * rank : (k + 1) * rank3] for k in range(layers)]
    square = square_ref[:, 0:1]

    acts, pres, invs = [], [], []
    for s in range(layers):
        inv = lax.rsqrt(jnp.maximum(square, 0.0) / width + norm_eps)
        pre = inv * down[s]
        act, _ = gelu_pair(pre)
        act = act.astype(LOW)
        acts.append(act)
        pres.append(pre)
        invs.append(inv)
        act_ref[:, s * rank : (s + 1) * rank] = act
        low = s * rank
        forward = dot_nn(act, cross_ref[low : low + rank, low:])
        before = up[s]
        up[s] = before + forward[:, :rank]
        square = square + jnp.sum(act.astype(WIDE) * (before + up[s]), axis=-1, keepdims=True)
        if s + 1 < layers:
            mirrored = dot_nt(act, cross_ref[low + rank :, low : low + rank])
            for k in range(s + 1, layers):
                at = (k - s) * rank
                down[k] = down[k] + forward[:, at : at + rank]
                up[k] = up[k] + mirrored[:, at - rank : at]

    trailing = jnp.zeros_like(square)
    lane = lax.broadcasted_iota(jnp.int32, (square.shape[0], rank), 1)
    tail = jnp.zeros((square.shape[0], rank), WIDE)
    for s in reversed(range(layers)):
        _, slope = gelu_pair(pres[s])
        d_pre = (back[s] - trailing * up[s]) * slope
        coef = invs[s] * invs[s] * (1.0 / width) * jnp.sum(d_pre * pres[s], axis=-1, keepdims=True)
        moved = (invs[s] * d_pre).astype(LOW)
        moved_ref[:, s * rank : (s + 1) * rank] = moved
        coef_high = coef.astype(LOW).astype(WIDE)
        tail = tail + jnp.where(lane == s, coef_high, 0.0)
        tail = tail + jnp.where(lane == s + layers, coef - coef_high, 0.0)
        if s > 0:
            low = s * rank
            gain_term = dot_nt(moved, cross_ref[:low, low : low + rank])
            scaled_act = (trailing * acts[s].astype(WIDE)).astype(LOW)
            norm_term = dot_nn(scaled_act, cross_ref[low : low + rank, :low])
            for k in range(s):
                sel = slice(k * rank, (k + 1) * rank)
                back[k] = back[k] + gain_term[:, sel] - norm_term[:, sel]
        trailing = trailing + coef
    act_ref[:, layers * rank :] = tail.astype(LOW)


def expand_kernel(
    layers,
    rank,
    place_ref,
    rows_ref,
    weight_ref,
    act_near_ref,
    act_far_ref,
    move_near_ref,
    move_far_ref,
    out_ref,
    grad_ref,
    wide_ref,
    act_ref,
    moved_ref,
    coef_ref,
):
    groups, both_rows, features = rows_ref.shape
    half = both_rows // 2
    piece = act_near_ref.shape[2]
    span = layers * rank
    core, section, column, line = (place_ref[i] for i in range(4))
    count = len(SHIFTS)
    for group in range(groups):
        base = group * half
        wide_ref[base : base + half, :] = rows_ref[group, :half, :].astype(WIDE)
    for slot_y, step_y in enumerate(SHIFTS):
        group = lax.rem(line - step_y + count, count)
        for slot_x, step_x in enumerate(SHIFTS):
            owner = lax.rem(column - step_x + count, count)
            for some_act, some_move, from_core in (
                (act_near_ref, move_near_ref, core),
                (act_far_ref, move_far_ref, 1 - core),
            ):
                at = pl.multiple_of(group * half + (2 * owner + from_core) * piece, piece)
                dest = pl.ds(at, piece)
                act_ref[dest, :] = some_act[slot_y, slot_x, :, :span]
                coef_ref[dest, :] = some_act[slot_y, slot_x, :, span:].astype(WIDE)
                moved_ref[dest, :] = some_move[slot_x, slot_y]

    for layer in range(layers):
        up_weight = weight_ref[lax.rem(section + TURNS[layer], layers), :, rank:]
        act = act_ref[:, layer * rank : (layer + 1) * rank]
        total = wide_ref[...] + dot_nt(act, up_weight)
        wide_ref[...] = total
        lowered = total.astype(LOW)
        for group in range(groups):
            out_ref[layer, group] = lowered[group * half : (group + 1) * half]

    for group in range(groups):
        base = group * half
        wide_ref[base : base + half, :] = rows_ref[group, half:, :].astype(WIDE)
    for layer in reversed(range(layers)):
        slot = lax.rem(section + TURNS[layer], layers)
        delta = wide_ref[...].astype(LOW)
        act = act_ref[:, layer * rank : (layer + 1) * rank]
        moved = moved_ref[:, layer * rank : (layer + 1) * rank]
        if layer > 0:
            current = out_ref[layer - 1].reshape(groups * half, features)
        else:
            current = rows_ref[:, :half, :].reshape(groups * half, features)
        grad_ref[slot, :, features:] = dot_tn(act, delta).astype(LOW)
        grad_ref[slot, :, :features] = dot_tn(moved, current).astype(LOW)
        if layer > 0:
            coef = coef_ref[:, layer : layer + 1] + coef_ref[:, layers + layer : layers + layer + 1]
            wide_ref[...] += dot_nt(moved, weight_ref[slot, :, :rank]) - coef * current.astype(WIDE)


def settle_kernel(gain_ref, grad_ref, in_ref, out_ref, square_ref):
    features = gain_ref.shape[1]
    grad_in = grad_ref[:, :features].astype(WIDE) * gain_ref[...]
    grad_out = grad_ref[:, features:].astype(WIDE)
    in_ref[...] = grad_in.T
    out_ref[...] = grad_out
    total = jnp.sum(grad_in * grad_in) + jnp.sum(grad_out * grad_out)
    square_ref[...] = jnp.full(square_ref.shape, total, WIDE)


def order_kernel(block_ref, out_ref):
    layers, features = block_ref.shape[0], block_ref.shape[3]
    for layer in range(layers):
        out_ref[:, layer * features : (layer + 1) * features] = block_ref[layer, 0]


def shards(
    stack_input,
    out_cotangent,
    norm_gain,
    master_in,
    master_out,
    first_in,
    first_out,
    second_in,
    second_out,
):
    count_x, count_c, count_y, count_z = (lax.axis_size(a) for a in EVERYONE)
    pos_x, pos_c, pos_y, pos_z = (lax.axis_index(a) for a in EVERYONE)
    layers = count_x * count_c
    pos_s = pos_x * count_c + pos_c
    place = jnp.stack([pos_c, pos_s, pos_x, pos_y]).astype(jnp.int32)
    sources = layers * count_y
    tok_rows, model_width = stack_input.shape
    features, rank = master_in.shape[1:]
    piece = tok_rows // layers
    swap_core = [(0, 1), (1, 0)]
    route = [
        (a * count_z + b, b * count_z + (b + TURNS[a]) % count_z)
        for a in range(layers)
        for b in range(count_z)
    ]
    back_route = [(j, i) for i, j in route]
    across = SECTION + ("z",)

    gain_own = lax.dynamic_slice_in_dim(norm_gain, (pos_y * count_z + pos_z) * features, features, 1)
    packed = local_call(
        pack_kernel, jax.ShapeDtypeStruct((features, 2 * rank), LOW), (gain_own, master_in, master_out)
    )
    swapped = lax.ppermute(packed, across, route)
    lined_near = gather_line(packed, "x")
    lined_far = lax.ppermute(lined_near, "c", swap_core)

    def blocks_of(rows):
        return jnp.stack(
            [
                lax.dynamic_slice_in_dim(rows, (g * count_z + pos_s) * features, features, 1)
                for g in range(count_y)
            ]
        )

    rows = jnp.concatenate([blocks_of(stack_input), blocks_of(out_cotangent)], axis=1)
    rows = lax.all_to_all(rows, "y", 0, 0, tiled=True)
    swapped, lined_near, lined_far, rows = lax.optimization_barrier((swapped, lined_near, lined_far, rows))
    weights = lax.all_gather(swapped, "z", axis=0)
    own_rows = lax.dynamic_slice_in_dim(stack_input, pos_s * piece, piece, 0).astype(WIDE)
    square = jnp.sum(own_rows * own_rows, axis=-1, keepdims=True)
    square = jnp.broadcast_to(square, (piece, 128))

    cut_r, cut_c = rank // count_z, count_c * rank
    cross = local_call(
        functools.partial(cross_kernel, rank),
        jax.ShapeDtypeStruct((count_y * count_z, cut_r, cut_c), LOW),
        (packed, lined_near, lined_far),
        scalars=place,
    )
    cross = lax.all_to_all(cross, ("y", "z"), 0, 0, tiled=True)
    cross = jnp.sum(cross.astype(WIDE), axis=0, keepdims=True).astype(LOW)
    cross = jnp.broadcast_to(cross, (count_y * count_z, cut_r, cut_c))
    cross = lax.all_to_all(cross, ("y", "z"), 0, 0, tiled=True)
    cross_near = gather_line(cross, "x")
    cross_near, rows = lax.optimization_barrier((cross_near, rows))
    cross_far = lax.ppermute(cross_near, "c", swap_core)

    part_shape = jax.ShapeDtypeStruct((count_x, count_y, piece, layers * 3 * rank), LOW)
    keep, send = local_call(
        functools.partial(project_kernel, rank),
        (part_shape, part_shape),
        (rows, weights),
        scalars=place,
        flops=2 * rows.shape[0] * tok_rows * features * layers * rank * 3,
    )
    came = lax.ppermute(send, "c", swap_core)
    parts = (keep.astype(WIDE) + came.astype(WIDE)).astype(LOW)
    parts = parts.reshape(count_x * count_y, piece, layers * 3 * rank)
    parts = lax.all_to_all(parts, ("x", "y"), 0, 0, tiled=True)
    span = layers * rank
    acts, moves = local_call(
        functools.partial(recursion_kernel, layers, rank, float(model_width)),
        (
            jax.ShapeDtypeStruct((piece, span + rank), LOW),
            jax.ShapeDtypeStruct((piece, span), LOW),
        ),
        (parts, square, cross_near, cross_far),
        scalars=place,
        scratch=[
            pltpu.VMEM((piece, layers * 3 * rank), WIDE),
            pltpu.VMEM((layers * rank, layers * rank), LOW),
        ],
    )
    acts_near = gather_line(acts, "x")
    moves_near = gather_line(moves, "y")
    acts_near = gather_line(acts_near, "y")
    moves_near = gather_line(moves_near, "x")
    acts_far = lax.ppermute(acts_near, "c", swap_core)
    moves_far = lax.ppermute(moves_near, "c", swap_core)

    group_tokens = count_y * tok_rows
    outputs, grads = local_call(
        functools.partial(expand_kernel, layers, rank),
        (
            jax.ShapeDtypeStruct((layers, count_y, tok_rows, features), LOW),
            jax.ShapeDtypeStruct((layers, rank, 2 * features), LOW),
        ),
        (rows, weights, acts_near, acts_far, moves_near, moves_far),
        scalars=place,
        scratch=[
            pltpu.VMEM((group_tokens, features), WIDE),
            pltpu.VMEM((group_tokens, layers * rank), LOW),
            pltpu.VMEM((group_tokens, layers * rank), LOW),
            pltpu.VMEM((group_tokens, rank), WIDE),
        ],
        flops=8 * group_tokens * features * layers * rank,
    )
    grads = lax.psum_scatter(grads, "z", scatter_dimension=0, tiled=True)[0]
    outputs = outputs.reshape(sources, tok_rows, features)
    outputs = lax.all_to_all(outputs, PLANE, 0, 0, tiled=True)
    outputs = outputs.reshape(layers, count_y, tok_rows, features)
    section_rows = pl.pallas_call(
        order_kernel,
        grid=(count_y,),
        out_shape=jax.ShapeDtypeStruct((tok_rows, model_width), LOW),
        in_specs=[pl.BlockSpec((layers, 1, tok_rows, features), lambda i: (0, i, 0, 0))],
        out_specs=pl.BlockSpec((tok_rows, layers * features), lambda i: (0, i)),
        compiler_params=pltpu.CompilerParams(vmem_limit_bytes=VMEM_BYTES),
    )(outputs)

    own_grads = lax.ppermute(grads, across, back_route)
    shard_in, shard_out, squares = local_call(
        settle_kernel,
        (
            jax.ShapeDtypeStruct((features, rank), WIDE),
            jax.ShapeDtypeStruct((rank, features), WIDE),
            jax.ShapeDtypeStruct((sources * count_z, 128), WIDE),
        ),
        (gain_own, own_grads),
    )
    squares = lax.all_to_all(squares, EVERYONE, 0, 0, tiled=True)
    total_sq = jnp.sum(squares[:, 0])
    norm_limit = clip_rms * math.sqrt(2.0 * model_width * rank * layers)
    clip_factor = norm_limit / jnp.maximum(jnp.sqrt(total_sq), norm_limit)
    new_in, new_first_in, new_second_in = adam_update(
        master_in[0], first_in[0], second_in[0], clip_factor * shard_in
    )
    new_out, new_first_out, new_second_out = adam_update(
        master_out[0], first_out[0], second_out[0], clip_factor * shard_out
    )
    return (
        section_rows[None],
        new_in[None],
        new_out[None],
        new_first_in[None],
        new_first_out[None],
        new_second_in[None],
        new_second_out[None],
    )


def solution(mesh):
    layers, groups = mesh.shape["section"], mesh.shape["dp"]
    sizes = (layers // 2, 2, groups // layers, layers)
    fine = Mesh(mesh.devices.reshape(sizes), EVERYONE)
    split = ("y", "z")
    by_rows = P(SECTION, split, None)
    by_cols = P(SECTION, None, split)
    in_specs = (
        P(split, None),
        P(split, None),
        P(SECTION, None),
        by_rows,
        by_cols,
        by_rows,
        by_cols,
        by_rows,
        by_cols,
    )
    out_specs = (by_rows, by_rows, by_cols, by_rows, by_cols, by_rows, by_cols)
    return jax.shard_map(shards, mesh=fine, in_specs=in_specs, out_specs=out_specs, check_vma=False)
```

```python
import functools
import math

import jax
import jax.numpy as jnp
from jax import lax
from jax.experimental import pallas as pl
from jax.experimental.pallas import tpu as pltpu
from jax.sharding import Mesh, PartitionSpec as P

STEP = 10

norm_eps = 1e-05
gelu_coef = 0.7978845608028654
beta_one = 0.9
beta_two = 0.95
adam_eps = 1e-08
learn_rate = 0.05
decay_rate = 0.1
clip_rms = 0.5

LOW = jnp.bfloat16
WIDE = jnp.float32
SECTION = ("x", "c")
PLANE = ("x", "c", "y")
EVERYONE = ("x", "c", "y", "z")
SHIFTS = (0, 1, -1, 2)
TURNS = (0, 4, 3, 7, 2, 6, 1, 5)
EXTRA = 16
VMEM_BYTES = 48 * 1024 * 1024


def dot_nn(left, right):
    return lax.dot_general(left, right, (((1,), (0,)), ((), ())), preferred_element_type=WIDE)


def dot_nt(left, right):
    return lax.dot_general(left, right, (((1,), (1,)), ((), ())), preferred_element_type=WIDE)


def dot_tn(left, right):
    return lax.dot_general(left, right, (((0,), (0,)), ((), ())), preferred_element_type=WIDE)


def gelu_pair(hidden_pre):
    inner_arg = gelu_coef * (hidden_pre + 0.044715 * hidden_pre * hidden_pre * hidden_pre)
    tangent = jnp.tanh(inner_arg)
    gelu_value = 0.5 * hidden_pre * (1.0 + tangent)
    gelu_slope = 0.5 * (1.0 + tangent) + 0.5 * hidden_pre * (
        1.0 - tangent * tangent
    ) * gelu_coef * (1.0 + 3.0 * 0.044715 * hidden_pre * hidden_pre)
    return (gelu_value, gelu_slope)


def adam_update(master, first, second, grad):
    first_new = beta_one * first + (1.0 - beta_one) * grad
    second_new = beta_two * second + (1.0 - beta_two) * grad * grad
    first_hat = first_new / (1.0 - beta_one**STEP)
    second_hat = second_new / (1.0 - beta_two**STEP)
    master_new = master - learn_rate * (
        first_hat / (jnp.sqrt(second_hat) + adam_eps) + decay_rate * master
    )
    return (master_new, first_new, second_new)


def local_call(kernel, out_shape, operands, scalars=None, scratch=(), flops=0):
    specs = jax.tree.map(lambda _: pl.BlockSpec(memory_space=pltpu.VMEM), out_shape)
    moved = sum(a.size * a.dtype.itemsize for a in operands)
    moved += sum(a.size * a.dtype.itemsize for a in jax.tree.leaves(out_shape))
    in_specs = [pl.BlockSpec(memory_space=pltpu.VMEM)] * len(operands)
    if scalars is not None:
        operands = (scalars,) + tuple(operands)
        in_specs = [pl.BlockSpec(memory_space=pltpu.SMEM)] + in_specs
    return pl.pallas_call(
        kernel,
        out_shape=out_shape,
        in_specs=in_specs,
        out_specs=specs,
        scratch_shapes=list(scratch),
        compiler_params=pltpu.CompilerParams(vmem_limit_bytes=VMEM_BYTES),
        cost_estimate=pl.CostEstimate(flops=flops, bytes_accessed=moved, transcendentals=0),
    )(*operands)


def shifted(block, axis, distance):
    size = lax.axis_size(axis)
    return lax.ppermute(block, axis, [(i, (i + distance) % size) for i in range(size)])


def gather_line(block, axis):
    return jnp.stack([block] + [shifted(block, axis, d) for d in SHIFTS[1:]])


def pack_kernel(gain_ref, in_ref, out_ref, pack_ref):
    features, rank = in_ref.shape[1:]
    gain = jnp.broadcast_to(gain_ref[...], (rank, features)).T
    work_in = in_ref[0].astype(LOW).astype(WIDE)
    pack_ref[:features, :rank] = (work_in * gain).astype(LOW)
    pack_ref[:features, rank:] = out_ref[0].T.astype(LOW)
    spare = (EXTRA, 2 * rank)
    row = lax.broadcasted_iota(jnp.int32, spare, 0)
    rows = jnp.zeros(spare, WIDE)
    left = gain_ref[...]
    chunks = features // rank
    for term in range(3):
        part = left.astype(LOW).astype(WIDE)
        left = left - part
        for k in range(chunks):
            chunk = part[:, k * rank : (k + 1) * rank]
            chunk = jnp.broadcast_to(jnp.concatenate([chunk, chunk], axis=1), spare)
            rows = jnp.where(row == term * chunks + k, chunk, rows)
    pack_ref[features:, :] = rows.astype(LOW)


def packed_gain(tail, chunks):
    rows = tail.astype(WIDE)
    parts = []
    for k in range(chunks):
        terms = [rows[t * chunks + k : t * chunks + k + 1] for t in range(3)]
        parts.append(terms[0] + terms[1] + terms[2])
    return jnp.concatenate(parts, axis=1)


def cross_kernel(rank, place_ref, own_ref, near_ref, far_ref, out_ref):
    core, section, column = place_ref[0], place_ref[1], place_ref[2]
    count = len(SHIFTS)
    cut = out_ref.shape[1]
    cuts = rank // cut
    features = own_ref.shape[0] - EXTRA
    own = own_ref[:features, rank:].T
    for slot, step in enumerate(SHIFTS):
        owner = lax.rem(column - step + count, count)
        blocks = []
        for line_ref, from_core in ((near_ref, core), (far_ref, 1 - core)):
            both = dot_nn(own, line_ref[slot, :features])
            later = 2 * owner + from_core > section
            blocks.append(jnp.where(later, both[:, :rank], both[:, rank:]).astype(LOW))
        even = jnp.where(core == 0, blocks[0], blocks[1])
        odd = jnp.where(core == 0, blocks[1], blocks[0])
        for k in range(cuts):
            sel = slice(k * cut, (k + 1) * cut)
            out_ref[owner * cuts + k, :, :rank] = even[sel]
            out_ref[owner * cuts + k, :, rank:] = odd[sel]


def project_kernel(rank, place_ref, rows_ref, weight_ref, keep_ref, send_ref):
    groups, both_rows, features = rows_ref.shape
    layers = weight_ref.shape[0]
    half = both_rows // 2
    columns = keep_ref.shape[0]
    piece = half // (2 * columns)
    core, section = place_ref[0], place_ref[1]
    for layer in range(layers):
        weight = weight_ref[lax.rem(section + TURNS[layer], layers), :features]
        base = layer * 3 * rank
        for group in range(groups):
            first = dot_nn(rows_ref[group, :half, :], weight).astype(LOW)
            second = dot_nn(rows_ref[group, half:, :], weight[:, rank:]).astype(LOW)
            for column in range(columns):
                low = 2 * column * piece
                even, odd = slice(low, low + piece), slice(low + piece, low + 2 * piece)
                for value, at, width in ((first, base, 2 * rank), (second, base + 2 * rank, rank)):
                    lanes = slice(at, at + width)
                    keep_ref[column, group, :, lanes] = jnp.where(core == 0, value[even], value[odd])
                    send_ref[column, group, :, lanes] = jnp.where(core == 0, value[odd], value[even])


def recursion_kernel(
    layers, rank, width, place_ref, parts_ref, square_ref, near_ref, far_ref, act_ref, moved_ref, sums_ref, cross_ref
):
    core, column = place_ref[0], place_ref[2]
    count = len(SHIFTS)
    pieces, cut = near_ref.shape[1:3]
    cuts = rank // cut
    for slot, distance in enumerate(SHIFTS):
        owner = lax.rem(column - distance + count, count)
        for piece_ref, from_core in ((near_ref, core), (far_ref, 1 - core)):
            start = (2 * owner + from_core) * rank
            for k in range(pieces):
                at = pl.multiple_of(start + (k % cuts) * cut, cut)
                low = (k // cuts) * 2 * rank
                cross_ref[pl.ds(at, cut), low : low + 2 * rank] = piece_ref[slot, k]

    total = parts_ref[0].astype(WIDE)
    for source in range(1, parts_ref.shape[0]):
        total = total + parts_ref[source].astype(WIDE)
    sums_ref[...] = total
    rank3 = 3 * rank
    down = [sums_ref[:, k * rank3 : k * rank3 + rank] for k in range(layers)]
    up = [sums_ref[:, k * rank3 + rank : k * rank3 + 2 * rank] for k in range(layers)]
    back = [sums_ref[:, k * rank3 + 2 * rank : (k + 1) * rank3] for k in range(layers)]
    square = square_ref[:, 0:1]

    acts, pres, invs = [], [], []
    for s in range(layers):
        inv = lax.rsqrt(jnp.maximum(square, 0.0) / width + norm_eps)
        pre = inv * down[s]
        act, _ = gelu_pair(pre)
        act = act.astype(LOW)
        acts.append(act)
        pres.append(pre)
        invs.append(inv)
        act_ref[:, s * rank : (s + 1) * rank] = act
        low = s * rank
        forward = dot_nn(act, cross_ref[low : low + rank, low:])
        before = up[s]
        up[s] = before + forward[:, :rank]
        square = square + jnp.sum(act.astype(WIDE) * (before + up[s]), axis=-1, keepdims=True)
        if s + 1 < layers:
            mirrored = dot_nt(act, cross_ref[low + rank :, low : low + rank])
            for k in range(s + 1, layers):
                at = (k - s) * rank
                down[k] = down[k] + forward[:, at : at + rank]
                up[k] = up[k] + mirrored[:, at - rank : at]

    trailing = jnp.zeros_like(square)
    lane = lax.broadcasted_iota(jnp.int32, (square.shape[0], rank), 1)
    tail = jnp.zeros((square.shape[0], rank), WIDE)
    for s in reversed(range(layers)):
        _, slope = gelu_pair(pres[s])
        d_pre = (back[s] - trailing * up[s]) * slope
        coef = invs[s] * invs[s] * (1.0 / width) * jnp.sum(d_pre * pres[s], axis=-1, keepdims=True)
        moved = (invs[s] * d_pre).astype(LOW)
        moved_ref[:, s * rank : (s + 1) * rank] = moved
        coef_high = coef.astype(LOW).astype(WIDE)
        tail = tail + jnp.where(lane == s, coef_high, 0.0)
        tail = tail + jnp.where(lane == s + layers, coef - coef_high, 0.0)
        if s > 0:
            low = s * rank
            gain_term = dot_nt(moved, cross_ref[:low, low : low + rank])
            scaled_act = (trailing * acts[s].astype(WIDE)).astype(LOW)
            norm_term = dot_nn(scaled_act, cross_ref[low : low + rank, :low])
            for k in range(s):
                sel = slice(k * rank, (k + 1) * rank)
                back[k] = back[k] + gain_term[:, sel] - norm_term[:, sel]
        trailing = trailing + coef
    act_ref[:, layers * rank :] = tail.astype(LOW)


def expand_kernel(
    layers,
    rank,
    place_ref,
    rows_ref,
    weight_ref,
    act_near_ref,
    act_far_ref,
    move_near_ref,
    move_far_ref,
    out_ref,
    grad_ref,
    wide_ref,
    act_ref,
    moved_ref,
    coef_ref,
):
    groups, both_rows, features = rows_ref.shape
    half = both_rows // 2
    piece = act_near_ref.shape[2]
    span = layers * rank
    core, section, column, line = (place_ref[i] for i in range(4))
    count = len(SHIFTS)
    for group in range(groups):
        base = group * half
        wide_ref[base : base + half, :] = rows_ref[group, :half, :].astype(WIDE)
    for slot_y, step_y in enumerate(SHIFTS):
        group = lax.rem(line - step_y + count, count)
        for slot_x, step_x in enumerate(SHIFTS):
            owner = lax.rem(column - step_x + count, count)
            for some_act, some_move, from_core in (
                (act_near_ref, move_near_ref, core),
                (act_far_ref, move_far_ref, 1 - core),
            ):
                at = pl.multiple_of(group * half + (2 * owner + from_core) * piece, piece)
                dest = pl.ds(at, piece)
                act_ref[dest, :] = some_act[slot_y, slot_x, :, :span]
                coef_ref[dest, :] = some_act[slot_y, slot_x, :, span:].astype(WIDE)
                moved_ref[dest, :] = some_move[slot_x, slot_y]

    for layer in range(layers):
        up_weight = weight_ref[lax.rem(section + TURNS[layer], layers), :features, rank:]
        act = act_ref[:, layer * rank : (layer + 1) * rank]
        total = wide_ref[...] + dot_nt(act, up_weight)
        wide_ref[...] = total
        lowered = total.astype(LOW)
        for group in range(groups):
            out_ref[layer, group] = lowered[group * half : (group + 1) * half]

    for group in range(groups):
        base = group * half
        wide_ref[base : base + half, :] = rows_ref[group, half:, :].astype(WIDE)
    for layer in reversed(range(layers)):
        slot = lax.rem(section + TURNS[layer], layers)
        delta = wide_ref[...].astype(LOW)
        act = act_ref[:, layer * rank : (layer + 1) * rank]
        moved = moved_ref[:, layer * rank : (layer + 1) * rank]
        if layer > 0:
            current = out_ref[layer - 1].reshape(groups * half, features)
        else:
            current = rows_ref[:, :half, :].reshape(groups * half, features)
        grad_ref[slot, :, features:] = dot_tn(act, delta).astype(LOW)
        gain = packed_gain(weight_ref[slot, features:, :rank], features // rank)
        grad_ref[slot, :, :features] = (dot_tn(moved, current) * gain).astype(LOW)
        if layer > 0:
            coef = coef_ref[:, layer : layer + 1] + coef_ref[:, layers + layer : layers + layer + 1]
            wide_ref[...] += dot_nt(moved, weight_ref[slot, :features, :rank]) - coef * current.astype(WIDE)


def square_kernel(grad_ref, out_ref):
    grad = grad_ref[...].astype(WIDE)
    out_ref[...] = jnp.full(out_ref.shape, jnp.sum(grad * grad), WIDE)


def settle_kernel(grad_ref, in_ref, out_ref):
    features = out_ref.shape[1]
    in_ref[...] = grad_ref[:, :features].astype(WIDE).T
    out_ref[...] = grad_ref[:, features:].astype(WIDE)


def order_kernel(block_ref, out_ref):
    layers, features = block_ref.shape[0], block_ref.shape[3]
    for layer in range(layers):
        out_ref[:, layer * features : (layer + 1) * features] = block_ref[layer, 0]


def shards(
    stack_input,
    out_cotangent,
    norm_gain,
    master_in,
    master_out,
    first_in,
    first_out,
    second_in,
    second_out,
):
    count_x, count_c, count_y, count_z = (lax.axis_size(a) for a in EVERYONE)
    pos_x, pos_c, pos_y, pos_z = (lax.axis_index(a) for a in EVERYONE)
    layers = count_x * count_c
    pos_s = pos_x * count_c + pos_c
    place = jnp.stack([pos_c, pos_s, pos_x, pos_y]).astype(jnp.int32)
    sources = layers * count_y
    tok_rows, model_width = stack_input.shape
    features, rank = master_in.shape[1:]
    piece = tok_rows // layers
    swap_core = [(0, 1), (1, 0)]
    route = [
        (a * count_z + b, b * count_z + (b + TURNS[a]) % count_z)
        for a in range(layers)
        for b in range(count_z)
    ]
    back_route = [(j, i) for i, j in route]
    across = SECTION + ("z",)

    gain_own = lax.dynamic_slice_in_dim(norm_gain, (pos_y * count_z + pos_z) * features, features, 1)
    packed = local_call(
        pack_kernel, jax.ShapeDtypeStruct((features + EXTRA, 2 * rank), LOW), (gain_own, master_in, master_out)
    )
    swapped = lax.ppermute(packed, across, route)
    lined_near = gather_line(packed, "x")
    lined_far = lax.ppermute(lined_near, "c", swap_core)

    def blocks_of(rows):
        return jnp.stack(
            [
                lax.dynamic_slice_in_dim(rows, (g * count_z + pos_s) * features, features, 1)
                for g in range(count_y)
            ]
        )

    rows = jnp.concatenate([blocks_of(stack_input), blocks_of(out_cotangent)], axis=1)
    swapped, lined_near, lined_far = lax.optimization_barrier((swapped, lined_near, lined_far))
    weights = lax.all_gather(swapped, "z", axis=0)
    own_rows = lax.dynamic_slice_in_dim(stack_input, pos_s * piece, piece, 0).astype(WIDE)
    square = jnp.sum(own_rows * own_rows, axis=-1, keepdims=True)
    square = jnp.broadcast_to(square, (piece, 128))

    cut_r, cut_c = rank // count_z, count_c * rank
    cross = local_call(
        functools.partial(cross_kernel, rank),
        jax.ShapeDtypeStruct((count_y * count_z, cut_r, cut_c), LOW),
        (packed, lined_near, lined_far),
        scalars=place,
    )
    cross = lax.all_to_all(cross, ("y", "z"), 0, 0, tiled=True)
    cross = jnp.sum(cross.astype(WIDE), axis=0, keepdims=True).astype(LOW)
    cross = jnp.broadcast_to(cross, (count_y * count_z, cut_r, cut_c))
    cross = lax.all_to_all(cross, ("y", "z"), 0, 0, tiled=True)
    cross, rows = lax.optimization_barrier((cross, rows))
    rows = lax.all_to_all(rows, "y", 0, 0, tiled=True)
    cross_near = gather_line(cross, "x")
    cross_near, rows = lax.optimization_barrier((cross_near, rows))
    cross_far = lax.ppermute(cross_near, "c", swap_core)

    part_shape = jax.ShapeDtypeStruct((count_x, count_y, piece, layers * 3 * rank), LOW)
    keep, send = local_call(
        functools.partial(project_kernel, rank),
        (part_shape, part_shape),
        (rows, weights),
        scalars=place,
        flops=2 * rows.shape[0] * tok_rows * features * layers * rank * 3,
    )
    came = lax.ppermute(send, "c", swap_core)
    parts = (keep.astype(WIDE) + came.astype(WIDE)).astype(LOW)
    parts = parts.reshape(count_x * count_y, piece, layers * 3 * rank)
    parts = lax.all_to_all(parts, ("x", "y"), 0, 0, tiled=True)
    span = layers * rank
    acts, moves = local_call(
        functools.partial(recursion_kernel, layers, rank, float(model_width)),
        (
            jax.ShapeDtypeStruct((piece, span + rank), LOW),
            jax.ShapeDtypeStruct((piece, span), LOW),
        ),
        (parts, square, cross_near, cross_far),
        scalars=place,
        scratch=[
            pltpu.VMEM((piece, layers * 3 * rank), WIDE),
            pltpu.VMEM((layers * rank, layers * rank), LOW),
        ],
    )
    acts_near = gather_line(acts, "x")
    moves_near = gather_line(moves, "y")
    acts_near = gather_line(acts_near, "y")
    moves_near = gather_line(moves_near, "x")
    acts_far = lax.ppermute(acts_near, "c", swap_core)
    moves_far = lax.ppermute(moves_near, "c", swap_core)

    group_tokens = count_y * tok_rows
    outputs, grads = local_call(
        functools.partial(expand_kernel, layers, rank),
        (
            jax.ShapeDtypeStruct((layers, count_y, tok_rows, features), LOW),
            jax.ShapeDtypeStruct((layers, rank, 2 * features), LOW),
        ),
        (rows, weights, acts_near, acts_far, moves_near, moves_far),
        scalars=place,
        scratch=[
            pltpu.VMEM((group_tokens, features), WIDE),
            pltpu.VMEM((group_tokens, layers * rank), LOW),
            pltpu.VMEM((group_tokens, layers * rank), LOW),
            pltpu.VMEM((group_tokens, rank), WIDE),
        ],
        flops=8 * group_tokens * features * layers * rank,
    )
    grads = lax.psum_scatter(grads, "z", scatter_dimension=0, tiled=True)[0]
    outputs = outputs.reshape(sources, tok_rows, features)
    outputs = lax.all_to_all(outputs, PLANE, 0, 0, tiled=True)
    outputs = outputs.reshape(layers, count_y, tok_rows, features)
    section_rows = pl.pallas_call(
        order_kernel,
        grid=(count_y,),
        out_shape=jax.ShapeDtypeStruct((tok_rows, model_width), LOW),
        in_specs=[pl.BlockSpec((layers, 1, tok_rows, features), lambda i: (0, i, 0, 0))],
        out_specs=pl.BlockSpec((tok_rows, layers * features), lambda i: (0, i)),
        compiler_params=pltpu.CompilerParams(vmem_limit_bytes=VMEM_BYTES),
    )(outputs)

    own_grads = lax.ppermute(grads, across, back_route)
    squares = local_call(square_kernel, jax.ShapeDtypeStruct((8, 128), WIDE), (grads,))
    squares = squares + lax.ppermute(squares, "c", swap_core)
    for axis in ("x", "y"):
        line = [shifted(squares, axis, d) for d in SHIFTS[1:]]
        squares = (squares + line[0]) + (line[1] + line[2])
    squares, own_grads = lax.optimization_barrier((squares, own_grads))
    shard_in, shard_out = local_call(
        settle_kernel,
        (
            jax.ShapeDtypeStruct((features, rank), WIDE),
            jax.ShapeDtypeStruct((rank, features), WIDE),
        ),
        (own_grads,),
    )
    for distance in (4, 2, 1):
        squares = squares + shifted(squares, "z", distance)
    total_sq = squares[0, 0]
    norm_limit = clip_rms * math.sqrt(2.0 * model_width * rank * layers)
    clip_factor = norm_limit / jnp.maximum(jnp.sqrt(total_sq), norm_limit)
    new_in, new_first_in, new_second_in = adam_update(
        master_in[0], first_in[0], second_in[0], clip_factor * shard_in
    )
    new_out, new_first_out, new_second_out = adam_update(
        master_out[0], first_out[0], second_out[0], clip_factor * shard_out
    )
    return (
        section_rows[None],
        new_in[None],
        new_out[None],
        new_first_in[None],
        new_first_out[None],
        new_second_in[None],
        new_second_out[None],
    )


def solution(mesh):
    layers, groups = mesh.shape["section"], mesh.shape["dp"]
    sizes = (layers // 2, 2, groups // layers, layers)
    fine = Mesh(mesh.devices.reshape(sizes), EVERYONE)
    split = ("y", "z")
    by_rows = P(SECTION, split, None)
    by_cols = P(SECTION, None, split)
    in_specs = (
        P(split, None),
        P(split, None),
        P(SECTION, None),
        by_rows,
        by_cols,
        by_rows,
        by_cols,
        by_rows,
        by_cols,
    )
    out_specs = (by_rows, by_rows, by_cols, by_rows, by_cols, by_rows, by_cols)
    return jax.shard_map(shards, mesh=fine, in_specs=in_specs, out_specs=out_specs, check_vma=False)
```

```python
import functools
import math

import jax
import jax.numpy as jnp
from jax import lax
from jax.experimental import pallas as pl
from jax.experimental.pallas import tpu as pltpu
from jax.sharding import Mesh, PartitionSpec as P

STEP = 10

norm_eps = 1e-05
gelu_coef = 0.7978845608028654
beta_one = 0.9
beta_two = 0.95
adam_eps = 1e-08
learn_rate = 0.05
decay_rate = 0.1
clip_rms = 0.5

LOW = jnp.bfloat16
WIDE = jnp.float32
SECTION = ("x", "c")
PLANE = ("x", "c", "y")
EVERYONE = ("x", "c", "y", "z")
SHIFTS = (0, 1, -1, 2)
TURNS = (0, 4, 3, 7, 2, 6, 1, 5)
EXTRA = 16
VMEM_BYTES = 48 * 1024 * 1024


def dot_nn(left, right):
    return lax.dot_general(left, right, (((1,), (0,)), ((), ())), preferred_element_type=WIDE)


def dot_nt(left, right):
    return lax.dot_general(left, right, (((1,), (1,)), ((), ())), preferred_element_type=WIDE)


def dot_tn(left, right):
    return lax.dot_general(left, right, (((0,), (0,)), ((), ())), preferred_element_type=WIDE)


def gelu_pair(hidden_pre):
    inner_arg = gelu_coef * (hidden_pre + 0.044715 * hidden_pre * hidden_pre * hidden_pre)
    tangent = jnp.tanh(inner_arg)
    gelu_value = 0.5 * hidden_pre * (1.0 + tangent)
    gelu_slope = 0.5 * (1.0 + tangent) + 0.5 * hidden_pre * (
        1.0 - tangent * tangent
    ) * gelu_coef * (1.0 + 3.0 * 0.044715 * hidden_pre * hidden_pre)
    return (gelu_value, gelu_slope)


def adam_update(master, first, second, grad):
    first_new = beta_one * first + (1.0 - beta_one) * grad
    second_new = beta_two * second + (1.0 - beta_two) * grad * grad
    first_hat = first_new / (1.0 - beta_one**STEP)
    second_hat = second_new / (1.0 - beta_two**STEP)
    master_new = master - learn_rate * (
        first_hat / (jnp.sqrt(second_hat) + adam_eps) + decay_rate * master
    )
    return (master_new, first_new, second_new)


def local_call(kernel, out_shape, operands, scalars=None, scratch=(), flops=0):
    specs = jax.tree.map(lambda _: pl.BlockSpec(memory_space=pltpu.VMEM), out_shape)
    moved = sum(a.size * a.dtype.itemsize for a in operands)
    moved += sum(a.size * a.dtype.itemsize for a in jax.tree.leaves(out_shape))
    in_specs = [pl.BlockSpec(memory_space=pltpu.VMEM)] * len(operands)
    if scalars is not None:
        operands = (scalars,) + tuple(operands)
        in_specs = [pl.BlockSpec(memory_space=pltpu.SMEM)] + in_specs
    return pl.pallas_call(
        kernel,
        out_shape=out_shape,
        in_specs=in_specs,
        out_specs=specs,
        scratch_shapes=list(scratch),
        compiler_params=pltpu.CompilerParams(vmem_limit_bytes=VMEM_BYTES),
        cost_estimate=pl.CostEstimate(flops=flops, bytes_accessed=moved, transcendentals=0),
    )(*operands)


def shifted(block, axis, distance):
    size = lax.axis_size(axis)
    return lax.ppermute(block, axis, [(i, (i + distance) % size) for i in range(size)])


def gather_line(block, axis):
    return jnp.stack([block] + [shifted(block, axis, d) for d in SHIFTS[1:]])


def pack_kernel(gain_ref, in_ref, out_ref, pack_ref):
    features, rank = in_ref.shape[1:]
    gain = jnp.broadcast_to(gain_ref[...], (rank, features)).T
    work_in = in_ref[0].astype(LOW).astype(WIDE)
    pack_ref[:features, :rank] = (work_in * gain).astype(LOW)
    pack_ref[:features, rank:] = out_ref[0].T.astype(LOW)
    spare = (EXTRA, 2 * rank)
    row = lax.broadcasted_iota(jnp.int32, spare, 0)
    rows = jnp.zeros(spare, WIDE)
    left = gain_ref[...]
    chunks = features // rank
    for term in range(3):
        part = left.astype(LOW).astype(WIDE)
        left = left - part
        for k in range(chunks):
            chunk = part[:, k * rank : (k + 1) * rank]
            chunk = jnp.broadcast_to(jnp.concatenate([chunk, chunk], axis=1), spare)
            rows = jnp.where(row == term * chunks + k, chunk, rows)
    pack_ref[features:, :] = rows.astype(LOW)


def packed_gain(tail, chunks):
    rows = tail.astype(WIDE)
    parts = []
    for k in range(chunks):
        terms = [rows[t * chunks + k : t * chunks + k + 1] for t in range(3)]
        parts.append(terms[0] + terms[1] + terms[2])
    return jnp.concatenate(parts, axis=1)


def cross_kernel(rank, place_ref, own_ref, near_ref, far_ref, out_ref):
    core, section, column = place_ref[0], place_ref[1], place_ref[2]
    count = len(SHIFTS)
    cut = out_ref.shape[1]
    cuts = rank // cut
    features = own_ref.shape[0] - EXTRA
    own = own_ref[:features, rank:].T
    for slot, step in enumerate(SHIFTS):
        owner = lax.rem(column - step + count, count)
        blocks = []
        for line_ref, from_core in ((near_ref, core), (far_ref, 1 - core)):
            both = dot_nn(own, line_ref[slot, :features])
            later = 2 * owner + from_core > section
            blocks.append(jnp.where(later, both[:, :rank], both[:, rank:]).astype(LOW))
        even = jnp.where(core == 0, blocks[0], blocks[1])
        odd = jnp.where(core == 0, blocks[1], blocks[0])
        for k in range(cuts):
            sel = slice(k * cut, (k + 1) * cut)
            out_ref[owner * cuts + k, :, :rank] = even[sel]
            out_ref[owner * cuts + k, :, rank:] = odd[sel]


def project_kernel(rank, place_ref, rows_ref, weight_ref, keep_ref, send_ref):
    groups, both_rows, features = rows_ref.shape
    layers = weight_ref.shape[0]
    half = both_rows // 2
    columns = keep_ref.shape[0]
    piece = half // (2 * columns)
    core, section = place_ref[0], place_ref[1]
    for layer in range(layers):
        weight = weight_ref[lax.rem(section + TURNS[layer], layers), :features]
        base = layer * 3 * rank
        for group in range(groups):
            first = dot_nn(rows_ref[group, :half, :], weight).astype(LOW)
            second = dot_nn(rows_ref[group, half:, :], weight[:, rank:]).astype(LOW)
            for column in range(columns):
                low = 2 * column * piece
                even, odd = slice(low, low + piece), slice(low + piece, low + 2 * piece)
                for value, at, width in ((first, base, 2 * rank), (second, base + 2 * rank, rank)):
                    lanes = slice(at, at + width)
                    keep_ref[column, group, :, lanes] = jnp.where(core == 0, value[even], value[odd])
                    send_ref[column, group, :, lanes] = jnp.where(core == 0, value[odd], value[even])


def recursion_kernel(
    layers, rank, width, place_ref, parts_ref, square_ref, near_ref, far_ref, act_ref, moved_ref, sums_ref, cross_ref
):
    core, column = place_ref[0], place_ref[2]
    count = len(SHIFTS)
    pieces, cut = near_ref.shape[1:3]
    cuts = rank // cut
    for slot, distance in enumerate(SHIFTS):
        owner = lax.rem(column - distance + count, count)
        for piece_ref, from_core in ((near_ref, core), (far_ref, 1 - core)):
            start = (2 * owner + from_core) * rank
            for k in range(pieces):
                at = pl.multiple_of(start + (k % cuts) * cut, cut)
                low = (k // cuts) * 2 * rank
                cross_ref[pl.ds(at, cut), low : low + 2 * rank] = piece_ref[slot, k]

    total = parts_ref[0].astype(WIDE)
    for source in range(1, parts_ref.shape[0]):
        total = total + parts_ref[source].astype(WIDE)
    sums_ref[...] = total
    rank3 = 3 * rank
    down = [sums_ref[:, k * rank3 : k * rank3 + rank] for k in range(layers)]
    up = [sums_ref[:, k * rank3 + rank : k * rank3 + 2 * rank] for k in range(layers)]
    back = [sums_ref[:, k * rank3 + 2 * rank : (k + 1) * rank3] for k in range(layers)]
    square = square_ref[:, 0:1]

    acts, pres, invs = [], [], []
    for s in range(layers):
        inv = lax.rsqrt(jnp.maximum(square, 0.0) / width + norm_eps)
        pre = inv * down[s]
        act, _ = gelu_pair(pre)
        act = act.astype(LOW)
        acts.append(act)
        pres.append(pre)
        invs.append(inv)
        act_ref[:, s * rank : (s + 1) * rank] = act
        low = s * rank
        forward = dot_nn(act, cross_ref[low : low + rank, low:])
        before = up[s]
        up[s] = before + forward[:, :rank]
        square = square + jnp.sum(act.astype(WIDE) * (before + up[s]), axis=-1, keepdims=True)
        if s + 1 < layers:
            mirrored = dot_nt(act, cross_ref[low + rank :, low : low + rank])
            for k in range(s + 1, layers):
                at = (k - s) * rank
                down[k] = down[k] + forward[:, at : at + rank]
                up[k] = up[k] + mirrored[:, at - rank : at]

    trailing = jnp.zeros_like(square)
    lane = lax.broadcasted_iota(jnp.int32, (square.shape[0], rank), 1)
    tail = jnp.zeros((square.shape[0], rank), WIDE)
    for s in reversed(range(layers)):
        _, slope = gelu_pair(pres[s])
        d_pre = (back[s] - trailing * up[s]) * slope
        coef = invs[s] * invs[s] * (1.0 / width) * jnp.sum(d_pre * pres[s], axis=-1, keepdims=True)
        moved = (invs[s] * d_pre).astype(LOW)
        moved_ref[:, s * rank : (s + 1) * rank] = moved
        coef_high = coef.astype(LOW).astype(WIDE)
        tail = tail + jnp.where(lane == s, coef_high, 0.0)
        tail = tail + jnp.where(lane == s + layers, coef - coef_high, 0.0)
        if s > 0:
            low = s * rank
            gain_term = dot_nt(moved, cross_ref[:low, low : low + rank])
            scaled_act = (trailing * acts[s].astype(WIDE)).astype(LOW)
            norm_term = dot_nn(scaled_act, cross_ref[low : low + rank, :low])
            for k in range(s):
                sel = slice(k * rank, (k + 1) * rank)
                back[k] = back[k] + gain_term[:, sel] - norm_term[:, sel]
        trailing = trailing + coef
    act_ref[:, layers * rank :] = tail.astype(LOW)


def expand_kernel(
    layers,
    rank,
    place_ref,
    rows_ref,
    weight_ref,
    act_near_ref,
    act_far_ref,
    move_near_ref,
    move_far_ref,
    out_ref,
    grad_ref,
    wide_ref,
    act_ref,
    moved_ref,
    coef_ref,
):
    groups, both_rows, features = rows_ref.shape
    half = both_rows // 2
    piece = act_near_ref.shape[2]
    span = layers * rank
    core, section, column, line = (place_ref[i] for i in range(4))
    count = len(SHIFTS)
    for group in range(groups):
        base = group * half
        wide_ref[base : base + half, :] = rows_ref[group, :half, :].astype(WIDE)
    for slot_y, step_y in enumerate(SHIFTS):
        group = lax.rem(line - step_y + count, count)
        for slot_x, step_x in enumerate(SHIFTS):
            owner = lax.rem(column - step_x + count, count)
            for some_act, some_move, from_core in (
                (act_near_ref, move_near_ref, core),
                (act_far_ref, move_far_ref, 1 - core),
            ):
                at = pl.multiple_of(group * half + (2 * owner + from_core) * piece, piece)
                dest = pl.ds(at, piece)
                act_ref[dest, :] = some_act[slot_y, slot_x, :, :span]
                coef_ref[dest, :] = some_act[slot_y, slot_x, :, span:].astype(WIDE)
                moved_ref[dest, :] = some_move[slot_x, slot_y]

    for layer in range(layers):
        up_weight = weight_ref[lax.rem(section + TURNS[layer], layers), :features, rank:]
        act = act_ref[:, layer * rank : (layer + 1) * rank]
        total = wide_ref[...] + dot_nt(act, up_weight)
        wide_ref[...] = total
        lowered = total.astype(LOW)
        for group in range(groups):
            out_ref[layer, group] = lowered[group * half : (group + 1) * half]

    for group in range(groups):
        base = group * half
        wide_ref[base : base + half, :] = rows_ref[group, half:, :].astype(WIDE)
    for layer in reversed(range(layers)):
        slot = lax.rem(section + TURNS[layer], layers)
        delta = wide_ref[...].astype(LOW)
        act = act_ref[:, layer * rank : (layer + 1) * rank]
        moved = moved_ref[:, layer * rank : (layer + 1) * rank]
        if layer > 0:
            current = out_ref[layer - 1].reshape(groups * half, features)
        else:
            current = rows_ref[:, :half, :].reshape(groups * half, features)
        grad_ref[slot, :, features:] = dot_tn(act, delta).astype(LOW)
        gain = packed_gain(weight_ref[slot, features:, :rank], features // rank)
        grad_ref[slot, :, :features] = (dot_tn(moved, current) * gain).astype(LOW)
        if layer > 0:
            coef = coef_ref[:, layer : layer + 1] + coef_ref[:, layers + layer : layers + layer + 1]
            wide_ref[...] += dot_nt(moved, weight_ref[slot, :features, :rank]) - coef * current.astype(WIDE)


def square_kernel(grad_ref, out_ref):
    grad = grad_ref[...].astype(WIDE)
    out_ref[...] = jnp.full(out_ref.shape, jnp.sum(grad * grad), WIDE)


def settle_kernel(grad_ref, in_ref, out_ref):
    features = out_ref.shape[1]
    in_ref[...] = grad_ref[:, :features].astype(WIDE).T
    out_ref[...] = grad_ref[:, features:].astype(WIDE)


def order_kernel(block_ref, out_ref):
    layers, features = block_ref.shape[0], block_ref.shape[3]
    for layer in range(layers):
        out_ref[:, layer * features : (layer + 1) * features] = block_ref[layer, 0]


def shards(
    stack_input,
    out_cotangent,
    norm_gain,
    master_in,
    master_out,
    first_in,
    first_out,
    second_in,
    second_out,
):
    count_x, count_c, count_y, count_z = (lax.axis_size(a) for a in EVERYONE)
    pos_x, pos_c, pos_y, pos_z = (lax.axis_index(a) for a in EVERYONE)
    layers = count_x * count_c
    pos_s = pos_x * count_c + pos_c
    place = jnp.stack([pos_c, pos_s, pos_x, pos_y]).astype(jnp.int32)
    sources = layers * count_y
    tok_rows, model_width = stack_input.shape
    features, rank = master_in.shape[1:]
    piece = tok_rows // layers
    swap_core = [(0, 1), (1, 0)]
    grid = [(a, b) for a in range(layers) for b in range(count_z)]
    turned = {(a, b): (b + TURNS[a]) % count_z for a, b in grid}
    turn = [(a * count_z + b, a * count_z + turned[a, b]) for a, b in grid]
    move = [(a * count_z + turned[a, b], b * count_z + turned[a, b]) for a, b in grid]
    turn_back, move_back = ([(j, i) for i, j in route] for route in (turn, move))
    across = SECTION + ("z",)

    gain_own = lax.dynamic_slice_in_dim(norm_gain, (pos_y * count_z + pos_z) * features, features, 1)
    packed = local_call(
        pack_kernel, jax.ShapeDtypeStruct((features + EXTRA, 2 * rank), LOW), (gain_own, master_in, master_out)
    )
    swapped = lax.ppermute(packed, across, turn)
    lined_near = gather_line(packed, "x")
    swapped, lined_near = lax.optimization_barrier((swapped, lined_near))
    swapped = lax.ppermute(swapped, across, move)
    lined_far = lax.ppermute(lined_near, "c", swap_core)

    def blocks_of(rows):
        return jnp.stack(
            [
                lax.dynamic_slice_in_dim(rows, (g * count_z + pos_s) * features, features, 1)
                for g in range(count_y)
            ]
        )

    rows = jnp.concatenate([blocks_of(stack_input), blocks_of(out_cotangent)], axis=1)
    weights = lax.all_gather(swapped, "z", axis=0)
    own_rows = lax.dynamic_slice_in_dim(stack_input, pos_s * piece, piece, 0).astype(WIDE)
    square = jnp.sum(own_rows * own_rows, axis=-1, keepdims=True)
    square = jnp.broadcast_to(square, (piece, 128))

    cut_r, cut_c = rank // count_z, count_c * rank
    cross = local_call(
        functools.partial(cross_kernel, rank),
        jax.ShapeDtypeStruct((count_y * count_z, cut_r, cut_c), LOW),
        (packed, lined_near, lined_far),
        scalars=place,
    )
    cross = lax.all_to_all(cross, ("y", "z"), 0, 0, tiled=True)
    cross = jnp.sum(cross.astype(WIDE), axis=0, keepdims=True).astype(LOW)
    cross = jnp.broadcast_to(cross, (count_y * count_z, cut_r, cut_c))
    cross = lax.all_to_all(cross, ("y", "z"), 0, 0, tiled=True)
    cross, rows = lax.optimization_barrier((cross, rows))
    rows = lax.all_to_all(rows, "y", 0, 0, tiled=True)
    cross_near = gather_line(cross, "x")
    cross_near, rows = lax.optimization_barrier((cross_near, rows))
    cross_far = lax.ppermute(cross_near, "c", swap_core)

    part_shape = jax.ShapeDtypeStruct((count_x, count_y, piece, layers * 3 * rank), LOW)
    keep, send = local_call(
        functools.partial(project_kernel, rank),
        (part_shape, part_shape),
        (rows, weights),
        scalars=place,
        flops=2 * rows.shape[0] * tok_rows * features * layers * rank * 3,
    )
    came = lax.ppermute(send, "c", swap_core)
    parts = (keep.astype(WIDE) + came.astype(WIDE)).astype(LOW)
    parts = parts.reshape(count_x * count_y, piece, layers * 3 * rank)
    parts = lax.all_to_all(parts, ("x", "y"), 0, 0, tiled=True)
    span = layers * rank
    acts, moves = local_call(
        functools.partial(recursion_kernel, layers, rank, float(model_width)),
        (
            jax.ShapeDtypeStruct((piece, span + rank), LOW),
            jax.ShapeDtypeStruct((piece, span), LOW),
        ),
        (parts, square, cross_near, cross_far),
        scalars=place,
        scratch=[
            pltpu.VMEM((piece, layers * 3 * rank), WIDE),
            pltpu.VMEM((layers * rank, layers * rank), LOW),
        ],
    )
    acts_near = gather_line(acts, "x")
    moves_near = gather_line(moves, "y")
    acts_near = gather_line(acts_near, "y")
    moves_near = gather_line(moves_near, "x")
    acts_far = lax.ppermute(acts_near, "c", swap_core)
    moves_far = lax.ppermute(moves_near, "c", swap_core)

    group_tokens = count_y * tok_rows
    outputs, grads = local_call(
        functools.partial(expand_kernel, layers, rank),
        (
            jax.ShapeDtypeStruct((layers, count_y, tok_rows, features), LOW),
            jax.ShapeDtypeStruct((layers, rank, 2 * features), LOW),
        ),
        (rows, weights, acts_near, acts_far, moves_near, moves_far),
        scalars=place,
        scratch=[
            pltpu.VMEM((group_tokens, features), WIDE),
            pltpu.VMEM((group_tokens, layers * rank), LOW),
            pltpu.VMEM((group_tokens, layers * rank), LOW),
            pltpu.VMEM((group_tokens, rank), WIDE),
        ],
        flops=8 * group_tokens * features * layers * rank,
    )
    grads = lax.psum_scatter(grads, "z", scatter_dimension=0, tiled=True)[0]
    outputs = outputs.reshape(sources, tok_rows, features)
    outputs = lax.all_to_all(outputs, PLANE, 0, 0, tiled=True)
    outputs = outputs.reshape(layers, count_y, tok_rows, features)
    section_rows = pl.pallas_call(
        order_kernel,
        grid=(count_y,),
        out_shape=jax.ShapeDtypeStruct((tok_rows, model_width), LOW),
        in_specs=[pl.BlockSpec((layers, 1, tok_rows, features), lambda i: (0, i, 0, 0))],
        out_specs=pl.BlockSpec((tok_rows, layers * features), lambda i: (0, i)),
        compiler_params=pltpu.CompilerParams(vmem_limit_bytes=VMEM_BYTES),
    )(outputs)

    grads = lax.ppermute(grads, across, move_back)
    squares = local_call(
        square_kernel, jax.ShapeDtypeStruct((sources * count_z, 128), WIDE), (grads,)
    )
    squares = lax.all_to_all(squares, EVERYONE, 0, 0, tiled=True)
    total_sq = jnp.sum(squares[:, 0])
    own_grads = lax.ppermute(grads, across, turn_back)
    shard_in, shard_out = local_call(
        settle_kernel,
        (
            jax.ShapeDtypeStruct((features, rank), WIDE),
            jax.ShapeDtypeStruct((rank, features), WIDE),
        ),
        (own_grads,),
    )
    norm_limit = clip_rms * math.sqrt(2.0 * model_width * rank * layers)
    clip_factor = norm_limit / jnp.maximum(jnp.sqrt(total_sq), norm_limit)
    new_in, new_first_in, new_second_in = adam_update(
        master_in[0], first_in[0], second_in[0], clip_factor * shard_in
    )
    new_out, new_first_out, new_second_out = adam_update(
        master_out[0], first_out[0], second_out[0], clip_factor * shard_out
    )
    return (
        section_rows[None],
        new_in[None],
        new_out[None],
        new_first_in[None],
        new_first_out[None],
        new_second_in[None],
        new_second_out[None],
    )


def solution(mesh):
    layers, groups = mesh.shape["section"], mesh.shape["dp"]
    sizes = (layers // 2, 2, groups // layers, layers)
    fine = Mesh(mesh.devices.reshape(sizes), EVERYONE)
    split = ("y", "z")
    by_rows = P(SECTION, split, None)
    by_cols = P(SECTION, None, split)
    in_specs = (
        P(split, None),
        P(split, None),
        P(SECTION, None),
        by_rows,
        by_cols,
        by_rows,
        by_cols,
        by_rows,
        by_cols,
    )
    out_specs = (by_rows, by_rows, by_cols, by_rows, by_cols, by_rows, by_cols)
    return jax.shard_map(shards, mesh=fine, in_specs=in_specs, out_specs=out_specs, check_vma=False)
```

```python
import functools
import math

import jax
import jax.numpy as jnp
from jax import lax
from jax.experimental import pallas as pl
from jax.experimental.pallas import tpu as pltpu
from jax.sharding import Mesh, PartitionSpec as P

STEP = 10

norm_eps = 1e-05
gelu_coef = 0.7978845608028654
beta_one = 0.9
beta_two = 0.95
adam_eps = 1e-08
learn_rate = 0.05
decay_rate = 0.1
clip_rms = 0.5

LOW = jnp.bfloat16
WIDE = jnp.float32
SECTION = ("x", "c")
PLANE = ("x", "c", "y")
EVERYONE = ("x", "c", "y", "z")
SHIFTS = (0, 1, -1, 2)
TURNS = (0, 4, 3, 7, 2, 6, 1, 5)
FIRST = (0, 2, 2, -1, 1, -1, 1, -2)
EXTRA = 16
VMEM_BYTES = 48 * 1024 * 1024


def dot_nn(left, right):
    return lax.dot_general(left, right, (((1,), (0,)), ((), ())), preferred_element_type=WIDE)


def dot_nt(left, right):
    return lax.dot_general(left, right, (((1,), (1,)), ((), ())), preferred_element_type=WIDE)


def dot_tn(left, right):
    return lax.dot_general(left, right, (((0,), (0,)), ((), ())), preferred_element_type=WIDE)


def gelu_pair(hidden_pre):
    inner_arg = gelu_coef * (hidden_pre + 0.044715 * hidden_pre * hidden_pre * hidden_pre)
    tangent = jnp.tanh(inner_arg)
    gelu_value = 0.5 * hidden_pre * (1.0 + tangent)
    gelu_slope = 0.5 * (1.0 + tangent) + 0.5 * hidden_pre * (
        1.0 - tangent * tangent
    ) * gelu_coef * (1.0 + 3.0 * 0.044715 * hidden_pre * hidden_pre)
    return (gelu_value, gelu_slope)


def adam_update(master, first, second, grad):
    first_new = beta_one * first + (1.0 - beta_one) * grad
    second_new = beta_two * second + (1.0 - beta_two) * grad * grad
    first_hat = first_new / (1.0 - beta_one**STEP)
    second_hat = second_new / (1.0 - beta_two**STEP)
    master_new = master - learn_rate * (
        first_hat / (jnp.sqrt(second_hat) + adam_eps) + decay_rate * master
    )
    return (master_new, first_new, second_new)


def local_call(kernel, out_shape, operands, scalars=None, scratch=(), flops=0):
    specs = jax.tree.map(lambda _: pl.BlockSpec(memory_space=pltpu.VMEM), out_shape)
    moved = sum(a.size * a.dtype.itemsize for a in operands)
    moved += sum(a.size * a.dtype.itemsize for a in jax.tree.leaves(out_shape))
    in_specs = [pl.BlockSpec(memory_space=pltpu.VMEM)] * len(operands)
    if scalars is not None:
        operands = (scalars,) + tuple(operands)
        in_specs = [pl.BlockSpec(memory_space=pltpu.SMEM)] + in_specs
    return pl.pallas_call(
        kernel,
        out_shape=out_shape,
        in_specs=in_specs,
        out_specs=specs,
        scratch_shapes=list(scratch),
        compiler_params=pltpu.CompilerParams(vmem_limit_bytes=VMEM_BYTES),
        cost_estimate=pl.CostEstimate(flops=flops, bytes_accessed=moved, transcendentals=0),
    )(*operands)


def shifted(block, axis, distance):
    size = lax.axis_size(axis)
    return lax.ppermute(block, axis, [(i, (i + distance) % size) for i in range(size)])


def gather_line(block, axis):
    return jnp.stack([block] + [shifted(block, axis, d) for d in SHIFTS[1:]])


def gather_line_both_ways(block, axis):
    before, after = shifted(block, axis, 1), shifted(block, axis, -1)
    half = block.shape[0] // 2
    far = [shifted(before[:half], axis, 1), shifted(after[half:], axis, -1)]
    return jnp.stack([block, before, after, jnp.concatenate(far)])


def pack_kernel(gain_ref, in_ref, out_ref, pack_ref):
    features, rank = in_ref.shape[1:]
    gain = jnp.broadcast_to(gain_ref[...], (rank, features)).T
    work_in = in_ref[0].astype(LOW).astype(WIDE)
    pack_ref[:features, :rank] = (work_in * gain).astype(LOW)
    pack_ref[:features, rank:] = out_ref[0].T.astype(LOW)
    spare = (EXTRA, 2 * rank)
    row = lax.broadcasted_iota(jnp.int32, spare, 0)
    rows = jnp.zeros(spare, WIDE)
    left = gain_ref[...]
    chunks = features // rank
    for term in range(3):
        part = left.astype(LOW).astype(WIDE)
        left = left - part
        for k in range(chunks):
            chunk = part[:, k * rank : (k + 1) * rank]
            chunk = jnp.broadcast_to(jnp.concatenate([chunk, chunk], axis=1), spare)
            rows = jnp.where(row == term * chunks + k, chunk, rows)
    pack_ref[features:, :] = rows.astype(LOW)


def packed_gain(tail, chunks):
    rows = tail.astype(WIDE)
    parts = []
    for k in range(chunks):
        terms = [rows[t * chunks + k : t * chunks + k + 1] for t in range(3)]
        parts.append(terms[0] + terms[1] + terms[2])
    return jnp.concatenate(parts, axis=1)


def cross_kernel(rank, place_ref, own_ref, near_ref, far_ref, out_ref):
    core, section, column = place_ref[0], place_ref[1], place_ref[2]
    count = len(SHIFTS)
    cut = out_ref.shape[1]
    cuts = rank // cut
    features = own_ref.shape[0] - EXTRA
    own = own_ref[:features, rank:].T
    for slot, step in enumerate(SHIFTS):
        owner = lax.rem(column - step + count, count)
        blocks = []
        for line_ref, from_core in ((near_ref, core), (far_ref, 1 - core)):
            both = dot_nn(own, line_ref[slot, :features])
            later = 2 * owner + from_core > section
            blocks.append(jnp.where(later, both[:, :rank], both[:, rank:]).astype(LOW))
        even = jnp.where(core == 0, blocks[0], blocks[1])
        odd = jnp.where(core == 0, blocks[1], blocks[0])
        for k in range(cuts):
            sel = slice(k * cut, (k + 1) * cut)
            out_ref[owner * cuts + k, :, :rank] = even[sel]
            out_ref[owner * cuts + k, :, rank:] = odd[sel]


def project_kernel(rank, place_ref, rows_ref, weight_ref, keep_ref, send_ref):
    groups, both_rows, features = rows_ref.shape
    layers = weight_ref.shape[0]
    half = both_rows // 2
    columns = keep_ref.shape[0]
    piece = half // (2 * columns)
    core, section = place_ref[0], place_ref[1]
    for layer in range(layers):
        weight = weight_ref[lax.rem(section + TURNS[layer], layers), :features]
        base = layer * 3 * rank
        for group in range(groups):
            first = dot_nn(rows_ref[group, :half, :], weight).astype(LOW)
            second = dot_nn(rows_ref[group, half:, :], weight[:, rank:]).astype(LOW)
            for column in range(columns):
                low = 2 * column * piece
                even, odd = slice(low, low + piece), slice(low + piece, low + 2 * piece)
                for value, at, width in ((first, base, 2 * rank), (second, base + 2 * rank, rank)):
                    lanes = slice(at, at + width)
                    keep_ref[column, group, :, lanes] = jnp.where(core == 0, value[even], value[odd])
                    send_ref[column, group, :, lanes] = jnp.where(core == 0, value[odd], value[even])


def recursion_kernel(
    layers, rank, width, place_ref, parts_ref, square_ref, near_ref, far_ref, act_ref, moved_ref, sums_ref, cross_ref
):
    core, column = place_ref[0], place_ref[2]
    count = len(SHIFTS)
    pieces, cut = near_ref.shape[1:3]
    cuts = rank // cut
    for slot, distance in enumerate(SHIFTS):
        owner = lax.rem(column - distance + count, count)
        for piece_ref, from_core in ((near_ref, core), (far_ref, 1 - core)):
            start = (2 * owner + from_core) * rank
            for k in range(pieces):
                at = pl.multiple_of(start + (k % cuts) * cut, cut)
                low = (k // cuts) * 2 * rank
                cross_ref[pl.ds(at, cut), low : low + 2 * rank] = piece_ref[slot, k]

    total = parts_ref[0].astype(WIDE)
    for source in range(1, parts_ref.shape[0]):
        total = total + parts_ref[source].astype(WIDE)
    sums_ref[...] = total
    rank3 = 3 * rank
    down = [sums_ref[:, k * rank3 : k * rank3 + rank] for k in range(layers)]
    up = [sums_ref[:, k * rank3 + rank : k * rank3 + 2 * rank] for k in range(layers)]
    back = [sums_ref[:, k * rank3 + 2 * rank : (k + 1) * rank3] for k in range(layers)]
    square = square_ref[:, 0:1]

    acts, pres, invs = [], [], []
    for s in range(layers):
        inv = lax.rsqrt(jnp.maximum(square, 0.0) / width + norm_eps)
        pre = inv * down[s]
        act, _ = gelu_pair(pre)
        act = act.astype(LOW)
        acts.append(act)
        pres.append(pre)
        invs.append(inv)
        act_ref[:, s * rank : (s + 1) * rank] = act
        low = s * rank
        forward = dot_nn(act, cross_ref[low : low + rank, low:])
        before = up[s]
        up[s] = before + forward[:, :rank]
        square = square + jnp.sum(act.astype(WIDE) * (before + up[s]), axis=-1, keepdims=True)
        if s + 1 < layers:
            mirrored = dot_nt(act, cross_ref[low + rank :, low : low + rank])
            for k in range(s + 1, layers):
                at = (k - s) * rank
                down[k] = down[k] + forward[:, at : at + rank]
                up[k] = up[k] + mirrored[:, at - rank : at]

    trailing = jnp.zeros_like(square)
    lane = lax.broadcasted_iota(jnp.int32, (square.shape[0], rank), 1)
    tail = jnp.zeros((square.shape[0], rank), WIDE)
    for s in reversed(range(layers)):
        _, slope = gelu_pair(pres[s])
        d_pre = (back[s] - trailing * up[s]) * slope
        coef = invs[s] * invs[s] * (1.0 / width) * jnp.sum(d_pre * pres[s], axis=-1, keepdims=True)
        moved = (invs[s] * d_pre).astype(LOW)
        moved_ref[:, s * rank : (s + 1) * rank] = moved
        coef_high = coef.astype(LOW).astype(WIDE)
        tail = tail + jnp.where(lane == s, coef_high, 0.0)
        tail = tail + jnp.where(lane == s + layers, coef - coef_high, 0.0)
        if s > 0:
            low = s * rank
            gain_term = dot_nt(moved, cross_ref[:low, low : low + rank])
            scaled_act = (trailing * acts[s].astype(WIDE)).astype(LOW)
            norm_term = dot_nn(scaled_act, cross_ref[low : low + rank, :low])
            for k in range(s):
                sel = slice(k * rank, (k + 1) * rank)
                back[k] = back[k] + gain_term[:, sel] - norm_term[:, sel]
        trailing = trailing + coef
    act_ref[:, layers * rank :] = tail.astype(LOW)


def expand_kernel(
    layers,
    rank,
    place_ref,
    rows_ref,
    weight_ref,
    act_near_ref,
    act_far_ref,
    move_near_ref,
    move_far_ref,
    out_ref,
    grad_ref,
    wide_ref,
    act_ref,
    moved_ref,
    coef_ref,
):
    groups, both_rows, features = rows_ref.shape
    half = both_rows // 2
    piece = act_near_ref.shape[2]
    span = layers * rank
    core, section, column, line = (place_ref[i] for i in range(4))
    count = len(SHIFTS)
    for group in range(groups):
        base = group * half
        wide_ref[base : base + half, :] = rows_ref[group, :half, :].astype(WIDE)
    for slot_y, step_y in enumerate(SHIFTS):
        group = lax.rem(line - step_y + count, count)
        for slot_x, step_x in enumerate(SHIFTS):
            owner = lax.rem(column - step_x + count, count)
            for some_act, some_move, from_core in (
                (act_near_ref, move_near_ref, core),
                (act_far_ref, move_far_ref, 1 - core),
            ):
                at = pl.multiple_of(group * half + (2 * owner + from_core) * piece, piece)
                dest = pl.ds(at, piece)
                act_ref[dest, :] = some_act[slot_y, slot_x, :, :span]
                coef_ref[dest, :] = some_act[slot_y, slot_x, :, span:].astype(WIDE)
                moved_ref[dest, :] = some_move[slot_x, slot_y]

    for layer in range(layers):
        up_weight = weight_ref[lax.rem(section + TURNS[layer], layers), :features, rank:]
        act = act_ref[:, layer * rank : (layer + 1) * rank]
        total = wide_ref[...] + dot_nt(act, up_weight)
        wide_ref[...] = total
        lowered = total.astype(LOW)
        for group in range(groups):
            out_ref[layer, group] = lowered[group * half : (group + 1) * half]

    for group in range(groups):
        base = group * half
        wide_ref[base : base + half, :] = rows_ref[group, half:, :].astype(WIDE)
    for layer in reversed(range(layers)):
        slot = lax.rem(section + TURNS[layer], layers)
        delta = wide_ref[...].astype(LOW)
        act = act_ref[:, layer * rank : (layer + 1) * rank]
        moved = moved_ref[:, layer * rank : (layer + 1) * rank]
        if layer > 0:
            current = out_ref[layer - 1].reshape(groups * half, features)
        else:
            current = rows_ref[:, :half, :].reshape(groups * half, features)
        grad_ref[slot, :, features:] = dot_tn(act, delta).astype(LOW)
        gain = packed_gain(weight_ref[slot, features:, :rank], features // rank)
        grad_ref[slot, :, :features] = (dot_tn(moved, current) * gain).astype(LOW)
        if layer > 0:
            coef = coef_ref[:, layer : layer + 1] + coef_ref[:, layers + layer : layers + layer + 1]
            wide_ref[...] += dot_nt(moved, weight_ref[slot, :features, :rank]) - coef * current.astype(WIDE)


def square_kernel(grad_ref, out_ref):
    grad = grad_ref[...].astype(WIDE)
    out_ref[...] = jnp.full(out_ref.shape, jnp.sum(grad * grad), WIDE)


def settle_kernel(grad_ref, in_ref, out_ref):
    features = out_ref.shape[1]
    in_ref[...] = grad_ref[:, :features].astype(WIDE).T
    out_ref[...] = grad_ref[:, features:].astype(WIDE)


def order_kernel(block_ref, out_ref):
    layers, features = block_ref.shape[0], block_ref.shape[3]
    for layer in range(layers):
        out_ref[:, layer * features : (layer + 1) * features] = block_ref[layer, 0]


def shards(
    stack_input,
    out_cotangent,
    norm_gain,
    master_in,
    master_out,
    first_in,
    first_out,
    second_in,
    second_out,
):
    count_x, count_c, count_y, count_z = (lax.axis_size(a) for a in EVERYONE)
    pos_x, pos_c, pos_y, pos_z = (lax.axis_index(a) for a in EVERYONE)
    layers = count_x * count_c
    pos_s = pos_x * count_c + pos_c
    place = jnp.stack([pos_c, pos_s, pos_x, pos_y]).astype(jnp.int32)
    sources = layers * count_y
    tok_rows, model_width = stack_input.shape
    features, rank = master_in.shape[1:]
    piece = tok_rows // layers
    swap_core = [(0, 1), (1, 0)]
    grid = [(a, b) for a in range(layers) for b in range(count_z)]
    turned = {(a, b): (b + TURNS[a]) % count_z for a, b in grid}
    turn = [(a * count_z + b, a * count_z + turned[a, b]) for a, b in grid]
    move = [(a * count_z + turned[a, b], b * count_z + turned[a, b]) for a, b in grid]
    move_back = [(j, i) for i, j in move]
    first_back = [(a * count_z + b, a * count_z + (b - FIRST[a]) % count_z) for a, b in grid]
    last_back = [(a * count_z + b, a * count_z + (b - TURNS[a] + FIRST[a]) % count_z) for a, b in grid]
    across = SECTION + ("z",)

    gain_own = lax.dynamic_slice_in_dim(norm_gain, (pos_y * count_z + pos_z) * features, features, 1)
    def blocks_of(rows):
        return jnp.stack(
            [
                lax.dynamic_slice_in_dim(rows, (g * count_z + pos_s) * features, features, 1)
                for g in range(count_y)
            ]
        )

    rows = jnp.concatenate([blocks_of(stack_input), blocks_of(out_cotangent)], axis=1)
    gain_own, rows = lax.optimization_barrier((gain_own, rows))
    rows = lax.all_to_all(rows, "y", 0, 0, tiled=True)
    packed = local_call(
        pack_kernel, jax.ShapeDtypeStruct((features + EXTRA, 2 * rank), LOW), (gain_own, master_in, master_out)
    )
    swapped = lax.ppermute(packed, across, turn)
    lined_near = gather_line(packed, "x")
    swapped, lined_near, rows = lax.optimization_barrier((swapped, lined_near, rows))
    swapped = lax.ppermute(swapped, across, move)
    lined_far = lax.ppermute(lined_near, "c", swap_core)
    swapped, lined_far = lax.optimization_barrier((swapped, lined_far))
    weights = lax.all_gather(swapped, "z", axis=0)

    own_rows = lax.dynamic_slice_in_dim(stack_input, pos_s * piece, piece, 0).astype(WIDE)
    square = jnp.sum(own_rows * own_rows, axis=-1, keepdims=True)
    square = jnp.broadcast_to(square, (piece, 128))

    cut_r, cut_c = rank // count_z, count_c * rank
    cross = local_call(
        functools.partial(cross_kernel, rank),
        jax.ShapeDtypeStruct((count_y * count_z, cut_r, cut_c), LOW),
        (packed, lined_near, lined_far),
        scalars=place,
    )
    cross = lax.all_to_all(cross, ("y", "z"), 0, 0, tiled=True)
    cross = jnp.sum(cross.astype(WIDE), axis=0, keepdims=True).astype(LOW)
    cross = jnp.broadcast_to(cross, (count_y * count_z, cut_r, cut_c))
    cross = lax.all_to_all(cross, ("y", "z"), 0, 0, tiled=True)
    cross_near = gather_line_both_ways(cross, "x")
    cross_near, rows = lax.optimization_barrier((cross_near, rows))
    cross_far = lax.ppermute(cross_near, "c", swap_core)

    part_shape = jax.ShapeDtypeStruct((count_x, count_y, piece, layers * 3 * rank), LOW)
    keep, send = local_call(
        functools.partial(project_kernel, rank),
        (part_shape, part_shape),
        (rows, weights),
        scalars=place,
        flops=2 * rows.shape[0] * tok_rows * features * layers * rank * 3,
    )
    came = lax.ppermute(send, "c", swap_core)
    parts = (keep.astype(WIDE) + came.astype(WIDE)).astype(LOW)
    parts = parts.reshape(count_x * count_y, piece, layers * 3 * rank)
    parts = lax.all_to_all(parts, ("x", "y"), 0, 0, tiled=True)
    span = layers * rank
    acts, moves = local_call(
        functools.partial(recursion_kernel, layers, rank, float(model_width)),
        (
            jax.ShapeDtypeStruct((piece, span + rank), LOW),
            jax.ShapeDtypeStruct((piece, span), LOW),
        ),
        (parts, square, cross_near, cross_far),
        scalars=place,
        scratch=[
            pltpu.VMEM((piece, layers * 3 * rank), WIDE),
            pltpu.VMEM((layers * rank, layers * rank), LOW),
        ],
    )
    acts_near = gather_line(acts, "x")
    moves_near = gather_line(moves, "y")
    acts_near = gather_line(acts_near, "y")
    moves_near = gather_line(moves_near, "x")
    acts_far = lax.ppermute(acts_near, "c", swap_core)
    moves_far = lax.ppermute(moves_near, "c", swap_core)

    group_tokens = count_y * tok_rows
    outputs, grads = local_call(
        functools.partial(expand_kernel, layers, rank),
        (
            jax.ShapeDtypeStruct((layers, count_y, tok_rows, features), LOW),
            jax.ShapeDtypeStruct((layers, rank, 2 * features), LOW),
        ),
        (rows, weights, acts_near, acts_far, moves_near, moves_far),
        scalars=place,
        scratch=[
            pltpu.VMEM((group_tokens, features), WIDE),
            pltpu.VMEM((group_tokens, layers * rank), LOW),
            pltpu.VMEM((group_tokens, layers * rank), LOW),
            pltpu.VMEM((group_tokens, rank), WIDE),
        ],
        flops=8 * group_tokens * features * layers * rank,
    )
    grads = lax.psum_scatter(grads, "z", scatter_dimension=0, tiled=True)[0]
    outputs = outputs.reshape(sources, tok_rows, features)
    outputs = lax.all_to_all(outputs, PLANE, 0, 0, tiled=True)
    outputs = outputs.reshape(layers, count_y, tok_rows, features)
    section_rows = pl.pallas_call(
        order_kernel,
        grid=(count_y,),
        out_shape=jax.ShapeDtypeStruct((tok_rows, model_width), LOW),
        in_specs=[pl.BlockSpec((layers, 1, tok_rows, features), lambda i: (0, i, 0, 0))],
        out_specs=pl.BlockSpec((tok_rows, layers * features), lambda i: (0, i)),
        compiler_params=pltpu.CompilerParams(vmem_limit_bytes=VMEM_BYTES),
    )(outputs)

    grads = lax.ppermute(grads, across, move_back)
    squares = local_call(
        square_kernel, jax.ShapeDtypeStruct((sources * count_z, 128), WIDE), (grads,)
    )
    squares = lax.all_to_all(squares, EVERYONE, 0, 0, tiled=True)
    total_sq = jnp.sum(squares[:, 0])
    own_grads = lax.ppermute(lax.ppermute(grads, across, first_back), across, last_back)
    shard_in, shard_out = local_call(
        settle_kernel,
        (
            jax.ShapeDtypeStruct((features, rank), WIDE),
            jax.ShapeDtypeStruct((rank, features), WIDE),
        ),
        (own_grads,),
    )
    norm_limit = clip_rms * math.sqrt(2.0 * model_width * rank * layers)
    clip_factor = norm_limit / jnp.maximum(jnp.sqrt(total_sq), norm_limit)
    new_in, new_first_in, new_second_in = adam_update(
        master_in[0], first_in[0], second_in[0], clip_factor * shard_in
    )
    new_out, new_first_out, new_second_out = adam_update(
        master_out[0], first_out[0], second_out[0], clip_factor * shard_out
    )
    return (
        section_rows[None],
        new_in[None],
        new_out[None],
        new_first_in[None],
        new_first_out[None],
        new_second_in[None],
        new_second_out[None],
    )


def solution(mesh):
    layers, groups = mesh.shape["section"], mesh.shape["dp"]
    sizes = (layers // 2, 2, groups // layers, layers)
    fine = Mesh(mesh.devices.reshape(sizes), EVERYONE)
    split = ("y", "z")
    by_rows = P(SECTION, split, None)
    by_cols = P(SECTION, None, split)
    in_specs = (
        P(split, None),
        P(split, None),
        P(SECTION, None),
        by_rows,
        by_cols,
        by_rows,
        by_cols,
        by_rows,
        by_cols,
    )
    out_specs = (by_rows, by_rows, by_cols, by_rows, by_cols, by_rows, by_cols)
    return jax.shard_map(shards, mesh=fine, in_specs=in_specs, out_specs=out_specs, check_vma=False)
```

```python
import functools
import math

import jax
import jax.numpy as jnp
from jax import lax
from jax.experimental import pallas as pl
from jax.experimental.pallas import tpu as pltpu
from jax.sharding import Mesh, PartitionSpec as P

STEP = 10

norm_eps = 1e-05
gelu_coef = 0.7978845608028654
beta_one = 0.9
beta_two = 0.95
adam_eps = 1e-08
learn_rate = 0.05
decay_rate = 0.1
clip_rms = 0.5

LOW = jnp.bfloat16
WIDE = jnp.float32
SECTION = ("x", "c")
PLANE = ("x", "c", "y")
EVERYONE = ("x", "c", "y", "z")
SHIFTS = (0, 1, -1, 2)
TURNS = (0, 4, 3, 7, 2, 6, 1, 5)
FIRST = (0, 2, 2, -1, 1, -1, 1, -2)
EXTRA = 16
VMEM_BYTES = 48 * 1024 * 1024


def dot_nn(left, right):
    return lax.dot_general(left, right, (((1,), (0,)), ((), ())), preferred_element_type=WIDE)


def dot_nt(left, right):
    return lax.dot_general(left, right, (((1,), (1,)), ((), ())), preferred_element_type=WIDE)


def dot_tn(left, right):
    return lax.dot_general(left, right, (((0,), (0,)), ((), ())), preferred_element_type=WIDE)


def gelu_pair(hidden_pre):
    inner_arg = gelu_coef * (hidden_pre + 0.044715 * hidden_pre * hidden_pre * hidden_pre)
    tangent = jnp.tanh(inner_arg)
    gelu_value = 0.5 * hidden_pre * (1.0 + tangent)
    gelu_slope = 0.5 * (1.0 + tangent) + 0.5 * hidden_pre * (
        1.0 - tangent * tangent
    ) * gelu_coef * (1.0 + 3.0 * 0.044715 * hidden_pre * hidden_pre)
    return (gelu_value, gelu_slope)


def adam_update(master, first, second, grad):
    first_new = beta_one * first + (1.0 - beta_one) * grad
    second_new = beta_two * second + (1.0 - beta_two) * grad * grad
    first_hat = first_new / (1.0 - beta_one**STEP)
    second_hat = second_new / (1.0 - beta_two**STEP)
    master_new = master - learn_rate * (
        first_hat / (jnp.sqrt(second_hat) + adam_eps) + decay_rate * master
    )
    return (master_new, first_new, second_new)


def local_call(kernel, out_shape, operands, scalars=None, scratch=(), flops=0):
    specs = jax.tree.map(lambda _: pl.BlockSpec(memory_space=pltpu.VMEM), out_shape)
    moved = sum(a.size * a.dtype.itemsize for a in operands)
    moved += sum(a.size * a.dtype.itemsize for a in jax.tree.leaves(out_shape))
    in_specs = [pl.BlockSpec(memory_space=pltpu.VMEM)] * len(operands)
    if scalars is not None:
        operands = (scalars,) + tuple(operands)
        in_specs = [pl.BlockSpec(memory_space=pltpu.SMEM)] + in_specs
    return pl.pallas_call(
        kernel,
        out_shape=out_shape,
        in_specs=in_specs,
        out_specs=specs,
        scratch_shapes=list(scratch),
        compiler_params=pltpu.CompilerParams(vmem_limit_bytes=VMEM_BYTES),
        cost_estimate=pl.CostEstimate(flops=flops, bytes_accessed=moved, transcendentals=0),
    )(*operands)


def shifted(block, axis, distance):
    size = lax.axis_size(axis)
    return lax.ppermute(block, axis, [(i, (i + distance) % size) for i in range(size)])


def gather_line(block, axis):
    return jnp.stack([block] + [shifted(block, axis, d) for d in SHIFTS[1:]])


def pack_kernel(gain_ref, in_ref, out_ref, pack_ref):
    features, rank = in_ref.shape[1:]
    gain = jnp.broadcast_to(gain_ref[...], (rank, features)).T
    work_in = in_ref[0].astype(LOW).astype(WIDE)
    pack_ref[:features, :rank] = (work_in * gain).astype(LOW)
    pack_ref[:features, rank:] = out_ref[0].T.astype(LOW)
    spare = (EXTRA, 2 * rank)
    row = lax.broadcasted_iota(jnp.int32, spare, 0)
    rows = jnp.zeros(spare, WIDE)
    left = gain_ref[...]
    chunks = features // rank
    for term in range(3):
        part = left.astype(LOW).astype(WIDE)
        left = left - part
        for k in range(chunks):
            chunk = part[:, k * rank : (k + 1) * rank]
            chunk = jnp.broadcast_to(jnp.concatenate([chunk, chunk], axis=1), spare)
            rows = jnp.where(row == term * chunks + k, chunk, rows)
    pack_ref[features:, :] = rows.astype(LOW)


def packed_gain(tail, chunks):
    rows = tail.astype(WIDE)
    parts = []
    for k in range(chunks):
        terms = [rows[t * chunks + k : t * chunks + k + 1] for t in range(3)]
        parts.append(terms[0] + terms[1] + terms[2])
    return jnp.concatenate(parts, axis=1)


def cross_kernel(rank, place_ref, own_ref, near_ref, far_ref, out_ref):
    core, section, column = place_ref[0], place_ref[1], place_ref[2]
    count = len(SHIFTS)
    cut = out_ref.shape[1]
    cuts = rank // cut
    features = own_ref.shape[0] - EXTRA
    own = own_ref[:features, rank:].T
    for slot, step in enumerate(SHIFTS):
        owner = lax.rem(column - step + count, count)
        blocks = []
        for line_ref, from_core in ((near_ref, core), (far_ref, 1 - core)):
            both = dot_nn(own, line_ref[slot, :features])
            later = 2 * owner + from_core > section
            blocks.append(jnp.where(later, both[:, :rank], both[:, rank:]).astype(LOW))
        even = jnp.where(core == 0, blocks[0], blocks[1])
        odd = jnp.where(core == 0, blocks[1], blocks[0])
        for k in range(cuts):
            sel = slice(k * cut, (k + 1) * cut)
            out_ref[owner * cuts + k, :, :rank] = even[sel]
            out_ref[owner * cuts + k, :, rank:] = odd[sel]


def project_kernel(rank, place_ref, rows_ref, weight_ref, keep_ref, send_ref):
    groups, both_rows, features = rows_ref.shape
    layers = weight_ref.shape[0]
    half = both_rows // 2
    columns = keep_ref.shape[0]
    piece = half // (2 * columns)
    core, section = place_ref[0], place_ref[1]
    for layer in range(layers):
        weight = weight_ref[lax.rem(section + TURNS[layer], layers), :features]
        base = layer * 3 * rank
        for group in range(groups):
            first = dot_nn(rows_ref[group, :half, :], weight).astype(LOW)
            second = dot_nn(rows_ref[group, half:, :], weight[:, rank:]).astype(LOW)
            for column in range(columns):
                low = 2 * column * piece
                even, odd = slice(low, low + piece), slice(low + piece, low + 2 * piece)
                for value, at, width in ((first, base, 2 * rank), (second, base + 2 * rank, rank)):
                    lanes = slice(at, at + width)
                    keep_ref[column, group, :, lanes] = jnp.where(core == 0, value[even], value[odd])
                    send_ref[column, group, :, lanes] = jnp.where(core == 0, value[odd], value[even])


def recursion_kernel(
    layers, rank, width, place_ref, parts_ref, square_ref, near_ref, far_ref, act_ref, moved_ref, sums_ref, cross_ref
):
    core, column = place_ref[0], place_ref[2]
    count = len(SHIFTS)
    pieces, cut = near_ref.shape[1:3]
    cuts = rank // cut
    for slot, distance in enumerate(SHIFTS):
        owner = lax.rem(column - distance + count, count)
        for piece_ref, from_core in ((near_ref, core), (far_ref, 1 - core)):
            start = (2 * owner + from_core) * rank
            for k in range(pieces):
                at = pl.multiple_of(start + (k % cuts) * cut, cut)
                low = (k // cuts) * 2 * rank
                cross_ref[pl.ds(at, cut), low : low + 2 * rank] = piece_ref[slot, k]

    total = parts_ref[0].astype(WIDE)
    for source in range(1, parts_ref.shape[0]):
        total = total + parts_ref[source].astype(WIDE)
    sums_ref[...] = total
    rank3 = 3 * rank
    down = [sums_ref[:, k * rank3 : k * rank3 + rank] for k in range(layers)]
    up = [sums_ref[:, k * rank3 + rank : k * rank3 + 2 * rank] for k in range(layers)]
    back = [sums_ref[:, k * rank3 + 2 * rank : (k + 1) * rank3] for k in range(layers)]
    square = square_ref[:, 0:1]

    acts, pres, invs = [], [], []
    for s in range(layers):
        inv = lax.rsqrt(jnp.maximum(square, 0.0) / width + norm_eps)
        pre = inv * down[s]
        act, _ = gelu_pair(pre)
        act = act.astype(LOW)
        acts.append(act)
        pres.append(pre)
        invs.append(inv)
        act_ref[:, s * rank : (s + 1) * rank] = act
        low = s * rank
        forward = dot_nn(act, cross_ref[low : low + rank, low:])
        before = up[s]
        up[s] = before + forward[:, :rank]
        square = square + jnp.sum(act.astype(WIDE) * (before + up[s]), axis=-1, keepdims=True)
        if s + 1 < layers:
            mirrored = dot_nt(act, cross_ref[low + rank :, low : low + rank])
            for k in range(s + 1, layers):
                at = (k - s) * rank
                down[k] = down[k] + forward[:, at : at + rank]
                up[k] = up[k] + mirrored[:, at - rank : at]

    trailing = jnp.zeros_like(square)
    lane = lax.broadcasted_iota(jnp.int32, (square.shape[0], rank), 1)
    tail = jnp.zeros((square.shape[0], rank), WIDE)
    for s in reversed(range(layers)):
        _, slope = gelu_pair(pres[s])
        d_pre = (back[s] - trailing * up[s]) * slope
        coef = invs[s] * invs[s] * (1.0 / width) * jnp.sum(d_pre * pres[s], axis=-1, keepdims=True)
        moved = (invs[s] * d_pre).astype(LOW)
        moved_ref[:, s * rank : (s + 1) * rank] = moved
        coef_high = coef.astype(LOW).astype(WIDE)
        tail = tail + jnp.where(lane == s, coef_high, 0.0)
        tail = tail + jnp.where(lane == s + layers, coef - coef_high, 0.0)
        if s > 0:
            low = s * rank
            gain_term = dot_nt(moved, cross_ref[:low, low : low + rank])
            scaled_act = (trailing * acts[s].astype(WIDE)).astype(LOW)
            norm_term = dot_nn(scaled_act, cross_ref[low : low + rank, :low])
            for k in range(s):
                sel = slice(k * rank, (k + 1) * rank)
                back[k] = back[k] + gain_term[:, sel] - norm_term[:, sel]
        trailing = trailing + coef
    act_ref[:, layers * rank :] = tail.astype(LOW)


def expand_kernel(
    layers,
    rank,
    place_ref,
    rows_ref,
    weight_ref,
    act_near_ref,
    act_far_ref,
    move_near_ref,
    move_far_ref,
    out_ref,
    grad_ref,
    wide_ref,
    act_ref,
    moved_ref,
    coef_ref,
):
    groups, both_rows, features = rows_ref.shape
    half = both_rows // 2
    piece = act_near_ref.shape[2]
    span = layers * rank
    core, section, column, line = (place_ref[i] for i in range(4))
    count = len(SHIFTS)
    for group in range(groups):
        base = group * half
        wide_ref[base : base + half, :] = rows_ref[group, :half, :].astype(WIDE)
    for slot_y, step_y in enumerate(SHIFTS):
        group = lax.rem(line - step_y + count, count)
        for slot_x, step_x in enumerate(SHIFTS):
            owner = lax.rem(column - step_x + count, count)
            for some_act, some_move, from_core in (
                (act_near_ref, move_near_ref, core),
                (act_far_ref, move_far_ref, 1 - core),
            ):
                at = pl.multiple_of(group * half + (2 * owner + from_core) * piece, piece)
                dest = pl.ds(at, piece)
                act_ref[dest, :] = some_act[slot_y, slot_x, :, :span]
                coef_ref[dest, :] = some_act[slot_y, slot_x, :, span:].astype(WIDE)
                moved_ref[dest, :] = some_move[slot_x, slot_y]

    for layer in range(layers):
        up_weight = weight_ref[lax.rem(section + TURNS[layer], layers), :features, rank:]
        act = act_ref[:, layer * rank : (layer + 1) * rank]
        total = wide_ref[...] + dot_nt(act, up_weight)
        wide_ref[...] = total
        lowered = total.astype(LOW)
        for group in range(groups):
            out_ref[layer, group] = lowered[group * half : (group + 1) * half]

    for group in range(groups):
        base = group * half
        wide_ref[base : base + half, :] = rows_ref[group, half:, :].astype(WIDE)
    for layer in reversed(range(layers)):
        slot = lax.rem(section + TURNS[layer], layers)
        delta = wide_ref[...].astype(LOW)
        act = act_ref[:, layer * rank : (layer + 1) * rank]
        moved = moved_ref[:, layer * rank : (layer + 1) * rank]
        if layer > 0:
            current = out_ref[layer - 1].reshape(groups * half, features)
        else:
            current = rows_ref[:, :half, :].reshape(groups * half, features)
        grad_ref[slot, :, features:] = dot_tn(act, delta).astype(LOW)
        gain = packed_gain(weight_ref[slot, features:, :rank], features // rank)
        grad_ref[slot, :, :features] = (dot_tn(moved, current) * gain).astype(LOW)
        if layer > 0:
            coef = coef_ref[:, layer : layer + 1] + coef_ref[:, layers + layer : layers + layer + 1]
            wide_ref[...] += dot_nt(moved, weight_ref[slot, :features, :rank]) - coef * current.astype(WIDE)


def square_kernel(grad_ref, out_ref):
    grad = grad_ref[...].astype(WIDE)
    out_ref[...] = jnp.full(out_ref.shape, jnp.sum(grad * grad), WIDE)


def settle_kernel(grad_ref, in_ref, out_ref):
    features = out_ref.shape[1]
    in_ref[...] = grad_ref[:, :features].astype(WIDE).T
    out_ref[...] = grad_ref[:, features:].astype(WIDE)


def order_kernel(block_ref, out_ref):
    layers, features = block_ref.shape[0], block_ref.shape[3]
    for layer in range(layers):
        out_ref[:, layer * features : (layer + 1) * features] = block_ref[layer, 0]


def shards(
    stack_input,
    out_cotangent,
    norm_gain,
    master_in,
    master_out,
    first_in,
    first_out,
    second_in,
    second_out,
):
    count_x, count_c, count_y, count_z = (lax.axis_size(a) for a in EVERYONE)
    pos_x, pos_c, pos_y, pos_z = (lax.axis_index(a) for a in EVERYONE)
    layers = count_x * count_c
    pos_s = pos_x * count_c + pos_c
    place = jnp.stack([pos_c, pos_s, pos_x, pos_y]).astype(jnp.int32)
    sources = layers * count_y
    tok_rows, model_width = stack_input.shape
    features, rank = master_in.shape[1:]
    piece = tok_rows // layers
    swap_core = [(0, 1), (1, 0)]
    grid = [(a, b) for a in range(layers) for b in range(count_z)]
    turned = {(a, b): (b + TURNS[a]) % count_z for a, b in grid}
    swap = [(a * count_z + b, b * count_z + turned[a, b]) for a, b in grid]
    move = [(a * count_z + turned[a, b], b * count_z + turned[a, b]) for a, b in grid]
    move_back = [(j, i) for i, j in move]
    first_back = [(a * count_z + b, a * count_z + (b - FIRST[a]) % count_z) for a, b in grid]
    last_back = [(a * count_z + b, a * count_z + (b - TURNS[a] + FIRST[a]) % count_z) for a, b in grid]
    across = SECTION + ("z",)

    gain_own = lax.dynamic_slice_in_dim(norm_gain, (pos_y * count_z + pos_z) * features, features, 1)
    def blocks_of(rows):
        return jnp.stack(
            [
                lax.dynamic_slice_in_dim(rows, (g * count_z + pos_s) * features, features, 1)
                for g in range(count_y)
            ]
        )

    rows = jnp.concatenate([blocks_of(stack_input), blocks_of(out_cotangent)], axis=1)
    gain_own, rows = lax.optimization_barrier((gain_own, rows))
    rows = lax.all_to_all(rows, "y", 0, 0, tiled=True)
    packed = local_call(
        pack_kernel, jax.ShapeDtypeStruct((features + EXTRA, 2 * rank), LOW), (gain_own, master_in, master_out)
    )
    swapped = lax.ppermute(packed, across, swap)
    lined_near = gather_line(packed, "x")
    swapped, lined_near, rows = lax.optimization_barrier((swapped, lined_near, rows))
    lined_far = lax.ppermute(lined_near, "c", swap_core)
    weights = lax.all_gather(swapped, "z", axis=0)

    own_rows = lax.dynamic_slice_in_dim(stack_input, pos_s * piece, piece, 0).astype(WIDE)
    square = jnp.sum(own_rows * own_rows, axis=-1, keepdims=True)
    square = jnp.broadcast_to(square, (piece, 128))

    cut_r, cut_c = rank // count_z, count_c * rank
    cross = local_call(
        functools.partial(cross_kernel, rank),
        jax.ShapeDtypeStruct((count_y * count_z, cut_r, cut_c), LOW),
        (packed, lined_near, lined_far),
        scalars=place,
    )
    cross = lax.all_to_all(cross, ("y", "z"), 0, 0, tiled=True)
    cross = jnp.sum(cross.astype(WIDE), axis=0, keepdims=True).astype(LOW)
    cross = jnp.broadcast_to(cross, (count_y * count_z, cut_r, cut_c))
    cross = lax.all_to_all(cross, ("y", "z"), 0, 0, tiled=True)
    before, after = shifted(cross, "x", 1), shifted(cross, "x", -1)
    before, after, rows = lax.optimization_barrier((before, after, rows))
    half = cross.shape[0] // 2
    beyond = [shifted(before[:half], "x", 1), shifted(after[half:], "x", -1)]
    cross_near = jnp.stack([cross, before, after, jnp.concatenate(beyond)])

    part_shape = jax.ShapeDtypeStruct((count_x, count_y, piece, layers * 3 * rank), LOW)
    keep, send = local_call(
        functools.partial(project_kernel, rank),
        (part_shape, part_shape),
        (rows, weights),
        scalars=place,
        flops=2 * rows.shape[0] * tok_rows * features * layers * rank * 3,
    )
    came = lax.ppermute(send, "c", swap_core)
    parts = (keep.astype(WIDE) + came.astype(WIDE)).astype(LOW)
    parts = parts.reshape(count_x * count_y, piece, layers * 3 * rank)
    parts, cross_near = lax.optimization_barrier((parts, cross_near))
    cross_far = lax.ppermute(cross_near, "c", swap_core)
    parts = lax.all_to_all(parts, ("x", "y"), 0, 0, tiled=True)
    span = layers * rank
    acts, moves = local_call(
        functools.partial(recursion_kernel, layers, rank, float(model_width)),
        (
            jax.ShapeDtypeStruct((piece, span + rank), LOW),
            jax.ShapeDtypeStruct((piece, span), LOW),
        ),
        (parts, square, cross_near, cross_far),
        scalars=place,
        scratch=[
            pltpu.VMEM((piece, layers * 3 * rank), WIDE),
            pltpu.VMEM((layers * rank, layers * rank), LOW),
        ],
    )
    acts_near = gather_line(acts, "x")
    moves_near = gather_line(moves, "y")
    acts_near = gather_line(acts_near, "y")
    moves_near = gather_line(moves_near, "x")
    acts_far = lax.ppermute(acts_near, "c", swap_core)
    moves_far = lax.ppermute(moves_near, "c", swap_core)

    group_tokens = count_y * tok_rows
    outputs, grads = local_call(
        functools.partial(expand_kernel, layers, rank),
        (
            jax.ShapeDtypeStruct((layers, count_y, tok_rows, features), LOW),
            jax.ShapeDtypeStruct((layers, rank, 2 * features), LOW),
        ),
        (rows, weights, acts_near, acts_far, moves_near, moves_far),
        scalars=place,
        scratch=[
            pltpu.VMEM((group_tokens, features), WIDE),
            pltpu.VMEM((group_tokens, layers * rank), LOW),
            pltpu.VMEM((group_tokens, layers * rank), LOW),
            pltpu.VMEM((group_tokens, rank), WIDE),
        ],
        flops=8 * group_tokens * features * layers * rank,
    )
    grads = lax.psum_scatter(grads, "z", scatter_dimension=0, tiled=True)[0]
    outputs = outputs.reshape(sources, tok_rows, features)
    outputs = lax.all_to_all(outputs, PLANE, 0, 0, tiled=True)
    outputs = outputs.reshape(layers, count_y, tok_rows, features)
    section_rows = pl.pallas_call(
        order_kernel,
        grid=(count_y,),
        out_shape=jax.ShapeDtypeStruct((tok_rows, model_width), LOW),
        in_specs=[pl.BlockSpec((layers, 1, tok_rows, features), lambda i: (0, i, 0, 0))],
        out_specs=pl.BlockSpec((tok_rows, layers * features), lambda i: (0, i)),
        compiler_params=pltpu.CompilerParams(vmem_limit_bytes=VMEM_BYTES),
    )(outputs)

    grads = lax.ppermute(grads, across, move_back)
    squares = local_call(
        square_kernel, jax.ShapeDtypeStruct((sources * count_z, 128), WIDE), (grads,)
    )
    squares = lax.all_to_all(squares, EVERYONE, 0, 0, tiled=True)
    total_sq = jnp.sum(squares[:, 0])
    own_grads = lax.ppermute(lax.ppermute(grads, across, first_back), across, last_back)
    shard_in, shard_out = local_call(
        settle_kernel,
        (
            jax.ShapeDtypeStruct((features, rank), WIDE),
            jax.ShapeDtypeStruct((rank, features), WIDE),
        ),
        (own_grads,),
    )
    norm_limit = clip_rms * math.sqrt(2.0 * model_width * rank * layers)
    clip_factor = norm_limit / jnp.maximum(jnp.sqrt(total_sq), norm_limit)
    new_in, new_first_in, new_second_in = adam_update(
        master_in[0], first_in[0], second_in[0], clip_factor * shard_in
    )
    new_out, new_first_out, new_second_out = adam_update(
        master_out[0], first_out[0], second_out[0], clip_factor * shard_out
    )
    return (
        section_rows[None],
        new_in[None],
        new_out[None],
        new_first_in[None],
        new_first_out[None],
        new_second_in[None],
        new_second_out[None],
    )


def solution(mesh):
    layers, groups = mesh.shape["section"], mesh.shape["dp"]
    sizes = (layers // 2, 2, groups // layers, layers)
    fine = Mesh(mesh.devices.reshape(sizes), EVERYONE)
    split = ("y", "z")
    by_rows = P(SECTION, split, None)
    by_cols = P(SECTION, None, split)
    in_specs = (
        P(split, None),
        P(split, None),
        P(SECTION, None),
        by_rows,
        by_cols,
        by_rows,
        by_cols,
        by_rows,
        by_cols,
    )
    out_specs = (by_rows, by_rows, by_cols, by_rows, by_cols, by_rows, by_cols)
    return jax.shard_map(shards, mesh=fine, in_specs=in_specs, out_specs=out_specs, check_vma=False)
```

```python
import functools
import math

import jax
import jax.numpy as jnp
from jax import lax
from jax.experimental import pallas as pl
from jax.experimental.pallas import tpu as pltpu
from jax.sharding import Mesh, PartitionSpec as P

STEP = 10

norm_eps = 1e-05
gelu_coef = 0.7978845608028654
beta_one = 0.9
beta_two = 0.95
adam_eps = 1e-08
learn_rate = 0.05
decay_rate = 0.1
clip_rms = 0.5

LOW = jnp.bfloat16
WIDE = jnp.float32
SECTION = ("x", "c")
PLANE = ("x", "c", "y")
EVERYONE = ("x", "c", "y", "z")
SHIFTS = (0, 1, -1, 2)
TURNS = (0, 4, 3, 7, 2, 6, 1, 5)
FIRST = (0, 3, 3, -1, 2, -2, 1, -3)
EXTRA = 16
VMEM_BYTES = 48 * 1024 * 1024


def dot_nn(left, right):
    return lax.dot_general(left, right, (((1,), (0,)), ((), ())), preferred_element_type=WIDE)


def dot_nt(left, right):
    return lax.dot_general(left, right, (((1,), (1,)), ((), ())), preferred_element_type=WIDE)


def dot_tn(left, right):
    return lax.dot_general(left, right, (((0,), (0,)), ((), ())), preferred_element_type=WIDE)


def gelu_pair(hidden_pre):
    inner_arg = gelu_coef * (hidden_pre + 0.044715 * hidden_pre * hidden_pre * hidden_pre)
    tangent = jnp.tanh(inner_arg)
    gelu_value = 0.5 * hidden_pre * (1.0 + tangent)
    gelu_slope = 0.5 * (1.0 + tangent) + 0.5 * hidden_pre * (
        1.0 - tangent * tangent
    ) * gelu_coef * (1.0 + 3.0 * 0.044715 * hidden_pre * hidden_pre)
    return (gelu_value, gelu_slope)


def adam_update(master, first, second, grad):
    first_new = beta_one * first + (1.0 - beta_one) * grad
    second_new = beta_two * second + (1.0 - beta_two) * grad * grad
    first_hat = first_new / (1.0 - beta_one**STEP)
    second_hat = second_new / (1.0 - beta_two**STEP)
    master_new = master - learn_rate * (
        first_hat / (jnp.sqrt(second_hat) + adam_eps) + decay_rate * master
    )
    return (master_new, first_new, second_new)


def local_call(kernel, out_shape, operands, scalars=None, scratch=(), flops=0):
    specs = jax.tree.map(lambda _: pl.BlockSpec(memory_space=pltpu.VMEM), out_shape)
    moved = sum(a.size * a.dtype.itemsize for a in operands)
    moved += sum(a.size * a.dtype.itemsize for a in jax.tree.leaves(out_shape))
    in_specs = [pl.BlockSpec(memory_space=pltpu.VMEM)] * len(operands)
    if scalars is not None:
        operands = (scalars,) + tuple(operands)
        in_specs = [pl.BlockSpec(memory_space=pltpu.SMEM)] + in_specs
    return pl.pallas_call(
        kernel,
        out_shape=out_shape,
        in_specs=in_specs,
        out_specs=specs,
        scratch_shapes=list(scratch),
        compiler_params=pltpu.CompilerParams(vmem_limit_bytes=VMEM_BYTES),
        cost_estimate=pl.CostEstimate(flops=flops, bytes_accessed=moved, transcendentals=0),
    )(*operands)


def shifted(block, axis, distance):
    size = lax.axis_size(axis)
    return lax.ppermute(block, axis, [(i, (i + distance) % size) for i in range(size)])


def gather_line(block, axis):
    return jnp.stack([block] + [shifted(block, axis, d) for d in SHIFTS[1:]])


def pack_kernel(gain_ref, in_ref, out_ref, pack_ref):
    features, rank = in_ref.shape[1:]
    gain = jnp.broadcast_to(gain_ref[...], (rank, features)).T
    work_in = in_ref[0].astype(LOW).astype(WIDE)
    pack_ref[:features, :rank] = (work_in * gain).astype(LOW)
    pack_ref[:features, rank:] = out_ref[0].T.astype(LOW)
    spare = (EXTRA, 2 * rank)
    row = lax.broadcasted_iota(jnp.int32, spare, 0)
    rows = jnp.zeros(spare, WIDE)
    left = gain_ref[...]
    chunks = features // rank
    for term in range(3):
        part = left.astype(LOW).astype(WIDE)
        left = left - part
        for k in range(chunks):
            chunk = part[:, k * rank : (k + 1) * rank]
            chunk = jnp.broadcast_to(jnp.concatenate([chunk, chunk], axis=1), spare)
            rows = jnp.where(row == term * chunks + k, chunk, rows)
    pack_ref[features:, :] = rows.astype(LOW)


def packed_gain(tail, chunks):
    rows = tail.astype(WIDE)
    parts = []
    for k in range(chunks):
        terms = [rows[t * chunks + k : t * chunks + k + 1] for t in range(3)]
        parts.append(terms[0] + terms[1] + terms[2])
    return jnp.concatenate(parts, axis=1)


def cross_kernel(rank, place_ref, own_ref, near_ref, far_ref, out_ref):
    core, section, column = place_ref[0], place_ref[1], place_ref[2]
    count = len(SHIFTS)
    cut = out_ref.shape[1]
    cuts = rank // cut
    features = own_ref.shape[0] - EXTRA
    own = own_ref[:features, rank:].T
    for slot, step in enumerate(SHIFTS):
        owner = lax.rem(column - step + count, count)
        blocks = []
        for line_ref, from_core in ((near_ref, core), (far_ref, 1 - core)):
            both = dot_nn(own, line_ref[slot, :features])
            later = 2 * owner + from_core > section
            blocks.append(jnp.where(later, both[:, :rank], both[:, rank:]).astype(LOW))
        even = jnp.where(core == 0, blocks[0], blocks[1])
        odd = jnp.where(core == 0, blocks[1], blocks[0])
        for k in range(cuts):
            sel = slice(k * cut, (k + 1) * cut)
            out_ref[owner * cuts + k, :, :rank] = even[sel]
            out_ref[owner * cuts + k, :, rank:] = odd[sel]


def project_kernel(rank, place_ref, rows_ref, weight_ref, keep_ref, send_ref):
    groups, both_rows, features = rows_ref.shape
    layers = weight_ref.shape[0]
    half = both_rows // 2
    columns = keep_ref.shape[0]
    piece = half // (2 * columns)
    core, section = place_ref[0], place_ref[1]
    for layer in range(layers):
        weight = weight_ref[lax.rem(section + TURNS[layer], layers), :features]
        base = layer * 3 * rank
        for group in range(groups):
            first = dot_nn(rows_ref[group, :half, :], weight).astype(LOW)
            second = dot_nn(rows_ref[group, half:, :], weight[:, rank:]).astype(LOW)
            for column in range(columns):
                low = 2 * column * piece
                even, odd = slice(low, low + piece), slice(low + piece, low + 2 * piece)
                for value, at, width in ((first, base, 2 * rank), (second, base + 2 * rank, rank)):
                    lanes = slice(at, at + width)
                    keep_ref[column, group, :, lanes] = jnp.where(core == 0, value[even], value[odd])
                    send_ref[column, group, :, lanes] = jnp.where(core == 0, value[odd], value[even])


def recursion_kernel(
    layers, rank, width, place_ref, parts_ref, square_ref, near_ref, far_ref, act_ref, moved_ref, sums_ref, cross_ref
):
    core, column = place_ref[0], place_ref[2]
    count = len(SHIFTS)
    pieces, cut = near_ref.shape[1:3]
    cuts = rank // cut
    for slot, distance in enumerate(SHIFTS):
        owner = lax.rem(column - distance + count, count)
        for piece_ref, from_core in ((near_ref, core), (far_ref, 1 - core)):
            start = (2 * owner + from_core) * rank
            for k in range(pieces):
                at = pl.multiple_of(start + (k % cuts) * cut, cut)
                low = (k // cuts) * 2 * rank
                cross_ref[pl.ds(at, cut), low : low + 2 * rank] = piece_ref[slot, k]

    total = parts_ref[0].astype(WIDE)
    for source in range(1, parts_ref.shape[0]):
        total = total + parts_ref[source].astype(WIDE)
    sums_ref[...] = total
    rank3 = 3 * rank
    down = [sums_ref[:, k * rank3 : k * rank3 + rank] for k in range(layers)]
    up = [sums_ref[:, k * rank3 + rank : k * rank3 + 2 * rank] for k in range(layers)]
    back = [sums_ref[:, k * rank3 + 2 * rank : (k + 1) * rank3] for k in range(layers)]
    square = square_ref[:, 0:1]

    acts, pres, invs = [], [], []
    for s in range(layers):
        inv = lax.rsqrt(jnp.maximum(square, 0.0) / width + norm_eps)
        pre = inv * down[s]
        act, _ = gelu_pair(pre)
        act = act.astype(LOW)
        acts.append(act)
        pres.append(pre)
        invs.append(inv)
        act_ref[:, s * rank : (s + 1) * rank] = act
        low = s * rank
        forward = dot_nn(act, cross_ref[low : low + rank, low:])
        before = up[s]
        up[s] = before + forward[:, :rank]
        square = square + jnp.sum(act.astype(WIDE) * (before + up[s]), axis=-1, keepdims=True)
        if s + 1 < layers:
            mirrored = dot_nt(act, cross_ref[low + rank :, low : low + rank])
            for k in range(s + 1, layers):
                at = (k - s) * rank
                down[k] = down[k] + forward[:, at : at + rank]
                up[k] = up[k] + mirrored[:, at - rank : at]

    trailing = jnp.zeros_like(square)
    lane = lax.broadcasted_iota(jnp.int32, (square.shape[0], rank), 1)
    tail = jnp.zeros((square.shape[0], rank), WIDE)
    for s in reversed(range(layers)):
        _, slope = gelu_pair(pres[s])
        d_pre = (back[s] - trailing * up[s]) * slope
        coef = invs[s] * invs[s] * (1.0 / width) * jnp.sum(d_pre * pres[s], axis=-1, keepdims=True)
        moved = (invs[s] * d_pre).astype(LOW)
        moved_ref[:, s * rank : (s + 1) * rank] = moved
        coef_high = coef.astype(LOW).astype(WIDE)
        tail = tail + jnp.where(lane == s, coef_high, 0.0)
        tail = tail + jnp.where(lane == s + layers, coef - coef_high, 0.0)
        if s > 0:
            low = s * rank
            gain_term = dot_nt(moved, cross_ref[:low, low : low + rank])
            scaled_act = (trailing * acts[s].astype(WIDE)).astype(LOW)
            norm_term = dot_nn(scaled_act, cross_ref[low : low + rank, :low])
            for k in range(s):
                sel = slice(k * rank, (k + 1) * rank)
                back[k] = back[k] + gain_term[:, sel] - norm_term[:, sel]
        trailing = trailing + coef
    act_ref[:, layers * rank :] = tail.astype(LOW)


def expand_kernel(
    layers,
    rank,
    place_ref,
    rows_ref,
    weight_ref,
    act_near_ref,
    act_far_ref,
    move_near_ref,
    move_far_ref,
    out_ref,
    grad_ref,
    wide_ref,
    act_ref,
    moved_ref,
    coef_ref,
):
    groups, both_rows, features = rows_ref.shape
    half = both_rows // 2
    piece = act_near_ref.shape[2]
    span = layers * rank
    core, section, column, line = (place_ref[i] for i in range(4))
    count = len(SHIFTS)
    for group in range(groups):
        base = group * half
        wide_ref[base : base + half, :] = rows_ref[group, :half, :].astype(WIDE)
    for slot_y, step_y in enumerate(SHIFTS):
        group = lax.rem(line - step_y + count, count)
        for slot_x, step_x in enumerate(SHIFTS):
            owner = lax.rem(column - step_x + count, count)
            for some_act, some_move, from_core in (
                (act_near_ref, move_near_ref, core),
                (act_far_ref, move_far_ref, 1 - core),
            ):
                at = pl.multiple_of(group * half + (2 * owner + from_core) * piece, piece)
                dest = pl.ds(at, piece)
                act_ref[dest, :] = some_act[slot_y, slot_x, :, :span]
                coef_ref[dest, :] = some_act[slot_y, slot_x, :, span:].astype(WIDE)
                moved_ref[dest, :] = some_move[slot_x, slot_y]

    for layer in range(layers):
        up_weight = weight_ref[lax.rem(section + TURNS[layer], layers), :features, rank:]
        act = act_ref[:, layer * rank : (layer + 1) * rank]
        total = wide_ref[...] + dot_nt(act, up_weight)
        wide_ref[...] = total
        lowered = total.astype(LOW)
        for group in range(groups):
            out_ref[layer, group] = lowered[group * half : (group + 1) * half]

    for group in range(groups):
        base = group * half
        wide_ref[base : base + half, :] = rows_ref[group, half:, :].astype(WIDE)
    for layer in reversed(range(layers)):
        slot = lax.rem(section + TURNS[layer], layers)
        delta = wide_ref[...].astype(LOW)
        act = act_ref[:, layer * rank : (layer + 1) * rank]
        moved = moved_ref[:, layer * rank : (layer + 1) * rank]
        if layer > 0:
            current = out_ref[layer - 1].reshape(groups * half, features)
        else:
            current = rows_ref[:, :half, :].reshape(groups * half, features)
        grad_ref[slot, :, features:] = dot_tn(act, delta).astype(LOW)
        gain = packed_gain(weight_ref[slot, features:, :rank], features // rank)
        grad_ref[slot, :, :features] = (dot_tn(moved, current) * gain).astype(LOW)
        if layer > 0:
            coef = coef_ref[:, layer : layer + 1] + coef_ref[:, layers + layer : layers + layer + 1]
            wide_ref[...] += dot_nt(moved, weight_ref[slot, :features, :rank]) - coef * current.astype(WIDE)


def square_kernel(grad_ref, out_ref):
    grad = grad_ref[...].astype(WIDE)
    out_ref[...] = jnp.full(out_ref.shape, jnp.sum(grad * grad), WIDE)


def settle_kernel(grad_ref, in_ref, out_ref):
    features = out_ref.shape[1]
    in_ref[...] = grad_ref[:, :features].astype(WIDE).T
    out_ref[...] = grad_ref[:, features:].astype(WIDE)


def order_kernel(block_ref, out_ref):
    layers, features = block_ref.shape[0], block_ref.shape[3]
    for layer in range(layers):
        out_ref[:, layer * features : (layer + 1) * features] = block_ref[layer, 0]


def shards(
    stack_input,
    out_cotangent,
    norm_gain,
    master_in,
    master_out,
    first_in,
    first_out,
    second_in,
    second_out,
):
    count_x, count_c, count_y, count_z = (lax.axis_size(a) for a in EVERYONE)
    pos_x, pos_c, pos_y, pos_z = (lax.axis_index(a) for a in EVERYONE)
    layers = count_x * count_c
    pos_s = pos_x * count_c + pos_c
    place = jnp.stack([pos_c, pos_s, pos_x, pos_y]).astype(jnp.int32)
    sources = layers * count_y
    tok_rows, model_width = stack_input.shape
    features, rank = master_in.shape[1:]
    piece = tok_rows // layers
    swap_core = [(0, 1), (1, 0)]
    grid = [(a, b) for a in range(layers) for b in range(count_z)]
    turned = {(a, b): (b + TURNS[a]) % count_z for a, b in grid}
    swap = [(a * count_z + b, b * count_z + turned[a, b]) for a, b in grid]
    move = [(a * count_z + turned[a, b], b * count_z + turned[a, b]) for a, b in grid]
    move_back = [(j, i) for i, j in move]
    first_back = [(a * count_z + b, a * count_z + (b - FIRST[a]) % count_z) for a, b in grid]
    last_back = [(a * count_z + b, a * count_z + (b - TURNS[a] + FIRST[a]) % count_z) for a, b in grid]
    across = SECTION + ("z",)

    gain_own = lax.dynamic_slice_in_dim(norm_gain, (pos_y * count_z + pos_z) * features, features, 1)
    def blocks_of(rows):
        return jnp.stack(
            [
                lax.dynamic_slice_in_dim(rows, (g * count_z + pos_s) * features, features, 1)
                for g in range(count_y)
            ]
        )

    rows = jnp.concatenate([blocks_of(stack_input), blocks_of(out_cotangent)], axis=1)
    gain_own, rows = lax.optimization_barrier((gain_own, rows))
    rows = lax.all_to_all(rows, "y", 0, 0, tiled=True)
    packed = local_call(
        pack_kernel, jax.ShapeDtypeStruct((features + EXTRA, 2 * rank), LOW), (gain_own, master_in, master_out)
    )
    swapped = lax.ppermute(packed, across, swap)
    lined_near = gather_line(packed, "x")
    swapped, lined_near, rows = lax.optimization_barrier((swapped, lined_near, rows))
    lined_far = lax.ppermute(lined_near, "c", swap_core)
    weights = lax.all_gather(swapped, "z", axis=0)

    own_rows = lax.dynamic_slice_in_dim(stack_input, pos_s * piece, piece, 0).astype(WIDE)
    square = jnp.sum(own_rows * own_rows, axis=-1, keepdims=True)
    square = jnp.broadcast_to(square, (piece, 128))

    cut_r, cut_c = rank // count_z, count_c * rank
    cross = local_call(
        functools.partial(cross_kernel, rank),
        jax.ShapeDtypeStruct((count_y * count_z, cut_r, cut_c), LOW),
        (packed, lined_near, lined_far),
        scalars=place,
    )
    cross = lax.all_to_all(cross, ("y", "z"), 0, 0, tiled=True)
    cross = jnp.sum(cross.astype(WIDE), axis=0, keepdims=True).astype(LOW)
    cross = jnp.broadcast_to(cross, (count_y * count_z, cut_r, cut_c))
    cross = lax.all_to_all(cross, ("y", "z"), 0, 0, tiled=True)
    before, after = shifted(cross, "x", 1), shifted(cross, "x", -1)

    part_shape = jax.ShapeDtypeStruct((count_x, count_y, piece, layers * 3 * rank), LOW)
    keep, send = local_call(
        functools.partial(project_kernel, rank),
        (part_shape, part_shape),
        (rows, weights),
        scalars=place,
        flops=2 * rows.shape[0] * tok_rows * features * layers * rank * 3,
    )
    send, before, after = lax.optimization_barrier((send, before, after))
    came = lax.ppermute(send, "c", swap_core)
    half = cross.shape[0] // 2
    beyond = [shifted(before[:half], "x", 1), shifted(after[half:], "x", -1)]
    parts = (keep.astype(WIDE) + came.astype(WIDE)).astype(LOW)
    parts = parts.reshape(count_x * count_y, piece, layers * 3 * rank)
    parts, *beyond = lax.optimization_barrier((parts, *beyond))
    cross_near = jnp.stack([cross, before, after, jnp.concatenate(beyond)])
    cross_far = lax.ppermute(cross_near, "c", swap_core)
    parts = lax.all_to_all(parts, ("x", "y"), 0, 0, tiled=True)
    span = layers * rank
    acts, moves = local_call(
        functools.partial(recursion_kernel, layers, rank, float(model_width)),
        (
            jax.ShapeDtypeStruct((piece, span + rank), LOW),
            jax.ShapeDtypeStruct((piece, span), LOW),
        ),
        (parts, square, cross_near, cross_far),
        scalars=place,
        scratch=[
            pltpu.VMEM((piece, layers * 3 * rank), WIDE),
            pltpu.VMEM((layers * rank, layers * rank), LOW),
        ],
    )
    acts_near = gather_line(acts, "x")
    moves_near = gather_line(moves, "y")
    acts_near = gather_line(acts_near, "y")
    moves_near = gather_line(moves_near, "x")
    acts_far = lax.ppermute(acts_near, "c", swap_core)
    moves_far = lax.ppermute(moves_near, "c", swap_core)

    group_tokens = count_y * tok_rows
    outputs, grads = local_call(
        functools.partial(expand_kernel, layers, rank),
        (
            jax.ShapeDtypeStruct((layers, count_y, tok_rows, features), LOW),
            jax.ShapeDtypeStruct((layers, rank, 2 * features), LOW),
        ),
        (rows, weights, acts_near, acts_far, moves_near, moves_far),
        scalars=place,
        scratch=[
            pltpu.VMEM((group_tokens, features), WIDE),
            pltpu.VMEM((group_tokens, layers * rank), LOW),
            pltpu.VMEM((group_tokens, layers * rank), LOW),
            pltpu.VMEM((group_tokens, rank), WIDE),
        ],
        flops=8 * group_tokens * features * layers * rank,
    )
    grads = lax.psum_scatter(grads, "z", scatter_dimension=0, tiled=True)[0]
    outputs = outputs.reshape(sources, tok_rows, features)
    outputs = lax.all_to_all(outputs, PLANE, 0, 0, tiled=True)
    outputs = outputs.reshape(layers, count_y, tok_rows, features)
    section_rows = pl.pallas_call(
        order_kernel,
        grid=(count_y,),
        out_shape=jax.ShapeDtypeStruct((tok_rows, model_width), LOW),
        in_specs=[pl.BlockSpec((layers, 1, tok_rows, features), lambda i: (0, i, 0, 0))],
        out_specs=pl.BlockSpec((tok_rows, layers * features), lambda i: (0, i)),
        compiler_params=pltpu.CompilerParams(vmem_limit_bytes=VMEM_BYTES),
    )(outputs)

    grads = lax.ppermute(grads, across, move_back)
    squares = local_call(
        square_kernel, jax.ShapeDtypeStruct((sources * count_z, 128), WIDE), (grads,)
    )
    squares = lax.all_to_all(squares, EVERYONE, 0, 0, tiled=True)
    total_sq = jnp.sum(squares[:, 0])
    own_grads = lax.ppermute(lax.ppermute(grads, across, first_back), across, last_back)
    shard_in, shard_out = local_call(
        settle_kernel,
        (
            jax.ShapeDtypeStruct((features, rank), WIDE),
            jax.ShapeDtypeStruct((rank, features), WIDE),
        ),
        (own_grads,),
    )
    norm_limit = clip_rms * math.sqrt(2.0 * model_width * rank * layers)
    clip_factor = norm_limit / jnp.maximum(jnp.sqrt(total_sq), norm_limit)
    new_in, new_first_in, new_second_in = adam_update(
        master_in[0], first_in[0], second_in[0], clip_factor * shard_in
    )
    new_out, new_first_out, new_second_out = adam_update(
        master_out[0], first_out[0], second_out[0], clip_factor * shard_out
    )
    return (
        section_rows[None],
        new_in[None],
        new_out[None],
        new_first_in[None],
        new_first_out[None],
        new_second_in[None],
        new_second_out[None],
    )


def solution(mesh):
    layers, groups = mesh.shape["section"], mesh.shape["dp"]
    sizes = (layers // 2, 2, groups // layers, layers)
    fine = Mesh(mesh.devices.reshape(sizes), EVERYONE)
    split = ("y", "z")
    by_rows = P(SECTION, split, None)
    by_cols = P(SECTION, None, split)
    in_specs = (
        P(split, None),
        P(split, None),
        P(SECTION, None),
        by_rows,
        by_cols,
        by_rows,
        by_cols,
        by_rows,
        by_cols,
    )
    out_specs = (by_rows, by_rows, by_cols, by_rows, by_cols, by_rows, by_cols)
    return jax.shard_map(shards, mesh=fine, in_specs=in_specs, out_specs=out_specs, check_vma=False)
```

```python
import functools
import math

import jax
import jax.numpy as jnp
from jax import lax
from jax.experimental import pallas as pl
from jax.experimental.pallas import tpu as pltpu
from jax.sharding import Mesh, PartitionSpec as P

STEP = 10

norm_eps = 1e-05
gelu_coef = 0.7978845608028654
beta_one = 0.9
beta_two = 0.95
adam_eps = 1e-08
learn_rate = 0.05
decay_rate = 0.1
clip_rms = 0.5

LOW = jnp.bfloat16
WIDE = jnp.float32
SECTION = ("x", "c")
PLANE = ("x", "c", "y")
EVERYONE = ("x", "c", "y", "z")
SHIFTS = (0, 1, -1, 2)
TURNS = (0, 4, 3, 7, 2, 6, 1, 5)
FIRST = (0, 3, 3, -1, 2, -2, 1, -3)
EXTRA = 16
VMEM_BYTES = 48 * 1024 * 1024


def dot_nn(left, right):
    return lax.dot_general(left, right, (((1,), (0,)), ((), ())), preferred_element_type=WIDE)


def dot_nt(left, right):
    return lax.dot_general(left, right, (((1,), (1,)), ((), ())), preferred_element_type=WIDE)


def dot_tn(left, right):
    return lax.dot_general(left, right, (((0,), (0,)), ((), ())), preferred_element_type=WIDE)


def gelu_pair(hidden_pre):
    inner_arg = gelu_coef * (hidden_pre + 0.044715 * hidden_pre * hidden_pre * hidden_pre)
    tangent = jnp.tanh(inner_arg)
    gelu_value = 0.5 * hidden_pre * (1.0 + tangent)
    gelu_slope = 0.5 * (1.0 + tangent) + 0.5 * hidden_pre * (
        1.0 - tangent * tangent
    ) * gelu_coef * (1.0 + 3.0 * 0.044715 * hidden_pre * hidden_pre)
    return (gelu_value, gelu_slope)


def adam_update(master, first, second, grad):
    first_new = beta_one * first + (1.0 - beta_one) * grad
    second_new = beta_two * second + (1.0 - beta_two) * grad * grad
    first_hat = first_new / (1.0 - beta_one**STEP)
    second_hat = second_new / (1.0 - beta_two**STEP)
    master_new = master - learn_rate * (
        first_hat / (jnp.sqrt(second_hat) + adam_eps) + decay_rate * master
    )
    return (master_new, first_new, second_new)


def local_call(kernel, out_shape, operands, scalars=None, scratch=(), flops=0):
    specs = jax.tree.map(lambda _: pl.BlockSpec(memory_space=pltpu.VMEM), out_shape)
    moved = sum(a.size * a.dtype.itemsize for a in operands)
    moved += sum(a.size * a.dtype.itemsize for a in jax.tree.leaves(out_shape))
    in_specs = [pl.BlockSpec(memory_space=pltpu.VMEM)] * len(operands)
    if scalars is not None:
        operands = (scalars,) + tuple(operands)
        in_specs = [pl.BlockSpec(memory_space=pltpu.SMEM)] + in_specs
    return pl.pallas_call(
        kernel,
        out_shape=out_shape,
        in_specs=in_specs,
        out_specs=specs,
        scratch_shapes=list(scratch),
        compiler_params=pltpu.CompilerParams(vmem_limit_bytes=VMEM_BYTES),
        cost_estimate=pl.CostEstimate(flops=flops, bytes_accessed=moved, transcendentals=0),
    )(*operands)


def shifted(block, axis, distance):
    size = lax.axis_size(axis)
    return lax.ppermute(block, axis, [(i, (i + distance) % size) for i in range(size)])


def gather_line(block, axis):
    return jnp.stack([block] + [shifted(block, axis, d) for d in SHIFTS[1:]])


def pack_kernel(gain_ref, in_ref, out_ref, pack_ref):
    features, rank = in_ref.shape[1:]
    gain = jnp.broadcast_to(gain_ref[...], (rank, features)).T
    work_in = in_ref[0].astype(LOW).astype(WIDE)
    pack_ref[:features, :rank] = (work_in * gain).astype(LOW)
    pack_ref[:features, rank:] = out_ref[0].T.astype(LOW)
    spare = (EXTRA, 2 * rank)
    row = lax.broadcasted_iota(jnp.int32, spare, 0)
    rows = jnp.zeros(spare, WIDE)
    left = gain_ref[...]
    chunks = features // rank
    for term in range(3):
        part = left.astype(LOW).astype(WIDE)
        left = left - part
        for k in range(chunks):
            chunk = part[:, k * rank : (k + 1) * rank]
            chunk = jnp.broadcast_to(jnp.concatenate([chunk, chunk], axis=1), spare)
            rows = jnp.where(row == term * chunks + k, chunk, rows)
    pack_ref[features:, :] = rows.astype(LOW)


def packed_gain(tail, chunks):
    rows = tail.astype(WIDE)
    parts = []
    for k in range(chunks):
        terms = [rows[t * chunks + k : t * chunks + k + 1] for t in range(3)]
        parts.append(terms[0] + terms[1] + terms[2])
    return jnp.concatenate(parts, axis=1)


def cross_kernel(rank, place_ref, own_ref, near_ref, far_ref, out_ref):
    core, section, column = place_ref[0], place_ref[1], place_ref[2]
    count = len(SHIFTS)
    cut = out_ref.shape[1]
    cuts = rank // cut
    features = own_ref.shape[0] - EXTRA
    own = own_ref[:features, rank:].T
    for slot, step in enumerate(SHIFTS):
        owner = lax.rem(column - step + count, count)
        blocks = []
        for line_ref, from_core in ((near_ref, core), (far_ref, 1 - core)):
            both = dot_nn(own, line_ref[slot, :features])
            later = 2 * owner + from_core > section
            blocks.append(jnp.where(later, both[:, :rank], both[:, rank:]).astype(LOW))
        even = jnp.where(core == 0, blocks[0], blocks[1])
        odd = jnp.where(core == 0, blocks[1], blocks[0])
        for k in range(cuts):
            sel = slice(k * cut, (k + 1) * cut)
            out_ref[owner * cuts + k, :, :rank] = even[sel]
            out_ref[owner * cuts + k, :, rank:] = odd[sel]


def project_kernel(rank, place_ref, rows_ref, weight_ref, keep_ref, send_ref):
    groups, both_rows, features = rows_ref.shape
    layers = weight_ref.shape[0]
    half = both_rows // 2
    columns = keep_ref.shape[0]
    piece = half // (2 * columns)
    core, section = place_ref[0], place_ref[1]
    for layer in range(layers):
        weight = weight_ref[lax.rem(section + TURNS[layer], layers), :features]
        base = layer * 3 * rank
        for group in range(groups):
            first = dot_nn(rows_ref[group, :half, :], weight).astype(LOW)
            second = dot_nn(rows_ref[group, half:, :], weight[:, rank:]).astype(LOW)
            for column in range(columns):
                low = 2 * column * piece
                even, odd = slice(low, low + piece), slice(low + piece, low + 2 * piece)
                for value, at, width in ((first, base, 2 * rank), (second, base + 2 * rank, rank)):
                    lanes = slice(at, at + width)
                    keep_ref[column, group, :, lanes] = jnp.where(core == 0, value[even], value[odd])
                    send_ref[column, group, :, lanes] = jnp.where(core == 0, value[odd], value[even])


def recursion_kernel(
    layers, rank, width, place_ref, parts_ref, square_ref, near_ref, far_ref, act_ref, moved_ref, sums_ref, cross_ref
):
    core, column = place_ref[0], place_ref[2]
    count = len(SHIFTS)
    pieces, cut = near_ref.shape[1:3]
    cuts = rank // cut
    for slot, distance in enumerate(SHIFTS):
        owner = lax.rem(column - distance + count, count)
        for piece_ref, from_core in ((near_ref, core), (far_ref, 1 - core)):
            start = (2 * owner + from_core) * rank
            for k in range(pieces):
                at = pl.multiple_of(start + (k % cuts) * cut, cut)
                low = (k // cuts) * 2 * rank
                cross_ref[pl.ds(at, cut), low : low + 2 * rank] = piece_ref[slot, k]

    total = parts_ref[0].astype(WIDE)
    for source in range(1, parts_ref.shape[0]):
        total = total + parts_ref[source].astype(WIDE)
    sums_ref[...] = total
    rank3 = 3 * rank
    down = [sums_ref[:, k * rank3 : k * rank3 + rank] for k in range(layers)]
    up = [sums_ref[:, k * rank3 + rank : k * rank3 + 2 * rank] for k in range(layers)]
    back = [sums_ref[:, k * rank3 + 2 * rank : (k + 1) * rank3] for k in range(layers)]
    square = square_ref[:, 0:1]

    acts, pres, invs = [], [], []
    for s in range(layers):
        inv = lax.rsqrt(jnp.maximum(square, 0.0) / width + norm_eps)
        pre = inv * down[s]
        act, _ = gelu_pair(pre)
        act = act.astype(LOW)
        acts.append(act)
        pres.append(pre)
        invs.append(inv)
        act_ref[:, s * rank : (s + 1) * rank] = act
        low = s * rank
        forward = dot_nn(act, cross_ref[low : low + rank, low:])
        before = up[s]
        up[s] = before + forward[:, :rank]
        square = square + jnp.sum(act.astype(WIDE) * (before + up[s]), axis=-1, keepdims=True)
        if s + 1 < layers:
            mirrored = dot_nt(act, cross_ref[low + rank :, low : low + rank])
            for k in range(s + 1, layers):
                at = (k - s) * rank
                down[k] = down[k] + forward[:, at : at + rank]
                up[k] = up[k] + mirrored[:, at - rank : at]

    trailing = jnp.zeros_like(square)
    lane = lax.broadcasted_iota(jnp.int32, (square.shape[0], rank), 1)
    tail = jnp.zeros((square.shape[0], rank), WIDE)
    for s in reversed(range(layers)):
        _, slope = gelu_pair(pres[s])
        d_pre = (back[s] - trailing * up[s]) * slope
        coef = invs[s] * invs[s] * (1.0 / width) * jnp.sum(d_pre * pres[s], axis=-1, keepdims=True)
        moved = (invs[s] * d_pre).astype(LOW)
        moved_ref[:, s * rank : (s + 1) * rank] = moved
        coef_high = coef.astype(LOW).astype(WIDE)
        tail = tail + jnp.where(lane == s, coef_high, 0.0)
        tail = tail + jnp.where(lane == s + layers, coef - coef_high, 0.0)
        if s > 0:
            low = s * rank
            gain_term = dot_nt(moved, cross_ref[:low, low : low + rank])
            scaled_act = (trailing * acts[s].astype(WIDE)).astype(LOW)
            norm_term = dot_nn(scaled_act, cross_ref[low : low + rank, :low])
            for k in range(s):
                sel = slice(k * rank, (k + 1) * rank)
                back[k] = back[k] + gain_term[:, sel] - norm_term[:, sel]
        trailing = trailing + coef
    act_ref[:, layers * rank :] = tail.astype(LOW)


def expand_kernel(
    layers,
    rank,
    place_ref,
    rows_ref,
    weight_ref,
    act_near_ref,
    act_far_ref,
    move_near_ref,
    move_far_ref,
    out_ref,
    grad_ref,
    wide_ref,
    act_ref,
    moved_ref,
    coef_ref,
):
    groups, both_rows, features = rows_ref.shape
    half = both_rows // 2
    piece = act_near_ref.shape[2]
    span = layers * rank
    core, section, column, line = (place_ref[i] for i in range(4))
    count = len(SHIFTS)
    for group in range(groups):
        base = group * half
        wide_ref[base : base + half, :] = rows_ref[group, :half, :].astype(WIDE)
    for slot_y, step_y in enumerate(SHIFTS):
        group = lax.rem(line - step_y + count, count)
        for slot_x, step_x in enumerate(SHIFTS):
            owner = lax.rem(column - step_x + count, count)
            for some_act, some_move, from_core in (
                (act_near_ref, move_near_ref, core),
                (act_far_ref, move_far_ref, 1 - core),
            ):
                at = pl.multiple_of(group * half + (2 * owner + from_core) * piece, piece)
                dest = pl.ds(at, piece)
                act_ref[dest, :] = some_act[slot_y, slot_x, :, :span]
                coef_ref[dest, :] = some_act[slot_y, slot_x, :, span:].astype(WIDE)
                moved_ref[dest, :] = some_move[slot_x, slot_y]

    for layer in range(layers):
        up_weight = weight_ref[lax.rem(section + TURNS[layer], layers), :features, rank:]
        act = act_ref[:, layer * rank : (layer + 1) * rank]
        total = wide_ref[...] + dot_nt(act, up_weight)
        wide_ref[...] = total
        lowered = total.astype(LOW)
        for group in range(groups):
            out_ref[layer, group] = lowered[group * half : (group + 1) * half]

    for group in range(groups):
        base = group * half
        wide_ref[base : base + half, :] = rows_ref[group, half:, :].astype(WIDE)
    for layer in reversed(range(layers)):
        slot = lax.rem(section + TURNS[layer], layers)
        delta = wide_ref[...].astype(LOW)
        act = act_ref[:, layer * rank : (layer + 1) * rank]
        moved = moved_ref[:, layer * rank : (layer + 1) * rank]
        if layer > 0:
            current = out_ref[layer - 1].reshape(groups * half, features)
        else:
            current = rows_ref[:, :half, :].reshape(groups * half, features)
        grad_ref[slot, :, features:] = dot_tn(act, delta).astype(LOW)
        gain = packed_gain(weight_ref[slot, features:, :rank], features // rank)
        grad_ref[slot, :, :features] = (dot_tn(moved, current) * gain).astype(LOW)
        if layer > 0:
            coef = coef_ref[:, layer : layer + 1] + coef_ref[:, layers + layer : layers + layer + 1]
            wide_ref[...] += dot_nt(moved, weight_ref[slot, :features, :rank]) - coef * current.astype(WIDE)


def square_kernel(grad_ref, out_ref):
    grad = grad_ref[...].astype(WIDE)
    out_ref[...] = jnp.full(out_ref.shape, jnp.sum(grad * grad), WIDE)


def settle_kernel(grad_ref, in_ref, out_ref):
    features = out_ref.shape[1]
    in_ref[...] = grad_ref[:, :features].astype(WIDE).T
    out_ref[...] = grad_ref[:, features:].astype(WIDE)


def order_kernel(block_ref, out_ref):
    layers, features = block_ref.shape[0], block_ref.shape[3]
    for layer in range(layers):
        out_ref[:, layer * features : (layer + 1) * features] = block_ref[layer, 0]


def shards(
    stack_input,
    out_cotangent,
    norm_gain,
    master_in,
    master_out,
    first_in,
    first_out,
    second_in,
    second_out,
):
    count_x, count_c, count_y, count_z = (lax.axis_size(a) for a in EVERYONE)
    pos_x, pos_c, pos_y, pos_z = (lax.axis_index(a) for a in EVERYONE)
    layers = count_x * count_c
    pos_s = pos_x * count_c + pos_c
    place = jnp.stack([pos_c, pos_s, pos_x, pos_y]).astype(jnp.int32)
    sources = layers * count_y
    tok_rows, model_width = stack_input.shape
    features, rank = master_in.shape[1:]
    piece = tok_rows // layers
    swap_core = [(0, 1), (1, 0)]
    grid = [(a, b) for a in range(layers) for b in range(count_z)]
    turned = {(a, b): (b + TURNS[a]) % count_z for a, b in grid}
    swap = [(a * count_z + b, b * count_z + turned[a, b]) for a, b in grid]
    most_back = [
        (b * count_z + turned[a, b], a * count_z + (turned[a, b] - FIRST[a]) % count_z) for a, b in grid
    ]
    last_back = [(a * count_z + b, a * count_z + (b - TURNS[a] + FIRST[a]) % count_z) for a, b in grid]
    across = SECTION + ("z",)

    gain_own = lax.dynamic_slice_in_dim(norm_gain, (pos_y * count_z + pos_z) * features, features, 1)
    def blocks_of(rows):
        return jnp.stack(
            [
                lax.dynamic_slice_in_dim(rows, (g * count_z + pos_s) * features, features, 1)
                for g in range(count_y)
            ]
        )

    rows = jnp.concatenate([blocks_of(stack_input), blocks_of(out_cotangent)], axis=1)
    gain_own, rows = lax.optimization_barrier((gain_own, rows))
    rows = lax.all_to_all(rows, "y", 0, 0, tiled=True)
    packed = local_call(
        pack_kernel, jax.ShapeDtypeStruct((features + EXTRA, 2 * rank), LOW), (gain_own, master_in, master_out)
    )
    swapped = lax.ppermute(packed, across, swap)
    lined_near = gather_line(packed, "x")
    swapped, lined_near, rows = lax.optimization_barrier((swapped, lined_near, rows))
    lined_far = lax.ppermute(lined_near, "c", swap_core)
    weights = lax.all_gather(swapped, "z", axis=0)

    own_rows = lax.dynamic_slice_in_dim(stack_input, pos_s * piece, piece, 0).astype(WIDE)
    square = jnp.sum(own_rows * own_rows, axis=-1, keepdims=True)
    square = jnp.broadcast_to(square, (piece, 128))

    cut_r, cut_c = rank // count_z, count_c * rank
    cross = local_call(
        functools.partial(cross_kernel, rank),
        jax.ShapeDtypeStruct((count_y * count_z, cut_r, cut_c), LOW),
        (packed, lined_near, lined_far),
        scalars=place,
    )
    cross = lax.all_to_all(cross, ("y", "z"), 0, 0, tiled=True)
    cross = jnp.sum(cross.astype(WIDE), axis=0, keepdims=True).astype(LOW)
    cross = jnp.broadcast_to(cross, (count_y * count_z, cut_r, cut_c))
    cross = lax.all_to_all(cross, ("y", "z"), 0, 0, tiled=True)
    before, after = shifted(cross, "x", 1), shifted(cross, "x", -1)

    part_shape = jax.ShapeDtypeStruct((count_x, count_y, piece, layers * 3 * rank), LOW)
    keep, send = local_call(
        functools.partial(project_kernel, rank),
        (part_shape, part_shape),
        (rows, weights),
        scalars=place,
        flops=2 * rows.shape[0] * tok_rows * features * layers * rank * 3,
    )
    send, before, after = lax.optimization_barrier((send, before, after))
    came = lax.ppermute(send, "c", swap_core)
    half = cross.shape[0] // 2
    beyond = [shifted(before[:half], "x", 1), shifted(after[half:], "x", -1)]
    parts = (keep.astype(WIDE) + came.astype(WIDE)).astype(LOW)
    parts = parts.reshape(count_x * count_y, piece, layers * 3 * rank)
    parts, *beyond = lax.optimization_barrier((parts, *beyond))
    cross_near = jnp.stack([cross, before, after, jnp.concatenate(beyond)])
    cross_far = lax.ppermute(cross_near, "c", swap_core)
    parts = lax.all_to_all(parts, ("x", "y"), 0, 0, tiled=True)
    span = layers * rank
    acts, moves = local_call(
        functools.partial(recursion_kernel, layers, rank, float(model_width)),
        (
            jax.ShapeDtypeStruct((piece, span + rank), LOW),
            jax.ShapeDtypeStruct((piece, span), LOW),
        ),
        (parts, square, cross_near, cross_far),
        scalars=place,
        scratch=[
            pltpu.VMEM((piece, layers * 3 * rank), WIDE),
            pltpu.VMEM((layers * rank, layers * rank), LOW),
        ],
    )
    acts_near = gather_line(acts, "x")
    moves_near = gather_line(moves, "y")
    acts_near = gather_line(acts_near, "y")
    moves_near = gather_line(moves_near, "x")
    acts_far = lax.ppermute(acts_near, "c", swap_core)
    moves_far = lax.ppermute(moves_near, "c", swap_core)

    group_tokens = count_y * tok_rows
    outputs, grads = local_call(
        functools.partial(expand_kernel, layers, rank),
        (
            jax.ShapeDtypeStruct((layers, count_y, tok_rows, features), LOW),
            jax.ShapeDtypeStruct((layers, rank, 2 * features), LOW),
        ),
        (rows, weights, acts_near, acts_far, moves_near, moves_far),
        scalars=place,
        scratch=[
            pltpu.VMEM((group_tokens, features), WIDE),
            pltpu.VMEM((group_tokens, layers * rank), LOW),
            pltpu.VMEM((group_tokens, layers * rank), LOW),
            pltpu.VMEM((group_tokens, rank), WIDE),
        ],
        flops=8 * group_tokens * features * layers * rank,
    )
    grads = lax.psum_scatter(grads, "z", scatter_dimension=0, tiled=True)[0]
    outputs = outputs.reshape(sources, tok_rows, features)
    outputs = lax.all_to_all(outputs, PLANE, 0, 0, tiled=True)
    outputs = outputs.reshape(layers, count_y, tok_rows, features)
    section_rows = pl.pallas_call(
        order_kernel,
        grid=(count_y,),
        out_shape=jax.ShapeDtypeStruct((tok_rows, model_width), LOW),
        in_specs=[pl.BlockSpec((layers, 1, tok_rows, features), lambda i: (0, i, 0, 0))],
        out_specs=pl.BlockSpec((tok_rows, layers * features), lambda i: (0, i)),
        compiler_params=pltpu.CompilerParams(vmem_limit_bytes=VMEM_BYTES),
    )(outputs)

    squares = local_call(
        square_kernel, jax.ShapeDtypeStruct((sources * count_z, 128), WIDE), (grads,)
    )
    squares = lax.all_to_all(squares, EVERYONE, 0, 0, tiled=True)
    total_sq = jnp.sum(squares[:, 0])
    own_grads = lax.ppermute(lax.ppermute(grads, across, most_back), across, last_back)
    shard_in, shard_out = local_call(
        settle_kernel,
        (
            jax.ShapeDtypeStruct((features, rank), WIDE),
            jax.ShapeDtypeStruct((rank, features), WIDE),
        ),
        (own_grads,),
    )
    norm_limit = clip_rms * math.sqrt(2.0 * model_width * rank * layers)
    clip_factor = norm_limit / jnp.maximum(jnp.sqrt(total_sq), norm_limit)
    new_in, new_first_in, new_second_in = adam_update(
        master_in[0], first_in[0], second_in[0], clip_factor * shard_in
    )
    new_out, new_first_out, new_second_out = adam_update(
        master_out[0], first_out[0], second_out[0], clip_factor * shard_out
    )
    return (
        section_rows[None],
        new_in[None],
        new_out[None],
        new_first_in[None],
        new_first_out[None],
        new_second_in[None],
        new_second_out[None],
    )


def solution(mesh):
    layers, groups = mesh.shape["section"], mesh.shape["dp"]
    sizes = (layers // 2, 2, groups // layers, layers)
    fine = Mesh(mesh.devices.reshape(sizes), EVERYONE)
    split = ("y", "z")
    by_rows = P(SECTION, split, None)
    by_cols = P(SECTION, None, split)
    in_specs = (
        P(split, None),
        P(split, None),
        P(SECTION, None),
        by_rows,
        by_cols,
        by_rows,
        by_cols,
        by_rows,
        by_cols,
    )
    out_specs = (by_rows, by_rows, by_cols, by_rows, by_cols, by_rows, by_cols)
    return jax.shard_map(shards, mesh=fine, in_specs=in_specs, out_specs=out_specs, check_vma=False)
```

```python
import functools
import math

import jax
import jax.numpy as jnp
from jax import lax
from jax.experimental import pallas as pl
from jax.experimental.pallas import tpu as pltpu
from jax.sharding import Mesh, PartitionSpec as P

STEP = 10

norm_eps = 1e-05
gelu_coef = 0.7978845608028654
beta_one = 0.9
beta_two = 0.95
adam_eps = 1e-08
learn_rate = 0.05
decay_rate = 0.1
clip_rms = 0.5

LOW = jnp.bfloat16
WIDE = jnp.float32
SECTION = ("x", "c")
PLANE = ("x", "c", "y")
EVERYONE = ("x", "c", "y", "z")
SHIFTS = (0, 1, -1, 2)
TURNS = (0, 4, 3, 7, 2, 6, 1, 5)
EXTRA = 16
VMEM_BYTES = 48 * 1024 * 1024


def dot_nn(left, right):
    return lax.dot_general(left, right, (((1,), (0,)), ((), ())), preferred_element_type=WIDE)


def dot_nt(left, right):
    return lax.dot_general(left, right, (((1,), (1,)), ((), ())), preferred_element_type=WIDE)


def dot_tn(left, right):
    return lax.dot_general(left, right, (((0,), (0,)), ((), ())), preferred_element_type=WIDE)


def gelu_pair(hidden_pre):
    inner_arg = gelu_coef * (hidden_pre + 0.044715 * hidden_pre * hidden_pre * hidden_pre)
    tangent = jnp.tanh(inner_arg)
    gelu_value = 0.5 * hidden_pre * (1.0 + tangent)
    gelu_slope = 0.5 * (1.0 + tangent) + 0.5 * hidden_pre * (
        1.0 - tangent * tangent
    ) * gelu_coef * (1.0 + 3.0 * 0.044715 * hidden_pre * hidden_pre)
    return (gelu_value, gelu_slope)


def adam_update(master, first, second, grad):
    first_new = beta_one * first + (1.0 - beta_one) * grad
    second_new = beta_two * second + (1.0 - beta_two) * grad * grad
    first_hat = first_new / (1.0 - beta_one**STEP)
    second_hat = second_new / (1.0 - beta_two**STEP)
    master_new = master - learn_rate * (
        first_hat / (jnp.sqrt(second_hat) + adam_eps) + decay_rate * master
    )
    return (master_new, first_new, second_new)


def local_call(kernel, out_shape, operands, scalars=None, scratch=(), flops=0):
    specs = jax.tree.map(lambda _: pl.BlockSpec(memory_space=pltpu.VMEM), out_shape)
    moved = sum(a.size * a.dtype.itemsize for a in operands)
    moved += sum(a.size * a.dtype.itemsize for a in jax.tree.leaves(out_shape))
    in_specs = [pl.BlockSpec(memory_space=pltpu.VMEM)] * len(operands)
    if scalars is not None:
        operands = (scalars,) + tuple(operands)
        in_specs = [pl.BlockSpec(memory_space=pltpu.SMEM)] + in_specs
    return pl.pallas_call(
        kernel,
        out_shape=out_shape,
        in_specs=in_specs,
        out_specs=specs,
        scratch_shapes=list(scratch),
        compiler_params=pltpu.CompilerParams(vmem_limit_bytes=VMEM_BYTES),
        cost_estimate=pl.CostEstimate(flops=flops, bytes_accessed=moved, transcendentals=0),
    )(*operands)


def shifted(block, axis, distance):
    size = lax.axis_size(axis)
    return lax.ppermute(block, axis, [(i, (i + distance) % size) for i in range(size)])


def gather_line(block, axis):
    return jnp.stack([block] + [shifted(block, axis, d) for d in SHIFTS[1:]])


def pack_kernel(gain_ref, in_ref, out_ref, pack_ref):
    features, rank = in_ref.shape[1:]
    gain = jnp.broadcast_to(gain_ref[...], (rank, features)).T
    work_in = in_ref[0].astype(LOW).astype(WIDE)
    pack_ref[:features, :rank] = (work_in * gain).astype(LOW)
    pack_ref[:features, rank:] = out_ref[0].T.astype(LOW)
    spare = (EXTRA, 2 * rank)
    row = lax.broadcasted_iota(jnp.int32, spare, 0)
    rows = jnp.zeros(spare, WIDE)
    left = gain_ref[...]
    chunks = features // rank
    for term in range(3):
        part = left.astype(LOW).astype(WIDE)
        left = left - part
        for k in range(chunks):
            chunk = part[:, k * rank : (k + 1) * rank]
            chunk = jnp.broadcast_to(jnp.concatenate([chunk, chunk], axis=1), spare)
            rows = jnp.where(row == term * chunks + k, chunk, rows)
    pack_ref[features:, :] = rows.astype(LOW)


def packed_gain(tail, chunks):
    rows = tail.astype(WIDE)
    parts = []
    for k in range(chunks):
        terms = [rows[t * chunks + k : t * chunks + k + 1] for t in range(3)]
        parts.append(terms[0] + terms[1] + terms[2])
    return jnp.concatenate(parts, axis=1)


def cross_kernel(rank, place_ref, own_ref, near_ref, far_ref, out_ref):
    core, section, column = place_ref[0], place_ref[1], place_ref[2]
    count = len(SHIFTS)
    cut = out_ref.shape[1]
    cuts = rank // cut
    features = own_ref.shape[0] - EXTRA
    own = own_ref[:features, rank:].T
    for slot, step in enumerate(SHIFTS):
        owner = lax.rem(column - step + count, count)
        blocks = []
        for line_ref, from_core in ((near_ref, core), (far_ref, 1 - core)):
            both = dot_nn(own, line_ref[slot, :features])
            later = 2 * owner + from_core > section
            blocks.append(jnp.where(later, both[:, :rank], both[:, rank:]).astype(LOW))
        even = jnp.where(core == 0, blocks[0], blocks[1])
        odd = jnp.where(core == 0, blocks[1], blocks[0])
        for k in range(cuts):
            sel = slice(k * cut, (k + 1) * cut)
            out_ref[owner * cuts + k, :, :rank] = even[sel]
            out_ref[owner * cuts + k, :, rank:] = odd[sel]


def project_kernel(rank, place_ref, rows_ref, weight_ref, keep_ref, send_ref):
    groups, both_rows, features = rows_ref.shape
    layers = weight_ref.shape[0]
    half = both_rows // 2
    columns = keep_ref.shape[0]
    piece = half // (2 * columns)
    core, section = place_ref[0], place_ref[1]
    for layer in range(layers):
        weight = weight_ref[lax.rem(section + TURNS[layer], layers), :features]
        base = layer * 3 * rank
        for group in range(groups):
            first = dot_nn(rows_ref[group, :half, :], weight).astype(LOW)
            second = dot_nn(rows_ref[group, half:, :], weight[:, rank:]).astype(LOW)
            for column in range(columns):
                low = 2 * column * piece
                even, odd = slice(low, low + piece), slice(low + piece, low + 2 * piece)
                for value, at, width in ((first, base, 2 * rank), (second, base + 2 * rank, rank)):
                    lanes = slice(at, at + width)
                    keep_ref[column, group, :, lanes] = jnp.where(core == 0, value[even], value[odd])
                    send_ref[column, group, :, lanes] = jnp.where(core == 0, value[odd], value[even])


def recursion_kernel(
    layers, rank, width, place_ref, parts_ref, square_ref, near_ref, far_ref, act_ref, moved_ref, sums_ref, cross_ref
):
    core, column = place_ref[0], place_ref[2]
    count = len(SHIFTS)
    pieces, cut = near_ref.shape[1:3]
    cuts = rank // cut
    for slot, distance in enumerate(SHIFTS):
        owner = lax.rem(column - distance + count, count)
        for piece_ref, from_core in ((near_ref, core), (far_ref, 1 - core)):
            start = (2 * owner + from_core) * rank
            for k in range(pieces):
                at = pl.multiple_of(start + (k % cuts) * cut, cut)
                low = (k // cuts) * 2 * rank
                cross_ref[pl.ds(at, cut), low : low + 2 * rank] = piece_ref[slot, k]

    total = parts_ref[0].astype(WIDE)
    for source in range(1, parts_ref.shape[0]):
        total = total + parts_ref[source].astype(WIDE)
    sums_ref[...] = total
    rank3 = 3 * rank
    down = [sums_ref[:, k * rank3 : k * rank3 + rank] for k in range(layers)]
    up = [sums_ref[:, k * rank3 + rank : k * rank3 + 2 * rank] for k in range(layers)]
    back = [sums_ref[:, k * rank3 + 2 * rank : (k + 1) * rank3] for k in range(layers)]
    square = square_ref[:, 0:1]

    acts, pres, invs = [], [], []
    for s in range(layers):
        inv = lax.rsqrt(jnp.maximum(square, 0.0) / width + norm_eps)
        pre = inv * down[s]
        act, _ = gelu_pair(pre)
        act = act.astype(LOW)
        acts.append(act)
        pres.append(pre)
        invs.append(inv)
        act_ref[:, s * rank : (s + 1) * rank] = act
        low = s * rank
        forward = dot_nn(act, cross_ref[low : low + rank, low:])
        before = up[s]
        up[s] = before + forward[:, :rank]
        square = square + jnp.sum(act.astype(WIDE) * (before + up[s]), axis=-1, keepdims=True)
        if s + 1 < layers:
            mirrored = dot_nt(act, cross_ref[low + rank :, low : low + rank])
            for k in range(s + 1, layers):
                at = (k - s) * rank
                down[k] = down[k] + forward[:, at : at + rank]
                up[k] = up[k] + mirrored[:, at - rank : at]

    trailing = jnp.zeros_like(square)
    lane = lax.broadcasted_iota(jnp.int32, (square.shape[0], rank), 1)
    tail = jnp.zeros((square.shape[0], rank), WIDE)
    for s in reversed(range(layers)):
        _, slope = gelu_pair(pres[s])
        d_pre = (back[s] - trailing * up[s]) * slope
        coef = invs[s] * invs[s] * (1.0 / width) * jnp.sum(d_pre * pres[s], axis=-1, keepdims=True)
        moved = (invs[s] * d_pre).astype(LOW)
        moved_ref[:, s * rank : (s + 1) * rank] = moved
        coef_high = coef.astype(LOW).astype(WIDE)
        tail = tail + jnp.where(lane == s, coef_high, 0.0)
        tail = tail + jnp.where(lane == s + layers, coef - coef_high, 0.0)
        if s > 0:
            low = s * rank
            gain_term = dot_nt(moved, cross_ref[:low, low : low + rank])
            scaled_act = (trailing * acts[s].astype(WIDE)).astype(LOW)
            norm_term = dot_nn(scaled_act, cross_ref[low : low + rank, :low])
            for k in range(s):
                sel = slice(k * rank, (k + 1) * rank)
                back[k] = back[k] + gain_term[:, sel] - norm_term[:, sel]
        trailing = trailing + coef
    act_ref[:, layers * rank :] = tail.astype(LOW)


def expand_kernel(
    layers,
    rank,
    place_ref,
    rows_ref,
    weight_ref,
    act_near_ref,
    act_far_ref,
    move_near_ref,
    move_far_ref,
    out_ref,
    grad_ref,
    wide_ref,
    act_ref,
    moved_ref,
    coef_ref,
):
    groups, both_rows, features = rows_ref.shape
    half = both_rows // 2
    piece = act_near_ref.shape[2]
    span = layers * rank
    core, section, column, line = (place_ref[i] for i in range(4))
    count = len(SHIFTS)
    for group in range(groups):
        base = group * half
        wide_ref[base : base + half, :] = rows_ref[group, :half, :].astype(WIDE)
    for slot_y, step_y in enumerate(SHIFTS):
        group = lax.rem(line - step_y + count, count)
        for slot_x, step_x in enumerate(SHIFTS):
            owner = lax.rem(column - step_x + count, count)
            for some_act, some_move, from_core in (
                (act_near_ref, move_near_ref, core),
                (act_far_ref, move_far_ref, 1 - core),
            ):
                at = pl.multiple_of(group * half + (2 * owner + from_core) * piece, piece)
                dest = pl.ds(at, piece)
                act_ref[dest, :] = some_act[slot_y, slot_x, :, :span]
                coef_ref[dest, :] = some_act[slot_y, slot_x, :, span:].astype(WIDE)
                moved_ref[dest, :] = some_move[slot_x, slot_y]

    for layer in range(layers):
        up_weight = weight_ref[lax.rem(section + TURNS[layer], layers), :features, rank:]
        act = act_ref[:, layer * rank : (layer + 1) * rank]
        total = wide_ref[...] + dot_nt(act, up_weight)
        wide_ref[...] = total
        lowered = total.astype(LOW)
        for group in range(groups):
            out_ref[layer, group] = lowered[group * half : (group + 1) * half]

    for group in range(groups):
        base = group * half
        wide_ref[base : base + half, :] = rows_ref[group, half:, :].astype(WIDE)
    for layer in reversed(range(layers)):
        slot = lax.rem(section + TURNS[layer], layers)
        delta = wide_ref[...].astype(LOW)
        act = act_ref[:, layer * rank : (layer + 1) * rank]
        moved = moved_ref[:, layer * rank : (layer + 1) * rank]
        if layer > 0:
            current = out_ref[layer - 1].reshape(groups * half, features)
        else:
            current = rows_ref[:, :half, :].reshape(groups * half, features)
        grad_ref[slot, :, features:] = dot_tn(act, delta).astype(LOW)
        gain = packed_gain(weight_ref[slot, features:, :rank], features // rank)
        grad_ref[slot, :, :features] = (dot_tn(moved, current) * gain).astype(LOW)
        if layer > 0:
            coef = coef_ref[:, layer : layer + 1] + coef_ref[:, layers + layer : layers + layer + 1]
            wide_ref[...] += dot_nt(moved, weight_ref[slot, :features, :rank]) - coef * current.astype(WIDE)


def square_kernel(grad_ref, out_ref):
    grad = grad_ref[...].astype(WIDE)
    out_ref[...] = jnp.full(out_ref.shape, jnp.sum(grad * grad), WIDE)


def settle_kernel(grad_ref, in_ref, out_ref):
    features = out_ref.shape[1]
    in_ref[...] = grad_ref[:, :features].astype(WIDE).T
    out_ref[...] = grad_ref[:, features:].astype(WIDE)


def order_kernel(block_ref, out_ref):
    layers, features = block_ref.shape[0], block_ref.shape[3]
    for layer in range(layers):
        out_ref[:, layer * features : (layer + 1) * features] = block_ref[layer, 0]


def shards(
    stack_input,
    out_cotangent,
    norm_gain,
    master_in,
    master_out,
    first_in,
    first_out,
    second_in,
    second_out,
):
    count_x, count_c, count_y, count_z = (lax.axis_size(a) for a in EVERYONE)
    pos_x, pos_c, pos_y, pos_z = (lax.axis_index(a) for a in EVERYONE)
    layers = count_x * count_c
    pos_s = pos_x * count_c + pos_c
    place = jnp.stack([pos_c, pos_s, pos_x, pos_y]).astype(jnp.int32)
    sources = layers * count_y
    tok_rows, model_width = stack_input.shape
    features, rank = master_in.shape[1:]
    piece = tok_rows // layers
    swap_core = [(0, 1), (1, 0)]
    grid = [(a, b) for a in range(layers) for b in range(count_z)]
    turned = {(a, b): (b + TURNS[a]) % count_z for a, b in grid}
    swap = [(a * count_z + b, b * count_z + turned[a, b]) for a, b in grid]
    home = [(j, i) for i, j in swap]
    across = SECTION + ("z",)

    gain_own = lax.dynamic_slice_in_dim(norm_gain, (pos_y * count_z + pos_z) * features, features, 1)
    def blocks_of(rows):
        return jnp.stack(
            [
                lax.dynamic_slice_in_dim(rows, (g * count_z + pos_s) * features, features, 1)
                for g in range(count_y)
            ]
        )

    rows = jnp.concatenate([blocks_of(stack_input), blocks_of(out_cotangent)], axis=1)
    gain_own, rows = lax.optimization_barrier((gain_own, rows))
    rows = lax.all_to_all(rows, "y", 0, 0, tiled=True)
    packed = local_call(
        pack_kernel, jax.ShapeDtypeStruct((features + EXTRA, 2 * rank), LOW), (gain_own, master_in, master_out)
    )
    swapped = lax.ppermute(packed, across, swap)
    lined_near = gather_line(packed, "x")
    swapped, lined_near, rows = lax.optimization_barrier((swapped, lined_near, rows))
    lined_far = lax.ppermute(lined_near, "c", swap_core)
    weights = lax.all_gather(swapped, "z", axis=0)

    own_rows = lax.dynamic_slice_in_dim(stack_input, pos_s * piece, piece, 0).astype(WIDE)
    square = jnp.sum(own_rows * own_rows, axis=-1, keepdims=True)
    square = jnp.broadcast_to(square, (piece, 128))

    cut_r, cut_c = rank // count_z, count_c * rank
    cross = local_call(
        functools.partial(cross_kernel, rank),
        jax.ShapeDtypeStruct((count_y * count_z, cut_r, cut_c), LOW),
        (packed, lined_near, lined_far),
        scalars=place,
    )
    cross = lax.all_to_all(cross, ("y", "z"), 0, 0, tiled=True)
    cross = jnp.sum(cross.astype(WIDE), axis=0, keepdims=True).astype(LOW)
    cross = jnp.broadcast_to(cross, (count_y * count_z, cut_r, cut_c))
    cross = lax.all_to_all(cross, ("y", "z"), 0, 0, tiled=True)
    before, after = shifted(cross, "x", 1), shifted(cross, "x", -1)

    part_shape = jax.ShapeDtypeStruct((count_x, count_y, piece, layers * 3 * rank), LOW)
    keep, send = local_call(
        functools.partial(project_kernel, rank),
        (part_shape, part_shape),
        (rows, weights),
        scalars=place,
        flops=2 * rows.shape[0] * tok_rows * features * layers * rank * 3,
    )
    send, before, after = lax.optimization_barrier((send, before, after))
    came = lax.ppermute(send, "c", swap_core)
    half = cross.shape[0] // 2
    beyond = [shifted(before[:half], "x", 1), shifted(after[half:], "x", -1)]
    parts = (keep.astype(WIDE) + came.astype(WIDE)).astype(LOW)
    parts = parts.reshape(count_x * count_y, piece, layers * 3 * rank)
    parts, *beyond = lax.optimization_barrier((parts, *beyond))
    cross_near = jnp.stack([cross, before, after, jnp.concatenate(beyond)])
    cross_far = lax.ppermute(cross_near, "c", swap_core)
    parts = lax.all_to_all(parts, ("x", "y"), 0, 0, tiled=True)
    span = layers * rank
    acts, moves = local_call(
        functools.partial(recursion_kernel, layers, rank, float(model_width)),
        (
            jax.ShapeDtypeStruct((piece, span + rank), LOW),
            jax.ShapeDtypeStruct((piece, span), LOW),
        ),
        (parts, square, cross_near, cross_far),
        scalars=place,
        scratch=[
            pltpu.VMEM((piece, layers * 3 * rank), WIDE),
            pltpu.VMEM((layers * rank, layers * rank), LOW),
        ],
    )
    acts_near = gather_line(acts, "x")
    moves_near = gather_line(moves, "y")
    acts_near = gather_line(acts_near, "y")
    moves_near = gather_line(moves_near, "x")
    acts_far = lax.ppermute(acts_near, "c", swap_core)
    moves_far = lax.ppermute(moves_near, "c", swap_core)

    group_tokens = count_y * tok_rows
    outputs, grads = local_call(
        functools.partial(expand_kernel, layers, rank),
        (
            jax.ShapeDtypeStruct((layers, count_y, tok_rows, features), LOW),
            jax.ShapeDtypeStruct((layers, rank, 2 * features), LOW),
        ),
        (rows, weights, acts_near, acts_far, moves_near, moves_far),
        scalars=place,
        scratch=[
            pltpu.VMEM((group_tokens, features), WIDE),
            pltpu.VMEM((group_tokens, layers * rank), LOW),
            pltpu.VMEM((group_tokens, layers * rank), LOW),
            pltpu.VMEM((group_tokens, rank), WIDE),
        ],
        flops=8 * group_tokens * features * layers * rank,
    )
    grads = lax.psum_scatter(grads, "z", scatter_dimension=0, tiled=True)[0]
    outputs = outputs.reshape(sources, tok_rows, features)
    outputs = lax.all_to_all(outputs, PLANE, 0, 0, tiled=True)
    outputs = outputs.reshape(layers, count_y, tok_rows, features)
    section_rows = pl.pallas_call(
        order_kernel,
        grid=(count_y,),
        out_shape=jax.ShapeDtypeStruct((tok_rows, model_width), LOW),
        in_specs=[pl.BlockSpec((layers, 1, tok_rows, features), lambda i: (0, i, 0, 0))],
        out_specs=pl.BlockSpec((tok_rows, layers * features), lambda i: (0, i)),
        compiler_params=pltpu.CompilerParams(vmem_limit_bytes=VMEM_BYTES),
    )(outputs)

    squares = local_call(
        square_kernel, jax.ShapeDtypeStruct((sources, 128), WIDE), (grads,)
    )
    for distance in (4, 2, 1):
        squares = squares + shifted(squares, "z", distance)
    squares = lax.all_to_all(squares, PLANE, 0, 0, tiled=True)
    total_sq = jnp.sum(squares[:, 0])
    own_grads = lax.ppermute(grads, across, home)
    shard_in, shard_out = local_call(
        settle_kernel,
        (
            jax.ShapeDtypeStruct((features, rank), WIDE),
            jax.ShapeDtypeStruct((rank, features), WIDE),
        ),
        (own_grads,),
    )
    norm_limit = clip_rms * math.sqrt(2.0 * model_width * rank * layers)
    clip_factor = norm_limit / jnp.maximum(jnp.sqrt(total_sq), norm_limit)
    new_in, new_first_in, new_second_in = adam_update(
        master_in[0], first_in[0], second_in[0], clip_factor * shard_in
    )
    new_out, new_first_out, new_second_out = adam_update(
        master_out[0], first_out[0], second_out[0], clip_factor * shard_out
    )
    return (
        section_rows[None],
        new_in[None],
        new_out[None],
        new_first_in[None],
        new_first_out[None],
        new_second_in[None],
        new_second_out[None],
    )


def solution(mesh):
    layers, groups = mesh.shape["section"], mesh.shape["dp"]
    sizes = (layers // 2, 2, groups // layers, layers)
    fine = Mesh(mesh.devices.reshape(sizes), EVERYONE)
    split = ("y", "z")
    by_rows = P(SECTION, split, None)
    by_cols = P(SECTION, None, split)
    in_specs = (
        P(split, None),
        P(split, None),
        P(SECTION, None),
        by_rows,
        by_cols,
        by_rows,
        by_cols,
        by_rows,
        by_cols,
    )
    out_specs = (by_rows, by_rows, by_cols, by_rows, by_cols, by_rows, by_cols)
    return jax.shard_map(shards, mesh=fine, in_specs=in_specs, out_specs=out_specs, check_vma=False)
```

```python
import functools
import math

import jax
import jax.numpy as jnp
from jax import lax
from jax.experimental import pallas as pl
from jax.experimental.pallas import tpu as pltpu
from jax.sharding import Mesh, PartitionSpec as P

STEP = 10

norm_eps = 1e-05
gelu_coef = 0.7978845608028654
beta_one = 0.9
beta_two = 0.95
adam_eps = 1e-08
learn_rate = 0.05
decay_rate = 0.1
clip_rms = 0.5

LOW = jnp.bfloat16
WIDE = jnp.float32
SECTION = ("x", "c")
PLANE = ("x", "c", "y")
EVERYONE = ("x", "c", "y", "z")
SHIFTS = (0, 1, -1, 2)
TURNS = (0, 4, 3, 7, 2, 6, 1, 5)
FIRST = (0, 3, 3, -1, 2, -2, 1, -3)
EXTRA = 16
VMEM_BYTES = 48 * 1024 * 1024


def dot_nn(left, right):
    return lax.dot_general(left, right, (((1,), (0,)), ((), ())), preferred_element_type=WIDE)


def dot_nt(left, right):
    return lax.dot_general(left, right, (((1,), (1,)), ((), ())), preferred_element_type=WIDE)


def dot_tn(left, right):
    return lax.dot_general(left, right, (((0,), (0,)), ((), ())), preferred_element_type=WIDE)


def gelu_pair(hidden_pre):
    inner_arg = gelu_coef * (hidden_pre + 0.044715 * hidden_pre * hidden_pre * hidden_pre)
    tangent = jnp.tanh(inner_arg)
    gelu_value = 0.5 * hidden_pre * (1.0 + tangent)
    gelu_slope = 0.5 * (1.0 + tangent) + 0.5 * hidden_pre * (
        1.0 - tangent * tangent
    ) * gelu_coef * (1.0 + 3.0 * 0.044715 * hidden_pre * hidden_pre)
    return (gelu_value, gelu_slope)


def adam_update(master, first, second, grad):
    first_new = beta_one * first + (1.0 - beta_one) * grad
    second_new = beta_two * second + (1.0 - beta_two) * grad * grad
    first_hat = first_new / (1.0 - beta_one**STEP)
    second_hat = second_new / (1.0 - beta_two**STEP)
    master_new = master - learn_rate * (
        first_hat / (jnp.sqrt(second_hat) + adam_eps) + decay_rate * master
    )
    return (master_new, first_new, second_new)


def local_call(kernel, out_shape, operands, scalars=None, scratch=(), flops=0):
    specs = jax.tree.map(lambda _: pl.BlockSpec(memory_space=pltpu.VMEM), out_shape)
    moved = sum(a.size * a.dtype.itemsize for a in operands)
    moved += sum(a.size * a.dtype.itemsize for a in jax.tree.leaves(out_shape))
    in_specs = [pl.BlockSpec(memory_space=pltpu.VMEM)] * len(operands)
    if scalars is not None:
        operands = (scalars,) + tuple(operands)
        in_specs = [pl.BlockSpec(memory_space=pltpu.SMEM)] + in_specs
    return pl.pallas_call(
        kernel,
        out_shape=out_shape,
        in_specs=in_specs,
        out_specs=specs,
        scratch_shapes=list(scratch),
        compiler_params=pltpu.CompilerParams(vmem_limit_bytes=VMEM_BYTES),
        cost_estimate=pl.CostEstimate(flops=flops, bytes_accessed=moved, transcendentals=0),
    )(*operands)


def shifted(block, axis, distance):
    size = lax.axis_size(axis)
    return lax.ppermute(block, axis, [(i, (i + distance) % size) for i in range(size)])


def gather_line(block, axis):
    return jnp.stack([block] + [shifted(block, axis, d) for d in SHIFTS[1:]])


def pack_kernel(gain_ref, in_ref, out_ref, pack_ref):
    features, rank = in_ref.shape[1:]
    gain = jnp.broadcast_to(gain_ref[...], (rank, features)).T
    work_in = in_ref[0].astype(LOW).astype(WIDE)
    pack_ref[:features, :rank] = (work_in * gain).astype(LOW)
    pack_ref[:features, rank:] = out_ref[0].T.astype(LOW)
    spare = (EXTRA, 2 * rank)
    row = lax.broadcasted_iota(jnp.int32, spare, 0)
    rows = jnp.zeros(spare, WIDE)
    left = gain_ref[...]
    chunks = features // rank
    for term in range(3):
        part = left.astype(LOW).astype(WIDE)
        left = left - part
        for k in range(chunks):
            chunk = part[:, k * rank : (k + 1) * rank]
            chunk = jnp.broadcast_to(jnp.concatenate([chunk, chunk], axis=1), spare)
            rows = jnp.where(row == term * chunks + k, chunk, rows)
    pack_ref[features:, :] = rows.astype(LOW)


def packed_gain(tail, chunks):
    rows = tail.astype(WIDE)
    parts = []
    for k in range(chunks):
        terms = [rows[t * chunks + k : t * chunks + k + 1] for t in range(3)]
        parts.append(terms[0] + terms[1] + terms[2])
    return jnp.concatenate(parts, axis=1)


def cross_kernel(rank, place_ref, own_ref, near_ref, far_ref, out_ref):
    core, section, column = place_ref[0], place_ref[1], place_ref[2]
    count = len(SHIFTS)
    cut = out_ref.shape[1]
    cuts = rank // cut
    features = own_ref.shape[0] - EXTRA
    own = own_ref[:features, rank:].T
    for slot, step in enumerate(SHIFTS):
        owner = lax.rem(column - step + count, count)
        blocks = []
        for line_ref, from_core in ((near_ref, core), (far_ref, 1 - core)):
            both = dot_nn(own, line_ref[slot, :features])
            later = 2 * owner + from_core > section
            blocks.append(jnp.where(later, both[:, :rank], both[:, rank:]).astype(LOW))
        even = jnp.where(core == 0, blocks[0], blocks[1])
        odd = jnp.where(core == 0, blocks[1], blocks[0])
        for k in range(cuts):
            sel = slice(k * cut, (k + 1) * cut)
            out_ref[owner * cuts + k, :, :rank] = even[sel]
            out_ref[owner * cuts + k, :, rank:] = odd[sel]


def project_kernel(rank, place_ref, rows_ref, weight_ref, keep_ref, send_ref):
    groups, both_rows, features = rows_ref.shape
    layers = weight_ref.shape[0]
    half = both_rows // 2
    columns = keep_ref.shape[0]
    piece = half // (2 * columns)
    core, section = place_ref[0], place_ref[1]
    for layer in range(layers):
        weight = weight_ref[lax.rem(section + TURNS[layer], layers), :features]
        base = layer * 3 * rank
        for group in range(groups):
            first = dot_nn(rows_ref[group, :half, :], weight).astype(LOW)
            second = dot_nn(rows_ref[group, half:, :], weight[:, rank:]).astype(LOW)
            for column in range(columns):
                low = 2 * column * piece
                even, odd = slice(low, low + piece), slice(low + piece, low + 2 * piece)
                for value, at, width in ((first, base, 2 * rank), (second, base + 2 * rank, rank)):
                    lanes = slice(at, at + width)
                    keep_ref[column, group, :, lanes] = jnp.where(core == 0, value[even], value[odd])
                    send_ref[column, group, :, lanes] = jnp.where(core == 0, value[odd], value[even])


def recursion_kernel(
    layers, rank, width, place_ref, parts_ref, square_ref, near_ref, far_ref, act_ref, moved_ref, sums_ref, cross_ref
):
    core, column = place_ref[0], place_ref[2]
    count = len(SHIFTS)
    pieces, cut = near_ref.shape[1:3]
    cuts = rank // cut
    for slot, distance in enumerate(SHIFTS):
        owner = lax.rem(column - distance + count, count)
        for piece_ref, from_core in ((near_ref, core), (far_ref, 1 - core)):
            start = (2 * owner + from_core) * rank
            for k in range(pieces):
                at = pl.multiple_of(start + (k % cuts) * cut, cut)
                low = (k // cuts) * 2 * rank
                cross_ref[pl.ds(at, cut), low : low + 2 * rank] = piece_ref[slot, k]

    total = parts_ref[0].astype(WIDE)
    for source in range(1, parts_ref.shape[0]):
        total = total + parts_ref[source].astype(WIDE)
    sums_ref[...] = total
    rank3 = 3 * rank
    down = [sums_ref[:, k * rank3 : k * rank3 + rank] for k in range(layers)]
    up = [sums_ref[:, k * rank3 + rank : k * rank3 + 2 * rank] for k in range(layers)]
    back = [sums_ref[:, k * rank3 + 2 * rank : (k + 1) * rank3] for k in range(layers)]
    square = square_ref[:, 0:1]

    acts, pres, invs = [], [], []
    for s in range(layers):
        inv = lax.rsqrt(jnp.maximum(square, 0.0) / width + norm_eps)
        pre = inv * down[s]
        act, _ = gelu_pair(pre)
        act = act.astype(LOW)
        acts.append(act)
        pres.append(pre)
        invs.append(inv)
        act_ref[:, s * rank : (s + 1) * rank] = act
        low = s * rank
        forward = dot_nn(act, cross_ref[low : low + rank, low:])
        before = up[s]
        up[s] = before + forward[:, :rank]
        square = square + jnp.sum(act.astype(WIDE) * (before + up[s]), axis=-1, keepdims=True)
        if s + 1 < layers:
            mirrored = dot_nt(act, cross_ref[low + rank :, low : low + rank])
            for k in range(s + 1, layers):
                at = (k - s) * rank
                down[k] = down[k] + forward[:, at : at + rank]
                up[k] = up[k] + mirrored[:, at - rank : at]

    trailing = jnp.zeros_like(square)
    lane = lax.broadcasted_iota(jnp.int32, (square.shape[0], rank), 1)
    tail = jnp.zeros((square.shape[0], rank), WIDE)
    for s in reversed(range(layers)):
        _, slope = gelu_pair(pres[s])
        d_pre = (back[s] - trailing * up[s]) * slope
        coef = invs[s] * invs[s] * (1.0 / width) * jnp.sum(d_pre * pres[s], axis=-1, keepdims=True)
        moved = (invs[s] * d_pre).astype(LOW)
        moved_ref[:, s * rank : (s + 1) * rank] = moved
        coef_high = coef.astype(LOW).astype(WIDE)
        tail = tail + jnp.where(lane == s, coef_high, 0.0)
        tail = tail + jnp.where(lane == s + layers, coef - coef_high, 0.0)
        if s > 0:
            low = s * rank
            gain_term = dot_nt(moved, cross_ref[:low, low : low + rank])
            scaled_act = (trailing * acts[s].astype(WIDE)).astype(LOW)
            norm_term = dot_nn(scaled_act, cross_ref[low : low + rank, :low])
            for k in range(s):
                sel = slice(k * rank, (k + 1) * rank)
                back[k] = back[k] + gain_term[:, sel] - norm_term[:, sel]
        trailing = trailing + coef
    act_ref[:, layers * rank :] = tail.astype(LOW)


def expand_kernel(
    layers,
    rank,
    place_ref,
    rows_ref,
    weight_ref,
    act_near_ref,
    act_far_ref,
    move_near_ref,
    move_far_ref,
    out_ref,
    grad_ref,
    wide_ref,
    act_ref,
    moved_ref,
    coef_ref,
):
    groups, both_rows, features = rows_ref.shape
    half = both_rows // 2
    piece = act_near_ref.shape[2]
    span = layers * rank
    core, section, column, line = (place_ref[i] for i in range(4))
    count = len(SHIFTS)
    for group in range(groups):
        base = group * half
        wide_ref[base : base + half, :] = rows_ref[group, :half, :].astype(WIDE)
    for slot_y, step_y in enumerate(SHIFTS):
        group = lax.rem(line - step_y + count, count)
        for slot_x, step_x in enumerate(SHIFTS):
            owner = lax.rem(column - step_x + count, count)
            for some_act, some_move, from_core in (
                (act_near_ref, move_near_ref, core),
                (act_far_ref, move_far_ref, 1 - core),
            ):
                at = pl.multiple_of(group * half + (2 * owner + from_core) * piece, piece)
                dest = pl.ds(at, piece)
                act_ref[dest, :] = some_act[slot_y, slot_x, :, :span]
                coef_ref[dest, :] = some_act[slot_y, slot_x, :, span:].astype(WIDE)
                moved_ref[dest, :] = some_move[slot_x, slot_y]

    for layer in range(layers):
        up_weight = weight_ref[lax.rem(section + TURNS[layer], layers), :features, rank:]
        act = act_ref[:, layer * rank : (layer + 1) * rank]
        total = wide_ref[...] + dot_nt(act, up_weight)
        wide_ref[...] = total
        lowered = total.astype(LOW)
        for group in range(groups):
            out_ref[layer, group] = lowered[group * half : (group + 1) * half]

    for group in range(groups):
        base = group * half
        wide_ref[base : base + half, :] = rows_ref[group, half:, :].astype(WIDE)
    for layer in reversed(range(layers)):
        slot = lax.rem(section + TURNS[layer], layers)
        delta = wide_ref[...].astype(LOW)
        act = act_ref[:, layer * rank : (layer + 1) * rank]
        moved = moved_ref[:, layer * rank : (layer + 1) * rank]
        if layer > 0:
            current = out_ref[layer - 1].reshape(groups * half, features)
        else:
            current = rows_ref[:, :half, :].reshape(groups * half, features)
        grad_ref[slot, :, features:] = dot_tn(act, delta).astype(LOW)
        gain = packed_gain(weight_ref[slot, features:, :rank], features // rank)
        grad_ref[slot, :, :features] = (dot_tn(moved, current) * gain).astype(LOW)
        if layer > 0:
            coef = coef_ref[:, layer : layer + 1] + coef_ref[:, layers + layer : layers + layer + 1]
            wide_ref[...] += dot_nt(moved, weight_ref[slot, :features, :rank]) - coef * current.astype(WIDE)


def square_kernel(grad_ref, out_ref):
    grad = grad_ref[...].astype(WIDE)
    out_ref[...] = jnp.full(out_ref.shape, jnp.sum(grad * grad), WIDE)


def settle_kernel(grad_ref, in_ref, out_ref):
    features = out_ref.shape[1]
    in_ref[...] = grad_ref[:, :features].astype(WIDE).T
    out_ref[...] = grad_ref[:, features:].astype(WIDE)


def order_kernel(block_ref, out_ref):
    layers, features = block_ref.shape[0], block_ref.shape[3]
    for layer in range(layers):
        out_ref[:, layer * features : (layer + 1) * features] = block_ref[layer, 0]


def shards(
    stack_input,
    out_cotangent,
    norm_gain,
    master_in,
    master_out,
    first_in,
    first_out,
    second_in,
    second_out,
):
    count_x, count_c, count_y, count_z = (lax.axis_size(a) for a in EVERYONE)
    pos_x, pos_c, pos_y, pos_z = (lax.axis_index(a) for a in EVERYONE)
    layers = count_x * count_c
    pos_s = pos_x * count_c + pos_c
    place = jnp.stack([pos_c, pos_s, pos_x, pos_y]).astype(jnp.int32)
    sources = layers * count_y
    tok_rows, model_width = stack_input.shape
    features, rank = master_in.shape[1:]
    piece = tok_rows // layers
    swap_core = [(0, 1), (1, 0)]
    grid = [(a, b) for a in range(layers) for b in range(count_z)]
    turned = {(a, b): (b + TURNS[a]) % count_z for a, b in grid}
    swap = [(a * count_z + b, b * count_z + turned[a, b]) for a, b in grid]
    most_back = [
        (b * count_z + turned[a, b], a * count_z + (turned[a, b] - FIRST[a]) % count_z) for a, b in grid
    ]
    last_back = [(a * count_z + b, a * count_z + (b - TURNS[a] + FIRST[a]) % count_z) for a, b in grid]
    across = SECTION + ("z",)

    gain_own = lax.dynamic_slice_in_dim(norm_gain, (pos_y * count_z + pos_z) * features, features, 1)
    def blocks_of(rows):
        return jnp.stack(
            [
                lax.dynamic_slice_in_dim(rows, (g * count_z + pos_s) * features, features, 1)
                for g in range(count_y)
            ]
        )

    rows = jnp.concatenate([blocks_of(stack_input), blocks_of(out_cotangent)], axis=1)
    gain_own, rows = lax.optimization_barrier((gain_own, rows))
    rows = lax.all_to_all(rows, "y", 0, 0, tiled=True)
    packed = local_call(
        pack_kernel, jax.ShapeDtypeStruct((features + EXTRA, 2 * rank), LOW), (gain_own, master_in, master_out)
    )
    swapped = lax.ppermute(packed, across, swap)
    lined_near = gather_line(packed, "x")
    swapped, lined_near, rows = lax.optimization_barrier((swapped, lined_near, rows))
    lined_far = lax.ppermute(lined_near, "c", swap_core)
    weights = lax.all_gather(swapped, "z", axis=0)

    own_rows = lax.dynamic_slice_in_dim(stack_input, pos_s * piece, piece, 0).astype(WIDE)
    square = jnp.sum(own_rows * own_rows, axis=-1, keepdims=True)
    square = jnp.broadcast_to(square, (piece, 128))

    cut_r, cut_c = rank // count_z, count_c * rank
    cross = local_call(
        functools.partial(cross_kernel, rank),
        jax.ShapeDtypeStruct((count_y * count_z, cut_r, cut_c), LOW),
        (packed, lined_near, lined_far),
        scalars=place,
    )
    cross = lax.all_to_all(cross, ("y", "z"), 0, 0, tiled=True)
    cross = jnp.sum(cross.astype(WIDE), axis=0, keepdims=True).astype(LOW)
    cross = jnp.broadcast_to(cross, (count_y * count_z, cut_r, cut_c))
    cross = lax.all_to_all(cross, ("y", "z"), 0, 0, tiled=True)
    before, after = shifted(cross, "x", 1), shifted(cross, "x", -1)

    part_shape = jax.ShapeDtypeStruct((count_x, count_y, piece, layers * 3 * rank), LOW)
    keep, send = local_call(
        functools.partial(project_kernel, rank),
        (part_shape, part_shape),
        (rows, weights),
        scalars=place,
        flops=2 * rows.shape[0] * tok_rows * features * layers * rank * 3,
    )
    send, before, after = lax.optimization_barrier((send, before, after))
    came = lax.ppermute(send, "c", swap_core)
    half = cross.shape[0] // 2
    beyond = [shifted(before[:half], "x", 1), shifted(after[half:], "x", -1)]
    parts = (keep.astype(WIDE) + came.astype(WIDE)).astype(LOW)
    parts = parts.reshape(count_x * count_y, piece, layers * 3 * rank)
    cross_near = jnp.stack([cross, before, after, jnp.concatenate(beyond)])
    cross_far = lax.ppermute(cross_near, "c", swap_core)
    parts = lax.all_to_all(parts, ("x", "y"), 0, 0, tiled=True)
    span = layers * rank
    acts, moves = local_call(
        functools.partial(recursion_kernel, layers, rank, float(model_width)),
        (
            jax.ShapeDtypeStruct((piece, span + rank), LOW),
            jax.ShapeDtypeStruct((piece, span), LOW),
        ),
        (parts, square, cross_near, cross_far),
        scalars=place,
        scratch=[
            pltpu.VMEM((piece, layers * 3 * rank), WIDE),
            pltpu.VMEM((layers * rank, layers * rank), LOW),
        ],
    )
    acts_near = gather_line(acts, "x")
    moves_near = gather_line(moves, "y")
    acts_near = gather_line(acts_near, "y")
    moves_near = gather_line(moves_near, "x")
    acts_far = lax.ppermute(acts_near, "c", swap_core)
    moves_far = lax.ppermute(moves_near, "c", swap_core)

    group_tokens = count_y * tok_rows
    outputs, grads = local_call(
        functools.partial(expand_kernel, layers, rank),
        (
            jax.ShapeDtypeStruct((layers, count_y, tok_rows, features), LOW),
            jax.ShapeDtypeStruct((layers, rank, 2 * features), LOW),
        ),
        (rows, weights, acts_near, acts_far, moves_near, moves_far),
        scalars=place,
        scratch=[
            pltpu.VMEM((group_tokens, features), WIDE),
            pltpu.VMEM((group_tokens, layers * rank), LOW),
            pltpu.VMEM((group_tokens, layers * rank), LOW),
            pltpu.VMEM((group_tokens, rank), WIDE),
        ],
        flops=8 * group_tokens * features * layers * rank,
    )
    grads = lax.psum_scatter(grads, "z", scatter_dimension=0, tiled=True)[0]
    outputs = outputs.reshape(sources, tok_rows, features)
    outputs = lax.all_to_all(outputs, PLANE, 0, 0, tiled=True)
    outputs = outputs.reshape(layers, count_y, tok_rows, features)
    section_rows = pl.pallas_call(
        order_kernel,
        grid=(count_y,),
        out_shape=jax.ShapeDtypeStruct((tok_rows, model_width), LOW),
        in_specs=[pl.BlockSpec((layers, 1, tok_rows, features), lambda i: (0, i, 0, 0))],
        out_specs=pl.BlockSpec((tok_rows, layers * features), lambda i: (0, i)),
        compiler_params=pltpu.CompilerParams(vmem_limit_bytes=VMEM_BYTES),
    )(outputs)

    squares = local_call(
        square_kernel, jax.ShapeDtypeStruct((sources * count_z, 128), WIDE), (grads,)
    )
    squares = lax.all_to_all(squares, EVERYONE, 0, 0, tiled=True)
    total_sq = jnp.sum(squares[:, 0])
    own_grads = lax.ppermute(lax.ppermute(grads, across, most_back), across, last_back)
    shard_in, shard_out = local_call(
        settle_kernel,
        (
            jax.ShapeDtypeStruct((features, rank), WIDE),
            jax.ShapeDtypeStruct((rank, features), WIDE),
        ),
        (own_grads,),
    )
    norm_limit = clip_rms * math.sqrt(2.0 * model_width * rank * layers)
    clip_factor = norm_limit / jnp.maximum(jnp.sqrt(total_sq), norm_limit)
    new_in, new_first_in, new_second_in = adam_update(
        master_in[0], first_in[0], second_in[0], clip_factor * shard_in
    )
    new_out, new_first_out, new_second_out = adam_update(
        master_out[0], first_out[0], second_out[0], clip_factor * shard_out
    )
    return (
        section_rows[None],
        new_in[None],
        new_out[None],
        new_first_in[None],
        new_first_out[None],
        new_second_in[None],
        new_second_out[None],
    )


def solution(mesh):
    layers, groups = mesh.shape["section"], mesh.shape["dp"]
    sizes = (layers // 2, 2, groups // layers, layers)
    fine = Mesh(mesh.devices.reshape(sizes), EVERYONE)
    split = ("y", "z")
    by_rows = P(SECTION, split, None)
    by_cols = P(SECTION, None, split)
    in_specs = (
        P(split, None),
        P(split, None),
        P(SECTION, None),
        by_rows,
        by_cols,
        by_rows,
        by_cols,
        by_rows,
        by_cols,
    )
    out_specs = (by_rows, by_rows, by_cols, by_rows, by_cols, by_rows, by_cols)
    return jax.shard_map(shards, mesh=fine, in_specs=in_specs, out_specs=out_specs, check_vma=False)
```
